32 devices in a mesh: span: 4 (over z), xsec: 2 (over x), leaf: 4 (over y, core).
Axes of the slice: x: 2, y: 2, z: 4, core: 2. Of those that a mesh axis runs over, the one named last changes fastest.
Arguments:
- snapshots: float32 [3, 8192, 256], P(None, ('span', 'xsec', 'leaf')), may hold values from -1800 to 1800
- member_ends: int32 [2, 32768], P(None, ('span', 'xsec', 'leaf')), may hold values from 0 to 383, as said below
- member_dir: float32 [3, 32768], P(None, ('span', 'xsec', 'leaf')), may hold values from -3 to 3
- member_stiff: float32 [32768], P(('span', 'xsec', 'leaf')), may hold values from 0.25 to 24
Outputs:
- basis: float32 [3, 8192, 256], P(None, ('span', 'xsec', 'leaf'))
- forces: float32 [3, 8192, 256], P(None, ('span', 'xsec', 'leaf'))
- reduced: float32 [256, 256], replicated
- coef: float32 [256, 256], replicated
- column_energy: float32 [256], replicated
The draws below stay inside these ranges and needn't reach their ends.
Inputs may be any that keep to these rules, and one draw needn't show every extreme that they name: member_ends[0] names a node of the member's own device block; member_ends[1] names such a node or, from 256 on, a node of the top level of the slab directly below in the same sector; both ends of a member lie on the same or neighbouring levels.
All inputs are finite; a program needn't handle non-finite values.
Results may differ from the reference program's by a relative error of at most 0.0008.
Values sent between devices are 32-bit elements; how exact they have to be, the bound alone decides.
No kernel may reach another device: no remote copies, remote signals or barrier semaphores. Data moves between devices by JAX's collectives and lax.ppermute only.
A program may use at most 64 MiB of HBM per device.

```python
import math
import jax
import jax.numpy as jnp
from jax import lax

K = 256
LEV_DEV = 2
SEC_NODES = 128
NODE_DEV = 256
MEMB_DEV = 1024
SECTORS = 8
NODES = 8192
MEMBERS = 32768
N_SPAN = 4
N_XSEC = 2
N_LEAF = 4


def draw_snapshots(key, part):
    key_noise = jax.random.fold_in(key, 11)
    key_common = jax.random.fold_in(key, 12)
    key_column = jax.random.fold_in(key, 13)
    key_row = jax.random.fold_in(key, 14)
    key_weak = jax.random.fold_in(key, 15)
    ratio = min(8.0, 3.0 * NODE_DEV / K)
    weakest = 0.002 * 8.0 / ratio
    noise = jnp.clip(jax.random.normal(key_noise, (3, NODES, K), jnp.float32), -5.0, 5.0)
    common = jnp.clip(jax.random.normal(key_common, (3, NODES, 1), jnp.float32), -4.0, 4.0)
    row_span = math.log(10.0)
    weight = jnp.exp(jax.random.uniform(key_weak, (K,), jnp.float32, math.log(weakest), 0.0))
    column_scale = jnp.exp(jax.random.uniform(key_column, (K,), jnp.float32, 0.0, math.log(10.0)))
    row_scale = jnp.exp(jax.random.uniform(key_row, (3, NODES, 1), jnp.float32, 0.0, row_span))
    height = 1.0 + 2.0 * jnp.arange(NODES, dtype=jnp.float32) / NODES
    mixed = common + weight[None, None, :] * noise
    values = mixed * column_scale[None, None, :] * row_scale * height[None, :, None]
    return jnp.clip(values, -1800.0, 1800.0)


def draw_member_ends(key, part):
    key_first = jax.random.fold_in(key, 21)
    key_kind = jax.random.fold_in(key, 22)
    key_across = jax.random.fold_in(key, 23)
    key_down = jax.random.fold_in(key, 24)
    first_end = jax.random.randint(key_first, (MEMBERS,), 0, NODE_DEV, dtype=jnp.int32)
    level_index = first_end // SEC_NODES
    position = first_end % SEC_NODES
    member_kind = jax.random.randint(key_kind, (MEMBERS,), 0, 3, dtype=jnp.int32)
    across_step = jax.random.randint(key_across, (MEMBERS,), 1, 4, dtype=jnp.int32)
    down_step = jax.random.randint(key_down, (MEMBERS,), -2, 3, dtype=jnp.int32)
    across_end = level_index * SEC_NODES + (position + across_step) % SEC_NODES
    down_position = (position + down_step) % SEC_NODES
    down_end = jnp.where(level_index > 0, (level_index - 1) * SEC_NODES + down_position, NODE_DEV + down_position)
    second_end = jnp.where(member_kind == 0, across_end, down_end)
    return jnp.stack([first_end, second_end]).astype(jnp.int32)


def draw_member_stiff(key, part):
    key_base = jax.random.fold_in(key, 31)
    lowest, highest_value = (0.5, 4.0)
    base = jnp.exp(jax.random.uniform(key_base, (MEMBERS,), jnp.float32, math.log(lowest), math.log(highest_value)))
    height = jnp.arange(MEMBERS, dtype=jnp.float32) / MEMBERS
    return base * (3.0 - 2.0 * height)


def level_of(stream_key, shape, pieces, smallest, high):
    factor_of, own = 1.0, jax.random.fold_in(stream_key, 6)
    for dim, parts in pieces:
        steps = jnp.exp(jax.random.uniform(jax.random.fold_in(own, dim), (parts,), jnp.float32, smallest / len(pieces), high / len(pieces)))
        factor_of = factor_of * jnp.repeat(steps, shape[dim] // parts).reshape([-1 if axis == dim else 1 for axis in range(len(shape))])
    return factor_of


def gaussian(key, dims, scale, bound, split=(), kind=jnp.bfloat16):
    level = level_of(key, dims, split, -0.22, 0.18) if split else 1.0
    values = jax.random.normal(key, dims, jnp.float32) * scale * level
    return jnp.minimum(jnp.maximum(values, -bound), bound).astype(kind)


def setup_inputs(seed: int = 0) -> dict:
    key_of = jax.random.split(jax.random.key(seed), 5)
    return {
        "snapshots": draw_snapshots(jax.random.fold_in(key_of[4], 71), 0),
        "member_ends": draw_member_ends(jax.random.fold_in(key_of[4], 71), 0),
        "member_dir": gaussian(key_of[2], (3, MEMBERS), 0.5, 3.0, ((1, 32),), jnp.float32),
        "member_stiff": draw_member_stiff(jax.random.fold_in(key_of[4], 71), 0),
    }


def member_block(basis, member_ends, member_dir, member_stiff, device_index):
    start = (device_index * MEMB_DEV).astype(jnp.int32)
    ends_here = lax.dynamic_slice_in_dim(member_ends, start, MEMB_DEV, 1)
    direction = lax.dynamic_slice_in_dim(member_dir, start, MEMB_DEV, 1)
    stiffness = lax.dynamic_slice_in_dim(member_stiff, start, MEMB_DEV, 0)
    own_block = lax.dynamic_slice_in_dim(basis, (device_index * NODE_DEV).astype(jnp.int32), NODE_DEV, 1)
    lower_index = jnp.maximum(device_index - SECTORS, 0)
    top_start = (lower_index * NODE_DEV + (LEV_DEV - 1) * SEC_NODES).astype(jnp.int32)
    below_top = lax.dynamic_slice_in_dim(basis, top_start, SEC_NODES, 1)
    below_top = jnp.where(device_index >= SECTORS, below_top, jnp.zeros_like(below_top))
    extended = jnp.concatenate([own_block, below_top], axis=1)
    first_end = ends_here[0]
    second_end = ends_here[1]
    difference = extended[:, first_end, :] - extended[:, second_end, :]
    elongation = jnp.einsum('cm,cmk->mk', direction, difference, precision=lax.Precision.HIGHEST)
    axial_force = elongation * stiffness[:, None]
    nodal_push = direction[:, :, None] * axial_force[None, :, :]
    extended_forces = jnp.zeros_like(extended).at[:, first_end, :].add(nodal_push).at[:, second_end, :].add(-nodal_push)
    partial_sum = jnp.einsum('mk,ml->kl', elongation, axial_force, precision=lax.Precision.HIGHEST)
    return (extended_forces, partial_sum)

def reference(snapshots, member_ends, member_dir, member_stiff):
    flattened = snapshots.reshape(3 * NODES, K)
    column_energy = jnp.log(lax.optimization_barrier(jnp.sum(flattened * flattened, axis=0)) / (3 * NODES))
    factor_q, factor_r = jnp.linalg.qr(flattened)
    signs = jnp.sign(jnp.diagonal(factor_r))
    root_rows = jnp.sqrt(jnp.float32(3 * NODES))
    basis = (factor_q * signs[None, :] * root_rows).reshape(3, NODES, K)
    coef = factor_r * signs[:, None] / root_rows
    device_count = N_SPAN * N_XSEC * N_LEAF
    indices = jnp.arange(device_count, dtype=jnp.int32)
    extended_forces, partials = lax.map(lambda index: member_block(basis, member_ends, member_dir, member_stiff, index), indices)
    own_forces = extended_forces[:, :, :NODE_DEV, :]
    returned = extended_forces[:, :, NODE_DEV:, :]
    from_above = jnp.concatenate([returned[SECTORS:], jnp.zeros_like(returned[:SECTORS])], axis=0)
    own_forces = own_forces.at[:, :, NODE_DEV - SEC_NODES:, :].add(from_above)
    forces = own_forces.transpose(1, 0, 2, 3).reshape(3, NODES, K)
    reduced = lax.optimization_barrier(jnp.sum(partials, axis=0)) / (3 * NODES)
    return (basis, forces, reduced, coef, column_energy)
```

```python
import math

import jax
import jax.numpy as jnp
from jax import lax
from jax.experimental import pallas as pl
from jax.experimental.pallas import tpu as pltpu
from jax.sharding import PartitionSpec as P

AXES = ("span", "xsec", "leaf")
SEC_NODES = 128
CHUNK = 256
highest = lax.Precision.HIGHEST
VMEM = pl.BlockSpec(memory_space=pltpu.VMEM)
SMEM = pl.BlockSpec(memory_space=pltpu.SMEM)


def dot(a, b, ca=1, cb=0):
    return lax.dot_general(
        a, b, (((ca,), (cb,)), ((), ())), precision=highest, preferred_element_type=jnp.float32
    )


def call(kernel, shapes, operands, specs=None, scratch=()):
    return pl.pallas_call(
        kernel,
        out_shape=tuple(jax.ShapeDtypeStruct(s, jnp.float32) for s in shapes),
        in_specs=specs or [VMEM] * len(operands),
        out_specs=tuple(VMEM for _ in shapes),
        scratch_shapes=list(scratch),
        compiler_params=pltpu.CompilerParams(vmem_limit_bytes=48 << 20),
    )(*operands)


def exchange(array, bit):
    count = math.prod(lax.axis_size(a) for a in AXES)
    return lax.ppermute(array, AXES, [(i, i ^ bit) for i in range(count)])


def sum_over_devices(keep, send):
    count = math.prod(lax.axis_size(a) for a in AXES)
    total = keep + exchange(send, 1)
    bit = 2
    while bit < count:
        total = total + exchange(total, bit)
        bit *= 2
    return total, exchange(total, 1)


def shifted(array, axis, by):
    length = lax.axis_size(axis)
    pairs = [(i, i + by) for i in range(length) if 0 <= i + by < length]
    return lax.ppermute(array, axis, pairs)


def order_halves(odd, mine, other):
    return jnp.where(odd == 0, mine, other), jnp.where(odd == 0, other, mine)


def pack_one(gram):
    h, q = gram.shape[0] // 2, gram.shape[0] // 4
    g11, g12, g22 = gram[:h, :h], gram[:h, h:], gram[h:, h:]
    lane = lax.broadcasted_iota(jnp.int32, (q, h), 1)
    corner = jnp.where(lane < q, pltpu.roll(g11[q:], q, 1), g22[q:])
    return jnp.concatenate([g11[:q], g22[:q], corner, g12], axis=0)


def unpack_one(rows, h):
    q = h // 2
    lane = lax.broadcasted_iota(jnp.int32, (q, h), 1)
    corner = rows[2 * q : 3 * q]

    def block(top, low):
        square = jnp.concatenate([top, low], axis=0)
        flipped = square.T[q:]
        return jnp.concatenate([top, jnp.where(lane < q, flipped, low)], axis=0)

    g11 = block(rows[:q], pltpu.roll(corner, q, 1))
    g22 = block(rows[q : 2 * q], corner)
    return g11, rows[3 * q :], g22


def gram_kernel(odd_ref, s_ref, keep_ref, send_ref, top_ref):
    nodes = s_ref.shape[1]
    top_ref[...] = s_ref[:, nodes - SEC_NODES :, :]
    flat = s_ref[...].reshape(-1, s_ref.shape[2])
    packed = pack_one(dot(flat, flat, 0, 0))
    half = packed.shape[0] // 2
    keep_ref[...], send_ref[...] = order_halves(odd_ref[0], packed[:half], packed[half:])


def pieces_of(x):
    first = x.astype(jnp.bfloat16)
    rest = x - first.astype(jnp.float32)
    second = rest.astype(jnp.bfloat16)
    third = (rest - second.astype(jnp.float32)).astype(jnp.bfloat16)
    return first, second, third


def member_kernel(s_ref, below_ref, ends_ref, table_ref, own_ref, back_ref, parts_ref):
    nodes, width = s_ref.shape[1:]
    total = nodes + SEC_NODES
    for c in range(3):
        for i, piece in enumerate(pieces_of(s_ref[c])):
            parts_ref[i, c, :nodes, :] = piece
        for i, piece in enumerate(pieces_of(below_ref[c])):
            parts_ref[i, c, nodes:, :] = piece
    own_ref[...] = jnp.zeros_like(own_ref)
    back_ref[...] = jnp.zeros_like(back_ref)

    def chunk(start):
        rows = pl.ds(pl.multiple_of(start, CHUNK), CHUNK)
        table = table_ref[rows, :]
        node = lax.broadcasted_iota(jnp.int32, (CHUNK, total), 1).astype(jnp.float32)
        pick = (node == table[:, 0:1]).astype(jnp.float32) - (node == table[:, 1:2]).astype(jnp.float32)
        pick = pick.astype(jnp.bfloat16)
        ends = ends_ref[:, rows]
        node_t = lax.broadcasted_iota(jnp.int32, (total, CHUNK), 0)
        spread = (node_t == ends[0:1]).astype(jnp.float32) - (node_t == ends[1:2]).astype(jnp.float32)
        spread = spread.astype(jnp.bfloat16)
        elongation = jnp.zeros((CHUNK, width), jnp.float32)
        for c in range(3):
            difference = jnp.zeros((CHUNK, width), jnp.float32)
            for i in range(3):
                difference = difference + jnp.dot(pick, parts_ref[i, c], preferred_element_type=jnp.float32)
            elongation = elongation + table[:, 2 + c : 3 + c] * difference
        axial = elongation * table[:, 5:6]
        for c in range(3):
            push = table[:, 2 + c : 3 + c] * axial
            force = jnp.zeros((total, width), jnp.float32)
            for piece in pieces_of(push):
                force = force + jnp.dot(spread, piece, preferred_element_type=jnp.float32)
            own_ref[c] += force[:nodes]
            back_ref[c] += force[nodes:]

    def step(i, carry):
        chunk(i * CHUNK)
        return carry

    lax.fori_loop(0, table_ref.shape[0] // CHUNK, step, 0)


def factor_block(x_ref, u_ref, m_ref):
    n = x_ref.shape[0]
    tiles = [x_ref[8 * i : 8 * i + 8, :] for i in range(n // 8)]
    lane = lax.broadcasted_iota(jnp.int32, (8, n), 1)
    sub = lax.broadcasted_iota(jnp.int32, (8, n), 0)

    def column(tile, c):
        return jnp.broadcast_to(tile[:, c : c + 1], (8, n))

    for p in range(n // 8):
        c0 = 8 * p
        rows = [jnp.broadcast_to(tiles[p][r : r + 1, :], (8, n)) for r in range(8)]
        a = [[column(rows[r], c0 + c) if c >= r else None for c in range(8)] for r in range(8)]
        cols = {i: [column(tiles[i], c0 + k) for k in range(8)] for i in range(p + 1, n // 8)}
        m = [[None] * 8 for _ in range(8)]
        inverse = [None] * 8
        for k in range(8):
            inverse[k] = pltpu.reciprocal(a[k][k])
            for i in range(k + 1, 8):
                f = a[k][i] * inverse[k]
                for j in range(i, 8):
                    a[i][j] = a[i][j] - f * a[k][j]
                for j in range(k):
                    m[i][j] = m[i][j] - f * m[k][j]
                m[i][k] = -f
        panel = (lane >= c0) & (lane < c0 + 8)
        v = [jnp.where(panel, jnp.where(lane == c0 + k, 1.0, 0.0), rows[k]) for k in range(8)]
        y, u = [], []
        for i in range(8):
            yi, ui = v[i], rows[i]
            for k in range(i):
                yi = yi + m[i][k] * v[k]
                ui = ui + m[i][k] * rows[k]
            y.append(yi)
            u.append(ui)
        scaled = [y[i] * inverse[i] for i in range(8)]
        for i in range(p + 1, n // 8):
            xi = jnp.where(panel, 0.0, tiles[i])
            for k in range(8):
                ck = cols[i][k]
                for j in range(k):
                    ck = ck + m[k][j] * cols[i][j]
                xi = xi - ck * scaled[k]
            tiles[i] = xi
        yt, ut = y[0], u[0]
        for i in range(1, 8):
            yt = jnp.where(sub == i, y[i], yt)
            ut = jnp.where(sub == i, u[i], ut)
        u_ref[c0 : c0 + 8, :] = ut
        m_ref[c0 : c0 + 8, :] = yt


def factor_and_inverse(g11, g12, g22, w_ref, r_ref, x, u, m):
    h = g11.shape[0]
    rowi = lax.broadcasted_iota(jnp.int32, (h, h), 0)
    coli = lax.broadcasted_iota(jnp.int32, (h, h), 1)

    def finish():
        upper = u[...]
        d = jnp.sum(jnp.where(rowi == coli, upper, 0.0), axis=1, keepdims=True)
        s = lax.rsqrt(d)
        return jnp.where(rowi <= coli, upper, 0.0) * s, jnp.where(rowi >= coli, m[...], 0.0) * s

    x[...] = g11
    factor_block(x, u, m)
    r11, m1 = finish()
    r12 = dot(m1, g12)
    x[...] = g22 - dot(r12, r12, 0, 0)
    factor_block(x, u, m)
    r22, m2 = finish()
    zero = jnp.zeros((h, h), jnp.float32)
    r_ref[:h, :h], r_ref[:h, h:], r_ref[h:, :h], r_ref[h:, h:] = r11, r12, zero, r22
    w_ref[:h, :h], w_ref[h:, h:], w_ref[h:, :h] = m1.T, m2.T, zero
    w_ref[:h, h:] = -dot(m1, dot(r12, m2, 1, 1), 0, 0)


def first_factor_kernel(odd_ref, mine_ref, other_ref, w_ref, r_ref, diag_ref, x, u, m):
    h = x.shape[0]
    lo, hi = order_halves(odd_ref[0], mine_ref[...], other_ref[...])
    g11, g12, g22 = unpack_one(jnp.concatenate([lo, hi], axis=0), h)
    eye = lax.broadcasted_iota(jnp.int32, (h, h), 0) == lax.broadcasted_iota(jnp.int32, (h, h), 1)
    diag_ref[:, :h] = jnp.sum(jnp.where(eye, g11, 0.0), axis=0, keepdims=True)
    diag_ref[:, h:] = jnp.sum(jnp.where(eye, g22, 0.0), axis=0, keepdims=True)
    factor_and_inverse(g11, g12, g22, w_ref, r_ref, x, u, m)


def middle_kernel(odd_ref, s_ref, own_ref, back_ref, w_ref, q_ref, f_ref, keep_ref, send_ref):
    parts, nodes, width = s_ref.shape
    h = width // 2
    w = w_ref[...]
    q = dot(s_ref[...].reshape(-1, width), w)
    q_ref[...] = q
    f_ref[...] = own_ref[...]
    f_ref[:, nodes - SEC_NODES :, :] += back_ref[...]
    f = dot(f_ref[...].reshape(-1, width), w)
    f_ref[...] = f.reshape(parts, nodes, width)
    gram = dot(q, q, 0, 0)
    energy = dot(q, f, 0, 0)
    rowi = lax.broadcasted_iota(jnp.int32, (width, width), 0)
    coli = lax.broadcasted_iota(jnp.int32, (width, width), 1)
    both = jnp.where(rowi < coli, gram, energy)
    diag = jnp.sum(jnp.where(rowi == coli, gram, 0.0), axis=0, keepdims=True)
    lo = jnp.concatenate([both[:, :h], jnp.broadcast_to(diag[:, :h], (8, h))], axis=0)
    hi = jnp.concatenate([both[:, h:], jnp.broadcast_to(diag[:, h:], (8, h))], axis=0)
    keep_ref[...], send_ref[...] = order_halves(odd_ref[0], lo, hi)


def final_kernel(
    rows_all, odd_ref, mine_ref, other_ref, q_ref, f_ref, w1_ref, r1_ref,
    basis_ref, forces_ref, reduced_ref, coef_ref, w2, r2, x, u, m,
):
    parts, nodes, width = f_ref.shape
    h = width // 2
    root = math.sqrt(rows_all)
    lo, hi = order_halves(odd_ref[0], mine_ref[...], other_ref[...])
    both = jnp.concatenate([lo[:width], hi[:width]], axis=1)
    diag = jnp.concatenate([lo[width : width + 1], hi[width : width + 1]], axis=1)
    rowi = lax.broadcasted_iota(jnp.int32, (width, width), 0)
    coli = lax.broadcasted_iota(jnp.int32, (width, width), 1)
    flipped = both.T
    gram = jnp.where(rowi < coli, both, jnp.where(rowi > coli, flipped, diag))
    energy = jnp.where(rowi < coli, flipped, both)
    eye = jnp.where(rowi == coli, 1.0, 0.0)

    def upper_half(e):
        return jnp.where(rowi < coli, e, jnp.where(rowi == coli, 0.5 * e, 0.0))

    def largest(e):
        return jnp.max(jnp.abs(e))

    e0 = gram - eye
    size = jnp.sum(e0 * e0)

    @pl.when(size < 0.04)
    def _():
        w2[...] = eye - upper_half(e0)

        def residual():
            w = w2[...]
            return dot(w, dot(gram, w), 0, 0) - eye

        def more(state):
            return (state[0] > 1e-6) & (state[1] < 6)

        def improve(state):
            e = residual()
            w2[...] = w2[...] - dot(w2[...], upper_half(e))
            return largest(e) ** 2, state[1] + 1

        lax.while_loop(more, improve, (jnp.float32(1.0), jnp.int32(0)))
        r2[...] = jnp.where(rowi <= coli, dot(w2[...], gram, 0, 0), 0.0)

    @pl.when(jnp.logical_not(size < 0.04))
    def _():
        factor_and_inverse(gram[:h, :h], gram[:h, h:], gram[h:, h:], w2, r2, x, u, m)

    w = w2[...]
    basis_ref[...] = dot(q_ref[...], w * root).reshape(parts, nodes, width)
    forces_ref[...] = dot(f_ref[...].reshape(-1, width), w * root).reshape(parts, nodes, width)
    reduced_ref[...] = dot(w, dot(energy, w), 0, 0)
    r1 = r1_ref[...]
    r1 = r1 + dot(eye - dot(r1, w1_ref[...]), r1)
    coef_ref[...] = jnp.where(rowi <= coli, dot(r2[...], r1), 0.0) * (1.0 / root)


def local(snapshots, member_ends, member_dir, member_stiff):
    parts, nodes, width = snapshots.shape
    h = width // 2
    count = math.prod(lax.axis_size(a) for a in AXES)
    rows_all = parts * nodes * count
    odd = (lax.axis_index(AXES) % 2).astype(jnp.int32).reshape(1)
    square = (width, width)
    field = (parts, nodes, width)
    level = (parts, SEC_NODES, width)
    scratch = [pltpu.VMEM((h, h), jnp.float32)] * 3
    quarter = (5 * width // 8, h)

    keep, send, top = call(gram_kernel, [quarter, quarter, level], (odd, snapshots), [SMEM, VMEM])
    below = shifted(top, "span", 1)
    mine, other = sum_over_devices(keep, send)

    ends = member_ends.astype(jnp.float32)
    table = jnp.concatenate([ends, member_dir, member_stiff[None], jnp.zeros_like(ends)], axis=0).T
    own, back = call(
        member_kernel,
        [field, level],
        (snapshots, below, member_ends, table),
        scratch=[pltpu.VMEM((3, parts, nodes + SEC_NODES, width), jnp.bfloat16)],
    )
    returned = shifted(back, "span", -1)

    w1, r1, diag = call(
        first_factor_kernel, [square, square, (1, width)], (odd, mine, other), [SMEM, VMEM, VMEM], scratch
    )
    column_energy = jnp.log(diag[0] / rows_all)

    half = (width + 8, h)
    q, f, keep, send = call(
        middle_kernel,
        [(parts * nodes, width), field, half, half],
        (odd, snapshots, own, returned, w1),
        [SMEM] + [VMEM] * 4,
    )
    mine, other = sum_over_devices(keep, send)
    basis, forces, reduced, coef = call(
        lambda *refs: final_kernel(rows_all, *refs),
        [field, field, square, square],
        (odd, mine, other, q, f, w1, r1),
        [SMEM] + [VMEM] * 6,
        [pltpu.VMEM(square, jnp.float32)] * 2 + scratch,
    )
    return (basis, forces, reduced, coef, column_energy)


def solution(mesh):
    placed = (
        P(None, AXES, None),
        P(None, AXES),
        P(None, AXES),
        P(AXES),
    )
    return jax.shard_map(
        local,
        mesh=mesh,
        in_specs=placed,
        out_specs=(P(None, AXES, None), P(None, AXES, None), P(), P(), P()),
        check_vma=False,
    )
```

```python
import math

import jax
import jax.numpy as jnp
from jax import lax
from jax.experimental import pallas as pl
from jax.experimental.pallas import tpu as pltpu
from jax.sharding import PartitionSpec as P

AXES = ("span", "xsec", "leaf")
SEC_NODES = 128
CHUNK = 256
highest = lax.Precision.HIGHEST
VMEM = pl.BlockSpec(memory_space=pltpu.VMEM)
SMEM = pl.BlockSpec(memory_space=pltpu.SMEM)
ANY = pl.BlockSpec(memory_space=pl.ANY)


def dot(a, b, ca=1, cb=0):
    return lax.dot_general(
        a, b, (((ca,), (cb,)), ((), ())), precision=highest, preferred_element_type=jnp.float32
    )


def call(kernel, shapes, operands, specs=None, scratch=()):
    return pl.pallas_call(
        kernel,
        out_shape=tuple(jax.ShapeDtypeStruct(s, jnp.float32) for s in shapes),
        in_specs=specs or [VMEM] * len(operands),
        out_specs=tuple(VMEM for _ in shapes),
        scratch_shapes=list(scratch),
        compiler_params=pltpu.CompilerParams(vmem_limit_bytes=48 << 20),
    )(*operands)


def exchange(array, bit):
    count = math.prod(lax.axis_size(a) for a in AXES)
    return lax.ppermute(array, AXES, [(i, i ^ bit) for i in range(count)])


def add_kernel(a_ref, b_ref, *rest):
    rest[-1][...] = a_ref[...] + b_ref[...]


def add(a, b, beside):
    return call(add_kernel, [a.shape], (a, b, *beside), [VMEM, VMEM] + [ANY] * len(beside))[0]


def after(array, tie):
    return pl.pallas_call(
        lambda *refs: None,
        out_shape=jax.ShapeDtypeStruct(array.shape, array.dtype),
        in_specs=[ANY, ANY],
        out_specs=ANY,
        input_output_aliases={0: 0},
    )(array, tie)


def sum_over_devices(keep, send, beside=()):
    count = math.prod(lax.axis_size(a) for a in AXES)
    total = add(keep, exchange(send, 1), ())
    bit, waiting = 2, list(beside)
    while bit < count:
        received = exchange(total, bit)
        done = waiting.pop(0)(total) if waiting else ()
        total = add(total, received, done)
        bit *= 2
    for work in waiting:
        work(total)
    return total, exchange(total, 1)


def shifted(array, axis, by):
    length = lax.axis_size(axis)
    pairs = [(i, i + by) for i in range(length) if 0 <= i + by < length]
    return lax.ppermute(array, axis, pairs)


def order_halves(odd, mine, other):
    return jnp.where(odd == 0, mine, other), jnp.where(odd == 0, other, mine)


def pack_one(gram):
    h, q = gram.shape[0] // 2, gram.shape[0] // 4
    g11, g12, g22 = gram[:h, :h], gram[:h, h:], gram[h:, h:]
    lane = lax.broadcasted_iota(jnp.int32, (q, h), 1)
    corner = jnp.where(lane < q, pltpu.roll(g11[q:], q, 1), g22[q:])
    return jnp.concatenate([g11[:q], g22[:q], corner, g12], axis=0)


def unpack_one(rows, h):
    q = h // 2
    lane = lax.broadcasted_iota(jnp.int32, (q, h), 1)
    corner = rows[2 * q : 3 * q]

    def block(top, low):
        square = jnp.concatenate([top, low], axis=0)
        flipped = square.T[q:]
        return jnp.concatenate([top, jnp.where(lane < q, flipped, low)], axis=0)

    g11 = block(rows[:q], pltpu.roll(corner, q, 1))
    g22 = block(rows[q : 2 * q], corner)
    return g11, rows[3 * q :], g22


def gram_kernel(odd_ref, s_ref, keep_ref, send_ref, top_ref):
    nodes = s_ref.shape[1]
    top_ref[...] = s_ref[:, nodes - SEC_NODES :, :]
    flat = s_ref[...].reshape(-1, s_ref.shape[2])
    packed = pack_one(dot(flat, flat, 0, 0))
    half = packed.shape[0] // 2
    keep_ref[...], send_ref[...] = order_halves(odd_ref[0], packed[:half], packed[half:])


def pieces_of(x):
    first = x.astype(jnp.bfloat16)
    rest = x - first.astype(jnp.float32)
    second = rest.astype(jnp.bfloat16)
    third = (rest - second.astype(jnp.float32)).astype(jnp.bfloat16)
    return first, second, third


def picks(node_count, first, second):
    node = lax.broadcasted_iota(jnp.int32, (first.shape[0], node_count), 1).astype(jnp.float32)
    pick = (node == first).astype(jnp.float32) - (node == second).astype(jnp.float32)
    return pick.astype(jnp.bfloat16)


def picked(pick, pieces):
    return sum(jnp.dot(pick, piece, preferred_element_type=jnp.float32) for piece in pieces)


def own_elongation_kernel(table_ref, s_ref, tie_ref, long_ref):
    del tie_ref
    nodes = s_ref.shape[1]
    pieces = [pieces_of(s_ref[c]) for c in range(3)]
    for start in range(0, table_ref.shape[0], CHUNK):
        table = table_ref[start : start + CHUNK, :]
        pick = picks(nodes, table[:, 0:1], table[:, 1:2])
        long_ref[start : start + CHUNK, :] = sum(table[:, 2 + c : 3 + c] * picked(pick, pieces[c]) for c in range(3))


def member_kernel(table_ref, ends_ref, long_ref, below_ref, *rest):
    own_ref, back_ref = rest[-2:]
    nodes = own_ref.shape[1]
    if len(rest) > 3:
        own_ref[...], back_ref[...] = rest[0][...], rest[1][...]
    else:
        own_ref[...], back_ref[...] = jnp.zeros_like(own_ref), jnp.zeros_like(back_ref)
    pieces = [pieces_of(below_ref[c]) for c in range(3)]
    for start in range(0, table_ref.shape[0], CHUNK):
        table = table_ref[start : start + CHUNK, :]
        pick = picks(SEC_NODES, table[:, 0:1] - nodes, table[:, 1:2] - nodes)
        elongation = long_ref[start : start + CHUNK, :]
        elongation += sum(table[:, 2 + c : 3 + c] * picked(pick, pieces[c]) for c in range(3))
        axial = elongation * table[:, 5:6]
        ends = ends_ref[:, start : start + CHUNK]
        node = lax.broadcasted_iota(jnp.int32, (nodes + SEC_NODES, CHUNK), 0)
        spread = (node == ends[0:1]).astype(jnp.float32) - (node == ends[1:2]).astype(jnp.float32)
        spread = spread.astype(jnp.bfloat16)
        for c in range(3):
            force = picked(spread, pieces_of(table[:, 2 + c : 3 + c] * axial))
            own_ref[c] += force[:nodes]
            back_ref[c] += force[nodes:]


def factor_block(x_ref, u_ref, m_ref):
    n = x_ref.shape[0]
    tiles = [x_ref[8 * i : 8 * i + 8, :] for i in range(n // 8)]
    lane = lax.broadcasted_iota(jnp.int32, (8, n), 1)
    sub = lax.broadcasted_iota(jnp.int32, (8, n), 0)

    def column(tile, c):
        return jnp.broadcast_to(tile[:, c : c + 1], (8, n))

    for p in range(n // 8):
        c0 = 8 * p
        rows = [jnp.broadcast_to(tiles[p][r : r + 1, :], (8, n)) for r in range(8)]
        a = [[column(rows[r], c0 + c) if c >= r else None for c in range(8)] for r in range(8)]
        cols = {i: [column(tiles[i], c0 + k) for k in range(8)] for i in range(p + 1, n // 8)}
        m = [[None] * 8 for _ in range(8)]
        inverse = [None] * 8
        for k in range(8):
            inverse[k] = pltpu.reciprocal(a[k][k])
            for i in range(k + 1, 8):
                f = a[k][i] * inverse[k]
                for j in range(i, 8):
                    a[i][j] = a[i][j] - f * a[k][j]
                for j in range(k):
                    m[i][j] = m[i][j] - f * m[k][j]
                m[i][k] = -f
        panel = (lane >= c0) & (lane < c0 + 8)
        v = [jnp.where(panel, jnp.where(lane == c0 + k, 1.0, 0.0), rows[k]) for k in range(8)]
        y, u = [], []
        for i in range(8):
            yi, ui = v[i], rows[i]
            for k in range(i):
                yi = yi + m[i][k] * v[k]
                ui = ui + m[i][k] * rows[k]
            y.append(yi)
            u.append(ui)
        scaled = [y[i] * inverse[i] for i in range(8)]
        for i in range(p + 1, n // 8):
            xi = jnp.where(panel, 0.0, tiles[i])
            for k in range(8):
                ck = cols[i][k]
                for j in range(k):
                    ck = ck + m[k][j] * cols[i][j]
                xi = xi - ck * scaled[k]
            tiles[i] = xi
        yt, ut = y[0], u[0]
        for i in range(1, 8):
            yt = jnp.where(sub == i, y[i], yt)
            ut = jnp.where(sub == i, u[i], ut)
        u_ref[c0 : c0 + 8, :] = ut
        m_ref[c0 : c0 + 8, :] = yt


def factor_and_inverse(g11, g12, g22, w_ref, r_ref, x, u, m):
    h = g11.shape[0]
    rowi = lax.broadcasted_iota(jnp.int32, (h, h), 0)
    coli = lax.broadcasted_iota(jnp.int32, (h, h), 1)

    def finish():
        upper = u[...]
        d = jnp.sum(jnp.where(rowi == coli, upper, 0.0), axis=1, keepdims=True)
        s = lax.rsqrt(d)
        return jnp.where(rowi <= coli, upper, 0.0) * s, jnp.where(rowi >= coli, m[...], 0.0) * s

    x[...] = g11
    factor_block(x, u, m)
    r11, m1 = finish()
    r12 = dot(m1, g12)
    x[...] = g22 - dot(r12, r12, 0, 0)
    factor_block(x, u, m)
    r22, m2 = finish()
    zero = jnp.zeros((h, h), jnp.float32)
    r_ref[:h, :h], r_ref[:h, h:], r_ref[h:, :h], r_ref[h:, h:] = r11, r12, zero, r22
    w_ref[:h, :h], w_ref[h:, h:], w_ref[h:, :h] = m1.T, m2.T, zero
    w_ref[:h, h:] = -dot(m1, dot(r12, m2, 1, 1), 0, 0)


def first_factor_kernel(odd_ref, mine_ref, other_ref, w_ref, r_ref, diag_ref, x, u, m):
    h = x.shape[0]
    lo, hi = order_halves(odd_ref[0], mine_ref[...], other_ref[...])
    g11, g12, g22 = unpack_one(jnp.concatenate([lo, hi], axis=0), h)
    eye = lax.broadcasted_iota(jnp.int32, (h, h), 0) == lax.broadcasted_iota(jnp.int32, (h, h), 1)
    diag_ref[:, :h] = jnp.sum(jnp.where(eye, g11, 0.0), axis=0, keepdims=True)
    diag_ref[:, h:] = jnp.sum(jnp.where(eye, g22, 0.0), axis=0, keepdims=True)
    factor_and_inverse(g11, g12, g22, w_ref, r_ref, x, u, m)


def middle_kernel(odd_ref, s_ref, own_ref, back_ref, w_ref, q_ref, f_ref, keep_ref, send_ref):
    parts, nodes, width = s_ref.shape
    h = width // 2
    w = w_ref[...]
    q = dot(s_ref[...].reshape(-1, width), w)
    q_ref[...] = q
    f_ref[...] = own_ref[...]
    f_ref[:, nodes - SEC_NODES :, :] += back_ref[...]
    f = dot(f_ref[...].reshape(-1, width), w)
    f_ref[...] = f.reshape(parts, nodes, width)
    gram = dot(q, q, 0, 0)
    energy = dot(q, f, 0, 0)
    rowi = lax.broadcasted_iota(jnp.int32, (width, width), 0)
    coli = lax.broadcasted_iota(jnp.int32, (width, width), 1)
    both = jnp.where(rowi < coli, gram, energy)
    diag = jnp.sum(jnp.where(rowi == coli, gram, 0.0), axis=0, keepdims=True)
    lo = jnp.concatenate([both[:, :h], jnp.broadcast_to(diag[:, :h], (8, h))], axis=0)
    hi = jnp.concatenate([both[:, h:], jnp.broadcast_to(diag[:, h:], (8, h))], axis=0)
    keep_ref[...], send_ref[...] = order_halves(odd_ref[0], lo, hi)


def refine_kernel(w_ref, r_ref, tie_ref, out_ref):
    del tie_ref
    r = r_ref[...]
    size = r.shape[0]
    eye = lax.broadcasted_iota(jnp.int32, (size, size), 0) == lax.broadcasted_iota(jnp.int32, (size, size), 1)
    out_ref[...] = r + dot(jnp.where(eye, 1.0, 0.0) - dot(r, w_ref[...]), r)


def final_kernel(
    rows_all, odd_ref, mine_ref, other_ref, q_ref, f_ref, r1_ref,
    basis_ref, forces_ref, reduced_ref, coef_ref, w2, r2, x, u, m,
):
    parts, nodes, width = f_ref.shape
    h = width // 2
    root = math.sqrt(rows_all)
    lo, hi = order_halves(odd_ref[0], mine_ref[...], other_ref[...])
    both = jnp.concatenate([lo[:width], hi[:width]], axis=1)
    diag = jnp.concatenate([lo[width : width + 1], hi[width : width + 1]], axis=1)
    rowi = lax.broadcasted_iota(jnp.int32, (width, width), 0)
    coli = lax.broadcasted_iota(jnp.int32, (width, width), 1)
    flipped = both.T
    gram = jnp.where(rowi < coli, both, jnp.where(rowi > coli, flipped, diag))
    energy = jnp.where(rowi < coli, flipped, both)
    eye = jnp.where(rowi == coli, 1.0, 0.0)

    def upper_half(e):
        return jnp.where(rowi < coli, e, jnp.where(rowi == coli, 0.5 * e, 0.0))

    def largest(e):
        return jnp.max(jnp.abs(e))

    e0 = gram - eye
    size = jnp.sum(e0 * e0)

    @pl.when(size < 0.04)
    def _():
        w2[...] = eye - upper_half(e0)

        def residual():
            w = w2[...]
            return dot(w, dot(gram, w), 0, 0) - eye

        def more(state):
            return (state[0] > 1e-6) & (state[1] < 6)

        def improve(state):
            e = residual()
            w2[...] = w2[...] - dot(w2[...], upper_half(e))
            return largest(e) ** 2, state[1] + 1

        lax.while_loop(more, improve, (jnp.float32(1.0), jnp.int32(0)))
        r2[...] = jnp.where(rowi <= coli, dot(w2[...], gram, 0, 0), 0.0)

    @pl.when(jnp.logical_not(size < 0.04))
    def _():
        factor_and_inverse(gram[:h, :h], gram[:h, h:], gram[h:, h:], w2, r2, x, u, m)

    w = w2[...]
    basis_ref[...] = dot(q_ref[...], w * root).reshape(parts, nodes, width)
    forces_ref[...] = dot(f_ref[...].reshape(-1, width), w * root).reshape(parts, nodes, width)
    reduced_ref[...] = dot(w, dot(energy, w), 0, 0)
    coef_ref[...] = jnp.where(rowi <= coli, dot(r2[...], r1_ref[...]), 0.0) * (1.0 / root)


def local(snapshots, member_ends, member_dir, member_stiff):
    parts, nodes, width = snapshots.shape
    h = width // 2
    count = math.prod(lax.axis_size(a) for a in AXES)
    rows_all = parts * nodes * count
    odd = (lax.axis_index(AXES) % 2).astype(jnp.int32).reshape(1)
    square = (width, width)
    field = (parts, nodes, width)
    level = (parts, SEC_NODES, width)
    scratch = [pltpu.VMEM((h, h), jnp.float32)] * 3
    quarter = (5 * width // 8, h)

    keep, send, top = call(gram_kernel, [quarter, quarter, level], (odd, snapshots), [SMEM, VMEM])
    below = shifted(top, "span", 1)
    ends = member_ends.astype(jnp.float32)
    table = jnp.concatenate([ends, member_dir, member_stiff[None], jnp.zeros_like(ends)], axis=0).T
    split = table.shape[0] // 2
    lows, highs = table[:split], table[split:]
    held = {}

    def own_part(name, rows):
        def work(tie):
            held[name] = call(own_elongation_kernel, [(split, width)], (rows, snapshots, tie), [VMEM, VMEM, ANY])
            return held[name]

        return work

    def member_part(name, rows, ends_of, before):
        def work(tie):
            given = held.get(before, ())
            operands = (rows, ends_of, held[name][0], below, *given, tie)
            held["forces" + name] = call(
                member_kernel, [field, level], operands, [VMEM] * (len(operands) - 1) + [ANY]
            )
            return held["forces" + name]

        return work

    mine, other = sum_over_devices(
        keep,
        send,
        [
            own_part("a", lows),
            own_part("b", highs),
            member_part("a", lows, member_ends[:, :split], None),
            member_part("b", highs, member_ends[:, split:], "forcesa"),
        ],
    )
    own, back = held["forcesb"]
    returned = shifted(after(back, mine), "span", -1)

    w1, r1, diag = call(
        first_factor_kernel, [square, square, (1, width)], (odd, mine, other), [SMEM, VMEM, VMEM], scratch
    )
    column_energy = jnp.log(diag[0] / rows_all)

    half = (width + 8, h)
    q, f, keep, send = call(
        middle_kernel,
        [(parts * nodes, width), field, half, half],
        (odd, snapshots, own, returned, w1),
        [SMEM] + [VMEM] * 4,
    )
    refined = []

    def refine(tie):
        refined.extend(call(refine_kernel, [square], (w1, r1, tie), [VMEM, VMEM, ANY]))
        return refined

    mine, other = sum_over_devices(keep, send, [refine])
    basis, forces, reduced, coef = call(
        lambda *refs: final_kernel(rows_all, *refs),
        [field, field, square, square],
        (odd, mine, other, q, f, refined[0]),
        [SMEM] + [VMEM] * 5,
        [pltpu.VMEM(square, jnp.float32)] * 2 + scratch,
    )
    return (basis, forces, reduced, coef, column_energy)


def solution(mesh):
    placed = (
        P(None, AXES, None),
        P(None, AXES),
        P(None, AXES),
        P(AXES),
    )
    return jax.shard_map(
        local,
        mesh=mesh,
        in_specs=placed,
        out_specs=(P(None, AXES, None), P(None, AXES, None), P(), P(), P()),
        check_vma=False,
    )
```

```python
import functools
import math

import jax
import jax.numpy as jnp
from jax import lax
from jax.experimental import pallas as pl
from jax.experimental.pallas import tpu as pltpu
from jax.sharding import PartitionSpec as P

AXES = ("span", "xsec", "leaf")
SEC_NODES = 128
CHUNK = 256
highest = lax.Precision.HIGHEST
VMEM = pl.BlockSpec(memory_space=pltpu.VMEM)
ANY = pl.BlockSpec(memory_space=pl.ANY)
HBM = pl.BlockSpec(memory_space=pltpu.HBM)


def dot(a, b, ca=1, cb=0):
    return lax.dot_general(
        a, b, (((ca,), (cb,)), ((), ())), precision=highest, preferred_element_type=jnp.float32
    )


def halves(x):
    high = x.astype(jnp.bfloat16)
    return high, (x - high.astype(jnp.float32)).astype(jnp.bfloat16)


def dot3(a, b, ca=1, cb=0):
    def one(x, y):
        return lax.dot_general(x, y, (((ca,), (cb,)), ((), ())), preferred_element_type=jnp.float32)

    return one(a[0], b[0]) + (one(a[0], b[1]) + one(a[1], b[0]))


def call(kernel, shapes, operands, specs=None, scratch=()):
    return pl.pallas_call(
        kernel,
        out_shape=tuple(s if isinstance(s, jax.ShapeDtypeStruct) else jax.ShapeDtypeStruct(s, jnp.float32) for s in shapes),
        in_specs=specs or [VMEM] * len(operands),
        out_specs=tuple(VMEM for _ in shapes),
        scratch_shapes=list(scratch),
        compiler_params=pltpu.CompilerParams(vmem_limit_bytes=48 << 20),
    )(*operands)


def exchange(array, bit):
    count = math.prod(lax.axis_size(a) for a in AXES)
    return lax.ppermute(array, AXES, [(i, i ^ bit) for i in range(count)])


def add_kernel(terms, handed, *refs):
    outs = refs[len(refs) - 1 - handed :]
    parts = [ref[...] for ref in refs[:terms]]
    while len(parts) > 1:
        parts = [sum(parts[i : i + 2]) for i in range(0, len(parts), 2)]
    outs[0][...] = parts[0]
    for given, out in zip(refs[terms : terms + handed], outs[1:], strict=True):
        out[...] = given[...]


def add(parts, beside=(), through=()):
    operands = (*parts, *through, *beside)
    specs = [VMEM] * (len(parts) + len(through)) + [ANY] * len(beside)
    kernel = functools.partial(add_kernel, len(parts), len(through))
    outs = call(kernel, [parts[0].shape, *(t.shape for t in through)], operands, specs)
    return outs if through else outs[0]


def sum_steps():
    count = math.prod(lax.axis_size(a) for a in AXES)
    bits = [1 << i for i in range(1, count.bit_length() - 1)]
    assert 1 << (len(bits) + 1) == count and len(bits) > 1
    return [(bits[0], bits[1], bits[0] | bits[1])] + [(bit,) for bit in bits[2:]]


def scatter_kernel(keep_ref, received_ref, mine_ref, *send_refs):
    place = lax.axis_index(AXES) // 2 % 4
    for i, ref in enumerate((mine_ref, *send_refs)):
        part = place ^ i
        ref[...] = (keep_ref[pl.ds(part, 1)] + received_ref[pl.ds(part, 1)])[0]


def gather_kernel(mine_ref, *rest):
    out_ref = rest[-1]
    place = lax.axis_index(AXES) // 2 % 4
    for i, ref in enumerate((mine_ref, *rest[:-1])):
        out_ref[pl.ds(place ^ i, 1)] = ref[...][None]


def sum_by_quarters(keep, send, work):
    first, *others = sum_steps()
    block = keep.shape[1:]
    mine, *parts = call(scatter_kernel, [block] * 4, (keep, exchange(send, 1)), [VMEM, VMEM])
    received = [exchange(part, bit) for part, bit in zip(parts, first, strict=True)]
    done = work(mine)
    mine = add((mine, *received), done[:1])
    for (bit,) in others:
        mine = add((mine, exchange(mine, bit)))
    received = [exchange(mine, bit) for bit in first]
    (total,) = call(gather_kernel, [keep.shape], (mine, *received), [VMEM] * 4)
    return total, exchange(total, 1), done


def shifted(array, axis, by):
    length = lax.axis_size(axis)
    pairs = [(i, i + by) for i in range(length) if 0 <= i + by < length]
    return lax.ppermute(array, axis, pairs)


def order_halves(mine, other):
    odd = lax.axis_index(AXES) % 2
    return jnp.where(odd == 0, mine, other), jnp.where(odd == 0, other, mine)


def pack_one(gram):
    h, q = gram.shape[0] // 2, gram.shape[0] // 4
    g11, g12, g22 = gram[:h, :h], gram[:h, h:], gram[h:, h:]
    lane = lax.broadcasted_iota(jnp.int32, (q, h), 1)
    corner = jnp.where(lane < q, pltpu.roll(g11[q:], q, 1), g22[q:])
    return jnp.concatenate([g11[:q], g22[:q], corner, g12], axis=0)


def unpack_one(rows, h):
    q = h // 2
    lane = lax.broadcasted_iota(jnp.int32, (q, h), 1)
    corner = rows[2 * q : 3 * q]

    def block(top, low):
        square = jnp.concatenate([top, low], axis=0)
        flipped = square.T[q:]
        return jnp.concatenate([top, jnp.where(lane < q, flipped, low)], axis=0)

    g11 = block(rows[:q], pltpu.roll(corner, q, 1))
    g22 = block(rows[q : 2 * q], corner)
    return g11, rows[3 * q :], g22


def gram_kernel(s_ref, keep_ref, send_ref, top_ref):
    nodes, width = s_ref.shape[1:]
    flat = s_ref[...].reshape(-1, width)
    packed = pack_one(dot(flat, flat, 0, 0))
    half = packed.shape[0] // 2
    keep_ref[...], send_ref[...] = order_halves(packed[:half], packed[half:])
    top_ref[...] = s_ref[:, nodes - SEC_NODES :, :]


def pieces_of(x):
    first = x.astype(jnp.bfloat16)
    rest = x - first.astype(jnp.float32)
    second = rest.astype(jnp.bfloat16)
    third = (rest - second.astype(jnp.float32)).astype(jnp.bfloat16)
    return first, second, third


def picks(node_count, first, second):
    node = lax.broadcasted_iota(jnp.int32, (first.shape[0], node_count), 1).astype(jnp.float32)
    pick = (node == first).astype(jnp.float32) - (node == second).astype(jnp.float32)
    return pick.astype(jnp.bfloat16)


def picked(pick, pieces):
    return sum(jnp.dot(pick, piece, preferred_element_type=jnp.float32) for piece in pieces)


def own_elongation(first, table, s_ref, long_ref):
    nodes = s_ref.shape[1]
    pieces = [pieces_of(s_ref[c]) for c in range(3)]
    for start in range(0, long_ref.shape[0], CHUNK):
        rows = table[first + start : first + start + CHUNK, :]
        pick = picks(nodes, rows[:, 0:1], rows[:, 1:2])
        long_ref[start : start + CHUNK, :] = sum(rows[:, 2 + c : 3 + c] * picked(pick, pieces[c]) for c in range(3))


def first_elongation_kernel(ends_ref, dir_ref, stiff_ref, s_ref, tie_ref, long_ref, table_ref):
    del tie_ref
    ends = ends_ref[...].astype(jnp.float32)
    table_ref[...] = jnp.concatenate([ends, dir_ref[...], stiff_ref[...], jnp.zeros_like(ends)], axis=0).T
    own_elongation(0, table_ref, s_ref, long_ref)


def second_elongation_kernel(table_ref, s_ref, tie_ref, long_ref):
    del tie_ref
    own_elongation(long_ref.shape[0], table_ref, s_ref, long_ref)


def member_kernel(first, table_ref, ends_ref, long_ref, below_ref, *rest):
    own_ref, back_ref = rest[-2:]
    nodes = own_ref.shape[1]
    if len(rest) > 3:
        own_ref[...], back_ref[...] = rest[0][...], rest[1][...]
    else:
        own_ref[...], back_ref[...] = jnp.zeros_like(own_ref), jnp.zeros_like(back_ref)
    pieces = [pieces_of(below_ref[c]) for c in range(3)]
    for start in range(0, long_ref.shape[0], CHUNK):
        table = table_ref[first + start : first + start + CHUNK, :]
        pick = picks(SEC_NODES, table[:, 0:1] - nodes, table[:, 1:2] - nodes)
        elongation = long_ref[start : start + CHUNK, :]
        elongation += sum(table[:, 2 + c : 3 + c] * picked(pick, pieces[c]) for c in range(3))
        axial = elongation * table[:, 5:6]
        ends = ends_ref[:, first + start : first + start + CHUNK]
        node = lax.broadcasted_iota(jnp.int32, (nodes + SEC_NODES, CHUNK), 0)
        spread = (node == ends[0:1]).astype(jnp.float32) - (node == ends[1:2]).astype(jnp.float32)
        spread = spread.astype(jnp.bfloat16)
        for c in range(3):
            force = picked(spread, pieces_of(table[:, 2 + c : 3 + c] * axial))
            own_ref[c] += force[:nodes]
            back_ref[c] += force[nodes:]


def factor_block(x_ref, u_ref, m_ref, rows_ref):
    n = x_ref.shape[0]
    count = n // 8
    tiles = [x_ref[8 * i : 8 * i + 8, :] for i in range(count)]
    lane = lax.broadcasted_iota(jnp.int32, (8, n), 1)
    sub = lax.broadcasted_iota(jnp.int32, (8, n), 0)

    def column(tile, c):
        return jnp.broadcast_to(tile[:, c : c + 1], (8, n))

    for p in range(count):
        c0 = 8 * p
        rows_ref[c0 : c0 + 8, :] = tiles[p]
        u = [rows_ref[pl.ds(c0 + r, 8, stride=0), :] for r in range(8)]
        a = [[column(u[r], c0 + c) if c >= r else None for c in range(8)] for r in range(8)]
        panel = (lane >= c0) & (lane < c0 + 8)
        v = [jnp.where(panel, jnp.where(lane == c0 + k, 1.0, 0.0), u[k]) for k in range(8)]
        cols = {t: [column(tiles[t], c0 + k) for k in range(8)] for t in range(p + 1, count)}
        for t in cols:
            tiles[t] = jnp.where(panel, 0.0, tiles[t])
        for k in range(8):
            inverse = pltpu.reciprocal(a[k][k])
            scaled = v[k] * inverse
            for i in range(k + 1, 8):
                f = a[k][i] * inverse
                for j in range(i, 8):
                    a[i][j] = a[i][j] - f * a[k][j]
                v[i] = v[i] - f * v[k]
                u[i] = u[i] - f * u[k]
                for t in cols:
                    cols[t][i] = cols[t][i] - f * cols[t][k]
            for t in cols:
                tiles[t] = tiles[t] - cols[t][k] * scaled
        yt, ut = v[0], u[0]
        for i in range(1, 8):
            yt = jnp.where(sub == i, v[i], yt)
            ut = jnp.where(sub == i, u[i], ut)
        u_ref[c0 : c0 + 8, :] = ut
        m_ref[c0 : c0 + 8, :] = yt


def factor_and_inverse(g11, g12, g22, w_ref, r_ref, x, u, m, rows):
    h = g11.shape[0]
    rowi = lax.broadcasted_iota(jnp.int32, (h, h), 0)
    coli = lax.broadcasted_iota(jnp.int32, (h, h), 1)

    def finish():
        upper = u[...]
        d = jnp.sum(jnp.where(rowi == coli, upper, 0.0), axis=1, keepdims=True)
        s = lax.rsqrt(d)
        return jnp.where(rowi <= coli, upper, 0.0) * s, jnp.where(rowi >= coli, m[...], 0.0) * s

    x[...] = g11
    factor_block(x, u, m, rows)
    r11, m1 = finish()
    r12 = dot(m1, g12)
    x[...] = g22 - dot(r12, r12, 0, 0)
    factor_block(x, u, m, rows)
    r22, m2 = finish()
    zero = jnp.zeros((h, h), jnp.float32)
    r_ref[:h, :h], r_ref[:h, h:], r_ref[h:, :h], r_ref[h:, h:] = r11, r12, zero, r22
    w_ref[:h, :h], w_ref[h:, h:], w_ref[h:, :h] = m1.T, m2.T, zero
    w_ref[:h, h:] = -dot(m1, dot(r12, m2, 1, 1), 0, 0)


def first_factor_kernel(mine_ref, other_ref, w_ref, r_ref, diag_ref, *scratch):
    h = scratch[0].shape[0]
    lo, hi = order_halves(mine_ref[...], other_ref[...])
    g11, g12, g22 = unpack_one(jnp.concatenate([lo, hi], axis=0), h)
    eye = lax.broadcasted_iota(jnp.int32, (h, h), 0) == lax.broadcasted_iota(jnp.int32, (h, h), 1)
    diag_ref[:, :h] = jnp.sum(jnp.where(eye, g11, 0.0), axis=0, keepdims=True)
    diag_ref[:, h:] = jnp.sum(jnp.where(eye, g22, 0.0), axis=0, keepdims=True)
    factor_and_inverse(g11, g12, g22, w_ref, r_ref, *scratch)


def middle_kernel(
    s_ref, own_ref, back_ref, w_ref, q_ref, f_ref, q_halves, f_halves, keep_ref, send_ref
):
    parts, nodes, width = s_ref.shape
    h = width // 2
    w = w_ref[...]
    q = dot(s_ref[...].reshape(-1, width), w)
    q_ref[...] = q.reshape(parts, nodes, width)
    f_ref[...] = own_ref[...]
    f_ref[:, nodes - SEC_NODES :, :] += back_ref[...]
    f = dot(f_ref[...].reshape(-1, width), w)
    f_ref[...] = f.reshape(parts, nodes, width)
    q, f = halves(q), halves(f)
    for i in range(2):
        q_halves[i] = q[i].reshape(parts, nodes, width)
        f_halves[i] = f[i].reshape(parts, nodes, width)
    gram = dot3(q, q, 0, 0)
    energy = dot3(q, f, 0, 0)
    rowi = lax.broadcasted_iota(jnp.int32, (width, width), 0)
    coli = lax.broadcasted_iota(jnp.int32, (width, width), 1)
    both = jnp.where(rowi < coli, gram, energy)
    diag = jnp.sum(jnp.where(rowi == coli, gram, 0.0), axis=0, keepdims=True)
    quarter = width // 4
    keep, send = order_halves(both[:, :h], both[:, h:])
    keep_diag, send_diag = order_halves(diag[:, :h], diag[:, h:])
    for i in range(4):
        keep_ref[i, :quarter], send_ref[i, :quarter] = (x[quarter * i : quarter * (i + 1)] for x in (keep, send))
        keep_ref[i, quarter:], send_ref[i, quarter:] = (jnp.broadcast_to(x, (8, h)) for x in (keep_diag, send_diag))


def refine_kernel(rows_all, w_ref, r_ref, diag_ref, tie_ref, out_ref, log_ref):
    del tie_ref
    r = r_ref[...]
    size = r.shape[0]
    eye = lax.broadcasted_iota(jnp.int32, (size, size), 0) == lax.broadcasted_iota(jnp.int32, (size, size), 1)
    log_ref[...] = jnp.log(diag_ref[...] / rows_all)
    out_ref[...] = r + dot(jnp.where(eye, 1.0, 0.0) - dot(r, w_ref[...]), r)


def final_kernel(
    rows_all, mine_ref, other_ref, q_ref, f_ref, q_halves, f_halves, r1_ref,
    basis_ref, forces_ref, reduced_ref, coef_ref, v_ref, e_ref, w2, r2, held, sems, *scratch,
):
    parts, _, width = f_ref.shape
    h = width // 2
    root = math.sqrt(rows_all)
    lo, hi = order_halves(mine_ref[...], other_ref[...])
    quarter = width // 4
    both = jnp.concatenate([x[:, :quarter].reshape(width, h) for x in (lo, hi)], axis=1)
    diag = jnp.concatenate([x[0, quarter : quarter + 1] for x in (lo, hi)], axis=1)
    rowi = lax.broadcasted_iota(jnp.int32, (width, width), 0)
    coli = lax.broadcasted_iota(jnp.int32, (width, width), 1)
    flipped = both.T
    energy = jnp.where(rowi < coli, flipped, both)
    eye = jnp.where(rowi == coli, 1.0, 0.0)
    start = jnp.where(rowi < coli, both, jnp.where(rowi > coli, flipped, diag - 1.0))

    def upper_half(e):
        return jnp.where(rowi < coli, e, jnp.where(rowi == coli, 0.5 * e, 0.0))

    e_ref[...] = start
    size = jnp.sum(start * start)

    @pl.when(size < 0.01)
    def _():
        first = upper_half(start)
        low = first.astype(jnp.bfloat16)
        p = jnp.dot(start.astype(jnp.bfloat16), low, preferred_element_type=jnp.float32)
        e = lax.dot_general(
            low, (first + p).astype(jnp.bfloat16), (((0,), (0,)), ((), ())), preferred_element_type=jnp.float32
        )
        upper = upper_half(e - (p + p.T))
        both = jnp.dot(low, upper.astype(jnp.bfloat16), preferred_element_type=jnp.float32)
        v_ref[...] = both - (first + upper)

    @pl.when((size >= 0.01) & (size < 0.04))
    def _():
        v_ref[...] = -upper_half(start)

        def improve(i, carry):
            e = e_ref[...]
            upper = upper_half(e)
            split = halves(upper)
            p = dot3(halves(e), split)
            e = dot3(split, halves(upper + p), 0, 0) - (p + p.T)
            e_ref[...] = e
            upper = upper_half(e)
            v = v_ref[...]
            v_ref[...] = v - (upper + dot3(halves(v), halves(upper)))
            return carry

        lax.fori_loop(0, 2, improve, 0)

    @pl.when(jnp.logical_not(size < 0.04))
    def _():
        square = start + eye
        factor_and_inverse(square[:h, :h], square[:h, h:], square[h:, h:], w2, r2, *scratch)
        v_ref[...] = w2[...] - eye

    v = v_ref[...]
    v_split = halves(v)
    copies = []
    for i, (source, split, target) in enumerate(((q_ref, q_halves, basis_ref), (f_ref, f_halves, forces_ref))):
        for c in range(parts):
            k = parts * i + c
            held[k] = (source[c] + dot3((split[0, c], split[1, c]), v_split)) * root
            copies.append(pltpu.make_async_copy(held.at[k], target.at[c], sems.at[k]))
            copies[-1].start()
    right = energy + dot3(halves(energy), v_split)
    reduced_ref[...] = right + dot3(v_split, halves(right), 0, 0)
    change = jnp.where(rowi <= coli, v.T + start + dot3(v_split, halves(start), 0, 0), 0.0)
    r1 = r1_ref[...]
    coef_ref[...] = (r1 + dot3(halves(change), halves(r1))) * (1.0 / root)
    for copy in copies:
        copy.wait()


def local(snapshots, member_ends, member_dir, member_stiff):
    parts, nodes, width = snapshots.shape
    h = width // 2
    count = math.prod(lax.axis_size(a) for a in AXES)
    rows_all = parts * nodes * count
    steps = sum_steps()
    square = (width, width)
    field = (parts, nodes, width)
    level = (parts, SEC_NODES, width)
    packed = (5 * width // 8, h)
    scratch = [pltpu.VMEM((h, h), jnp.float32)] * 4

    keep, send, top = call(gram_kernel, [packed, packed, level], (snapshots,), [VMEM])
    below = shifted(top, "span", 1)
    members = member_dir.shape[1]
    split = members // 2
    forces = []

    def member_part(i, tie):
        operands = (table, member_ends, long[i], below, *forces, tie)
        kernel = functools.partial(member_kernel, split * i)
        forces[:] = call(kernel, [field, level], operands, [VMEM] * (len(operands) - 1) + [ANY])

    total = add((keep, exchange(send, 1)))
    for i, bits in enumerate(steps):
        received = [exchange(total, bit) for bit in bits]
        if i == 0:
            first, table = call(
                first_elongation_kernel,
                [(split, width), (members, 8)],
                (member_ends, member_dir, member_stiff[None], snapshots, total),
                [VMEM] * 4 + [ANY],
            )
            second = call(second_elongation_kernel, [(split, width)], (table, snapshots, total), [VMEM, VMEM, ANY])
            long = [first, *second]
            total = add((total, *received), long)
        elif i < len(steps) - 1:
            if i == 1:
                member_part(0, total)
            total = add((total, *received), forces)
        else:
            if i == 1:
                member_part(0, total)
            member_part(1, total)
            total, back = add((total, *received), forces[:1], forces[1:])
    other = exchange(total, 1)
    returned = shifted(back, "span", -1)

    w1, r1, diag = call(
        first_factor_kernel, [square, square, (1, width)], (total, other), [VMEM, VMEM], scratch
    )

    half = (4, width // 4 + 8, h)
    two = jax.ShapeDtypeStruct((2, *field), jnp.bfloat16)
    q, f, q_halves, f_halves, keep, send = call(
        middle_kernel,
        [field, field, two, two, half, half],
        (snapshots, forces[0], returned, w1),
        [VMEM] * 4,
    )
    refine = functools.partial(refine_kernel, rows_all)
    total, other, (r1, column_energy) = sum_by_quarters(
        keep,
        send,
        lambda tie: call(refine, [square, (1, width)], (w1, r1, diag, tie), [VMEM] * 3 + [ANY]),
    )

    basis, forces, reduced, coef = pl.pallas_call(
        functools.partial(final_kernel, rows_all),
        out_shape=tuple(jax.ShapeDtypeStruct(s, jnp.float32) for s in (field, field, square, square)),
        in_specs=[VMEM] * 7,
        out_specs=(HBM, HBM, VMEM, VMEM),
        scratch_shapes=[pltpu.VMEM(square, jnp.float32)] * 4
        + [pltpu.VMEM((2 * parts, nodes, width), jnp.float32), pltpu.SemaphoreType.DMA((2 * parts,))]
        + scratch,
        compiler_params=pltpu.CompilerParams(vmem_limit_bytes=48 << 20),
    )(total, other, q, f, q_halves, f_halves, r1)
    return (basis, forces, reduced, coef, column_energy[0])


def solution(mesh):
    placed = (
        P(None, AXES, None),
        P(None, AXES),
        P(None, AXES),
        P(AXES),
    )
    return jax.shard_map(
        local,
        mesh=mesh,
        in_specs=placed,
        out_specs=(P(None, AXES, None), P(None, AXES, None), P(), P(), P()),
        check_vma=False,
    )
```

```python
import functools
import math

import jax
import jax.numpy as jnp
from jax import lax
from jax.experimental import pallas as pl
from jax.experimental.pallas import tpu as pltpu
from jax.sharding import PartitionSpec as P

AXES = ("span", "xsec", "leaf")
SEC_NODES = 128
NODES = 256
CHUNK = 256
highest = lax.Precision.HIGHEST
VMEM = pl.BlockSpec(memory_space=pltpu.VMEM)
ANY = pl.BlockSpec(memory_space=pl.ANY)
HBM = pl.BlockSpec(memory_space=pltpu.HBM)


def dot(a, b, ca=1, cb=0):
    return lax.dot_general(
        a, b, (((ca,), (cb,)), ((), ())), precision=highest, preferred_element_type=jnp.float32
    )


def halves(x):
    high = x.astype(jnp.bfloat16)
    return high, (x - high.astype(jnp.float32)).astype(jnp.bfloat16)


def dot3(a, b, ca=1, cb=0):
    def one(x, y):
        return lax.dot_general(x, y, (((ca,), (cb,)), ((), ())), preferred_element_type=jnp.float32)

    return one(a[0], b[0]) + (one(a[0], b[1]) + one(a[1], b[0]))


def call(kernel, shapes, operands, specs=None, scratch=()):
    return pl.pallas_call(
        kernel,
        out_shape=tuple(s if isinstance(s, jax.ShapeDtypeStruct) else jax.ShapeDtypeStruct(s, jnp.float32) for s in shapes),
        in_specs=specs or [VMEM] * len(operands),
        out_specs=tuple(VMEM for _ in shapes),
        scratch_shapes=list(scratch),
        compiler_params=pltpu.CompilerParams(vmem_limit_bytes=48 << 20),
    )(*operands)


def exchange(array, bit):
    count = math.prod(lax.axis_size(a) for a in AXES)
    return lax.ppermute(array, AXES, [(i, i ^ bit) for i in range(count)])


def add_kernel(terms, handed, *refs):
    outs = refs[len(refs) - 1 - handed :]
    parts = [ref[...] for ref in refs[:terms]]
    while len(parts) > 1:
        parts = [sum(parts[i : i + 2]) for i in range(0, len(parts), 2)]
    outs[0][...] = parts[0]
    for given, out in zip(refs[terms : terms + handed], outs[1:], strict=True):
        out[...] = given[...]


def add(parts, beside=(), through=()):
    operands = (*parts, *through, *beside)
    specs = [VMEM] * (len(parts) + len(through)) + [ANY] * len(beside)
    kernel = functools.partial(add_kernel, len(parts), len(through))
    outs = call(kernel, [parts[0].shape, *(t.shape for t in through)], operands, specs)
    return outs if through else outs[0]


def sum_steps():
    count = math.prod(lax.axis_size(a) for a in AXES)
    bits = [1 << i for i in range(1, count.bit_length() - 1)]
    assert 1 << (len(bits) + 1) == count and len(bits) > 1
    return [(bits[0], bits[1], bits[0] | bits[1])] + [(bit,) for bit in bits[2:]]


def scatter_kernel(keep_ref, received_ref, tie_ref, mine_ref, *send_refs):
    del tie_ref
    place = lax.axis_index(AXES) // 2 % 4
    for i, ref in enumerate((mine_ref, *send_refs)):
        part = place ^ i
        ref[...] = (keep_ref[pl.ds(part, 1)] + received_ref[pl.ds(part, 1)])[0]


def gather_kernel(mine_ref, *rest):
    out_ref = rest[-1]
    place = lax.axis_index(AXES) // 2 % 4
    for i, ref in enumerate((mine_ref, *rest[:-1])):
        out_ref[pl.ds(place ^ i, 1)] = ref[...][None]


def sum_by_quarters(keep, send, works):
    first, *others = sum_steps()
    others = [bit for (bit,) in others]
    others = [(*pair, sum(pair))[: 2 * len(pair) - 1] for pair in (others[i : i + 2] for i in range(0, len(others), 2))]
    block = keep.shape[1:]
    received = exchange(send, 1)
    tie = works[0](keep)
    mine, *parts = call(scatter_kernel, [block] * 4, (keep, received, tie), [VMEM, VMEM, ANY])
    received = [exchange(part, bit) for part, bit in zip(parts, first, strict=True)]
    handed = works[1](mine)
    mine = add((mine, *received), (handed,))
    for i, bits in enumerate(others):
        received = [exchange(mine, bit) for bit in bits]
        tie = works[2](mine) if i == 0 else ()
        if i < len(others) - 1:
            mine = add((mine, *received), tie)
        else:
            mine, handed = add((mine, *received), tie, (handed,))
    received = [exchange(mine, bit) for bit in first]
    (total,) = call(gather_kernel, [keep.shape], (mine, *received))
    return total, exchange(total, 1), handed


def shifted(array, axis, by, round_off=False):
    length = lax.axis_size(axis)
    pairs = [(i, (i + by) % length) for i in range(length) if round_off or 0 <= i + by < length]
    return lax.ppermute(array, axis, pairs)


def order_halves(mine, other):
    odd = lax.axis_index(AXES) % 2
    return jnp.where(odd == 0, mine, other), jnp.where(odd == 0, other, mine)


def pack_one(gram):
    h, q = gram.shape[0] // 2, gram.shape[0] // 4
    g11, g12, g22 = gram[:h, :h], gram[:h, h:], gram[h:, h:]
    lane = lax.broadcasted_iota(jnp.int32, (q, h), 1)
    corner = jnp.where(lane < q, pltpu.roll(g11[q:], q, 1), g22[q:])
    return jnp.concatenate([g11[:q], g22[:q], corner, g12], axis=0)


def unpack_one(rows, h):
    q = h // 2
    lane = lax.broadcasted_iota(jnp.int32, (q, h), 1)
    corner = rows[2 * q : 3 * q]

    def block(top, low):
        square = jnp.concatenate([top, low], axis=0)
        flipped = square.T[q:]
        return jnp.concatenate([top, jnp.where(lane < q, flipped, low)], axis=0)

    g11 = block(rows[:q], pltpu.roll(corner, q, 1))
    g22 = block(rows[q : 2 * q], corner)
    return g11, rows[3 * q :], g22


def gram_kernel(s_ref, keep_ref, send_ref, top_ref):
    nodes, width = s_ref.shape[1:]
    flat = s_ref[...].reshape(-1, width)
    packed = pack_one(dot(flat, flat, 0, 0))
    half = packed.shape[0] // 2
    keep_ref[...], send_ref[...] = order_halves(packed[:half], packed[half:])
    top_ref[...] = s_ref[:, nodes - SEC_NODES :, :]


def pieces_of(x):
    first = x.astype(jnp.bfloat16)
    rest = x - first.astype(jnp.float32)
    second = rest.astype(jnp.bfloat16)
    third = (rest - second.astype(jnp.float32)).astype(jnp.bfloat16)
    return first, second, third


def picks(node_count, first, second):
    node = lax.broadcasted_iota(jnp.int32, (first.shape[0], node_count), 1).astype(jnp.float32)
    pick = (node == first).astype(jnp.float32) - (node == second).astype(jnp.float32)
    return pick.astype(jnp.bfloat16)


def picked(pick, pieces):
    return sum(jnp.dot(pick, piece, preferred_element_type=jnp.float32) for piece in pieces)


def own_elongation(first, table, s_ref, long_ref):
    nodes = s_ref.shape[1]
    pieces = [pieces_of(s_ref[c]) for c in range(3)]
    for start in range(0, long_ref.shape[0], CHUNK):
        rows = table[first + start : first + start + CHUNK, :]
        pick = picks(nodes, rows[:, 0:1], rows[:, 1:2])
        long_ref[start : start + CHUNK, :] = sum(rows[:, 2 + c : 3 + c] * picked(pick, pieces[c]) for c in range(3))


def first_elongation_kernel(ends_ref, dir_ref, stiff_ref, s_ref, tie_ref, long_ref, table_ref):
    del tie_ref
    ends = ends_ref[...].astype(jnp.float32)
    table_ref[...] = jnp.concatenate([ends, dir_ref[...], stiff_ref[...], jnp.zeros_like(ends)], axis=0).T
    own_elongation(0, table_ref, s_ref, long_ref)


def second_elongation_kernel(table_ref, s_ref, tie_ref, long_ref):
    del tie_ref
    own_elongation(long_ref.shape[0], table_ref, s_ref, long_ref)


def below_elongation_kernel(table_ref, below_ref, first_ref, second_ref, tie_ref, long_ref):
    del tie_ref
    stands = lax.axis_index("span") == 0
    pieces = [pieces_of(jnp.where(stands, 0.0, below_ref[c])) for c in range(3)]
    split = first_ref.shape[0]
    for half, given in enumerate((first_ref, second_ref)):
        for start in range(0, split, CHUNK):
            at = split * half + start
            rows = table_ref[at : at + CHUNK, :]
            pick = picks(SEC_NODES, rows[:, 0:1] - NODES, rows[:, 1:2] - NODES)
            added = sum(rows[:, 2 + c : 3 + c] * picked(pick, pieces[c]) for c in range(3))
            long_ref[at : at + CHUNK, :] = given[start : start + CHUNK, :] + added


def force_kernel(first, count, table_ref, ends_ref, long_ref, tie_ref, *rest):
    del tie_ref
    own_ref, back_ref = rest[-2:]
    nodes = own_ref.shape[1]
    for start in range(first, first + count, CHUNK):
        rows = table_ref[start : start + CHUNK, :]
        axial = long_ref[start : start + CHUNK, :] * rows[:, 5:6]
        ends = ends_ref[:, start : start + CHUNK]
        node = lax.broadcasted_iota(jnp.int32, (nodes + SEC_NODES, CHUNK), 0)
        spread = (node == ends[0:1]).astype(jnp.float32) - (node == ends[1:2]).astype(jnp.float32)
        spread = spread.astype(jnp.bfloat16)
        for c in range(3):
            force = picked(spread, halves(rows[:, 2 + c : 3 + c] * axial))
            if start > first:
                given = own_ref[c], back_ref[c]
            elif len(rest) > 2:
                given = rest[0][c], rest[1][c]
            else:
                given = 0.0, 0.0
            own_ref[c] = given[0] + force[:nodes]
            back_ref[c] = given[1] + force[nodes:]


def factor_block(x_ref, u_ref, m_ref, rows_ref):
    n = x_ref.shape[0]
    count = n // 8
    tiles = [x_ref[8 * i : 8 * i + 8, :] for i in range(count)]
    lane = lax.broadcasted_iota(jnp.int32, (8, n), 1)
    sub = lax.broadcasted_iota(jnp.int32, (8, n), 0)

    def column(tile, c):
        return jnp.broadcast_to(tile[:, c : c + 1], (8, n))

    for p in range(count):
        c0 = 8 * p
        rows_ref[c0 : c0 + 8, :] = tiles[p]
        u = [rows_ref[pl.ds(c0 + r, 8, stride=0), :] for r in range(8)]
        a = [[column(u[r], c0 + c) if c >= r else None for c in range(8)] for r in range(8)]
        panel = (lane >= c0) & (lane < c0 + 8)
        v = [jnp.where(panel, jnp.where(lane == c0 + k, 1.0, 0.0), u[k]) for k in range(8)]
        cols = {t: [column(tiles[t], c0 + k) for k in range(8)] for t in range(p + 1, count)}
        for t in cols:
            tiles[t] = jnp.where(panel, 0.0, tiles[t])
        for k in range(8):
            inverse = pltpu.reciprocal(a[k][k])
            scaled = v[k] * inverse
            for i in range(k + 1, 8):
                f = a[k][i] * inverse
                for j in range(i, 8):
                    a[i][j] = a[i][j] - f * a[k][j]
                v[i] = v[i] - f * v[k]
                u[i] = u[i] - f * u[k]
                for t in cols:
                    cols[t][i] = cols[t][i] - f * cols[t][k]
            for t in cols:
                tiles[t] = tiles[t] - cols[t][k] * scaled
        yt, ut = v[0], u[0]
        for i in range(1, 8):
            yt = jnp.where(sub == i, v[i], yt)
            ut = jnp.where(sub == i, u[i], ut)
        u_ref[c0 : c0 + 8, :] = ut
        m_ref[c0 : c0 + 8, :] = yt


def factor_and_inverse(g11, g12, g22, w_ref, r_ref, x, u, m, rows):
    h = g11.shape[0]
    rowi = lax.broadcasted_iota(jnp.int32, (h, h), 0)
    coli = lax.broadcasted_iota(jnp.int32, (h, h), 1)

    def finish():
        upper = u[...]
        d = jnp.sum(jnp.where(rowi == coli, upper, 0.0), axis=1, keepdims=True)
        s = lax.rsqrt(d)
        return jnp.where(rowi <= coli, upper, 0.0) * s, jnp.where(rowi >= coli, m[...], 0.0) * s

    x[...] = g11
    factor_block(x, u, m, rows)
    r11, m1 = finish()
    r12 = dot(m1, g12)
    x[...] = g22 - dot(r12, r12, 0, 0)
    factor_block(x, u, m, rows)
    r22, m2 = finish()
    zero = jnp.zeros((h, h), jnp.float32)
    r_ref[:h, :h], r_ref[:h, h:], r_ref[h:, :h], r_ref[h:, h:] = r11, r12, zero, r22
    w_ref[:h, :h], w_ref[h:, h:], w_ref[h:, :h] = m1.T, m2.T, zero
    w_ref[:h, h:] = -dot(m1, dot(r12, m2, 1, 1), 0, 0)


def first_factor_kernel(mine_ref, other_ref, w_ref, r_ref, diag_ref, *scratch):
    h = scratch[0].shape[0]
    lo, hi = order_halves(mine_ref[...], other_ref[...])
    g11, g12, g22 = unpack_one(jnp.concatenate([lo, hi], axis=0), h)
    eye = lax.broadcasted_iota(jnp.int32, (h, h), 0) == lax.broadcasted_iota(jnp.int32, (h, h), 1)
    diag_ref[:, :h] = jnp.sum(jnp.where(eye, g11, 0.0), axis=0, keepdims=True)
    diag_ref[:, h:] = jnp.sum(jnp.where(eye, g22, 0.0), axis=0, keepdims=True)
    factor_and_inverse(g11, g12, g22, w_ref, r_ref, *scratch)


def middle_kernel(s_ref, long_ref, table_ref, w_ref, q_ref, q_halves, long_out, keep_ref, send_ref):
    parts, nodes, width = s_ref.shape
    h = width // 2
    w = w_ref[...]
    q = dot(s_ref[...].reshape(-1, width), w)
    q_ref[...] = q.reshape(parts, nodes, width)
    long = dot(long_ref[...], w)
    long_out[...] = long
    q = halves(q)
    for i in range(2):
        q_halves[i] = q[i].reshape(parts, nodes, width)
    gram = dot3(q, q, 0, 0)
    energy = dot3(halves(long), halves(long * table_ref[:, 5:6]), 0, 0)
    rowi = lax.broadcasted_iota(jnp.int32, (width, width), 0)
    coli = lax.broadcasted_iota(jnp.int32, (width, width), 1)
    both = jnp.where(rowi < coli, gram, energy)
    diag = jnp.sum(jnp.where(rowi == coli, gram, 0.0), axis=0, keepdims=True)
    quarter = width // 4
    keep, send = order_halves(both[:, :h], both[:, h:])
    keep_diag, send_diag = order_halves(diag[:, :h], diag[:, h:])
    for i in range(4):
        keep_ref[i, :quarter], send_ref[i, :quarter] = (x[quarter * i : quarter * (i + 1)] for x in (keep, send))
        keep_ref[i, quarter:], send_ref[i, quarter:] = (jnp.broadcast_to(x, (8, h)) for x in (keep_diag, send_diag))


def refine_kernel(rows_all, w_ref, r_ref, diag_ref, tie_ref, out_ref, log_ref):
    del tie_ref
    r = r_ref[...]
    size = r.shape[0]
    eye = lax.broadcasted_iota(jnp.int32, (size, size), 0) == lax.broadcasted_iota(jnp.int32, (size, size), 1)
    log_ref[...] = jnp.log(diag_ref[...] / rows_all)
    out_ref[...] = r + dot(jnp.where(eye, 1.0, 0.0) - dot(r, w_ref[...]), r)


def final_kernel(
    rows_all, mine_ref, other_ref, q_ref, q_halves, own_ref, back_ref, r1_ref,
    basis_ref, forces_ref, reduced_ref, coef_ref, v_ref, e_ref, w2, r2, held, sems, *scratch,
):
    parts, nodes, width = q_ref.shape
    h = width // 2
    root = math.sqrt(rows_all)
    lo, hi = order_halves(mine_ref[...], other_ref[...])
    quarter = width // 4
    both = jnp.concatenate([x[:, :quarter].reshape(width, h) for x in (lo, hi)], axis=1)
    diag = jnp.concatenate([x[0, quarter : quarter + 1] for x in (lo, hi)], axis=1)
    rowi = lax.broadcasted_iota(jnp.int32, (width, width), 0)
    coli = lax.broadcasted_iota(jnp.int32, (width, width), 1)
    flipped = both.T
    energy = jnp.where(rowi < coli, flipped, both)
    eye = jnp.where(rowi == coli, 1.0, 0.0)
    start = jnp.where(rowi < coli, both, jnp.where(rowi > coli, flipped, diag - 1.0))

    def upper_half(e):
        return jnp.where(rowi < coli, e, jnp.where(rowi == coli, 0.5 * e, 0.0))

    e_ref[...] = start
    size = jnp.sum(start * start)

    @pl.when(size < 0.02)
    def _():
        first = upper_half(start)
        low = first.astype(jnp.bfloat16)
        p = jnp.dot(start.astype(jnp.bfloat16), low, preferred_element_type=jnp.float32)
        e = lax.dot_general(
            low, (first + p).astype(jnp.bfloat16), (((0,), (0,)), ((), ())), preferred_element_type=jnp.float32
        )
        upper = upper_half(e - (p + p.T))
        both = jnp.dot(low, upper.astype(jnp.bfloat16), preferred_element_type=jnp.float32)
        v_ref[...] = both - (first + upper)

    @pl.when((size >= 0.02) & (size < 0.06))
    def _():
        v_ref[...] = -upper_half(start)

        def improve(i, carry):
            e = e_ref[...]
            upper = upper_half(e)
            split = halves(upper)
            p = dot3(halves(e), split)
            e = dot3(split, halves(upper + p), 0, 0) - (p + p.T)
            e_ref[...] = e
            upper = upper_half(e)
            v = v_ref[...]
            v_ref[...] = v - (upper + dot3(halves(v), halves(upper)))
            return carry

        lax.fori_loop(0, 2, improve, 0)

    @pl.when(jnp.logical_not(size < 0.06))
    def _():
        square = start + eye
        factor_and_inverse(square[:h, :h], square[:h, h:], square[h:, h:], w2, r2, *scratch)
        v_ref[...] = w2[...] - eye

    v = v_ref[...]
    v_split = halves(v)
    copies = []
    top = lax.axis_index("span") == lax.axis_size("span") - 1
    for k in range(2 * parts):
        c = k % parts
        if k < parts:
            source, split, target = q_ref[c], (q_halves[0, c], q_halves[1, c]), basis_ref
        else:
            returned = jnp.where(top, 0.0, back_ref[c])
            source = jnp.concatenate(
                [own_ref[c, : nodes - SEC_NODES], own_ref[c, nodes - SEC_NODES :] + returned], axis=0
            )
            split, target = halves(source), forces_ref
        held[k] = (source + dot3(split, v_split)) * root
        copies.append(pltpu.make_async_copy(held.at[k], target.at[c], sems.at[k]))
        copies[-1].start()
    right = energy + dot3(halves(energy), v_split)
    reduced_ref[...] = right + dot3(v_split, halves(right), 0, 0)
    change = jnp.where(rowi <= coli, v.T + start + dot3(v_split, halves(start), 0, 0), 0.0)
    r1 = r1_ref[...]
    coef_ref[...] = (r1 + dot3(halves(change), halves(r1))) * (1.0 / root)
    for copy in copies:
        copy.wait()


def local(snapshots, member_ends, member_dir, member_stiff):
    parts, nodes, width = snapshots.shape
    h = width // 2
    count = math.prod(lax.axis_size(a) for a in AXES)
    rows_all = parts * nodes * count
    steps = sum_steps()
    square = (width, width)
    field = (parts, nodes, width)
    level = (parts, SEC_NODES, width)
    packed = (5 * width // 8, h)
    scratch = [pltpu.VMEM((h, h), jnp.float32)] * 4

    keep, send, top = call(gram_kernel, [packed, packed, level], (snapshots,), [VMEM])
    below = shifted(top, "span", 1, True)
    members = member_dir.shape[1]
    split = members // 2
    total = add((keep, exchange(send, 1)))
    for i, bits in enumerate(steps):
        received = [exchange(total, bit) for bit in bits]
        if i == 0:
            first, table = call(
                first_elongation_kernel,
                [(split, width), (members, 8)],
                (member_ends, member_dir, member_stiff[None], snapshots, total),
                [VMEM] * 4 + [ANY],
            )
            second = call(second_elongation_kernel, [(split, width)], (table, snapshots, total), [VMEM, VMEM, ANY])
            long = [first, *second]
            total = add((total, *received), long)
        elif i < len(steps) - 1:
            total = add((total, *received))
        else:
            operands = (table, below, *long, total)
            (stretch,) = call(below_elongation_kernel, [(members, width)], operands, [VMEM] * 4 + [ANY])
            total = add((total, *received), (stretch,))
    other = exchange(total, 1)

    w1, r1, diag = call(
        first_factor_kernel, [square, square, (1, width)], (total, other), [VMEM, VMEM], scratch
    )

    half = (4, width // 4 + 8, h)
    q, q_halves, stretch, keep, send = call(
        middle_kernel,
        [field, jax.ShapeDtypeStruct((2, *field), jnp.bfloat16), (members, width), half, half],
        (snapshots, stretch, table, w1),
    )
    held = []

    def members_forces(tie):
        operands = (table, member_ends, stretch, tie, *held)
        first = split if held else 0
        kernel = functools.partial(force_kernel, first, split)
        held[:] = call(kernel, [field, level], operands, [VMEM] * 3 + [ANY] + [VMEM] * len(held))
        return held[1]

    def refined(tie):
        refine = functools.partial(refine_kernel, rows_all)
        r1_and_log.extend(call(refine, [square, (1, width)], (w1, r1, diag, tie), [VMEM] * 3 + [ANY]))
        return r1_and_log[:1]

    r1_and_log = []
    total, other, back = sum_by_quarters(keep, send, [members_forces, members_forces, refined])
    own = held[0]
    returned = shifted(back, "span", -1)
    r1, column_energy = r1_and_log

    basis, forces, reduced, coef = pl.pallas_call(
        functools.partial(final_kernel, rows_all),
        out_shape=tuple(jax.ShapeDtypeStruct(s, jnp.float32) for s in (field, field, square, square)),
        in_specs=[VMEM] * 7,
        out_specs=(HBM, HBM, VMEM, VMEM),
        scratch_shapes=[pltpu.VMEM(square, jnp.float32)] * 4
        + [pltpu.VMEM((2 * parts, nodes, width), jnp.float32), pltpu.SemaphoreType.DMA((2 * parts,))]
        + scratch,
        compiler_params=pltpu.CompilerParams(vmem_limit_bytes=48 << 20),
    )(total, other, q, q_halves, own, returned, r1)
    return (basis, forces, reduced, coef, column_energy[0])


def solution(mesh):
    placed = (
        P(None, AXES, None),
        P(None, AXES),
        P(None, AXES),
        P(AXES),
    )
    return jax.shard_map(
        local,
        mesh=mesh,
        in_specs=placed,
        out_specs=(P(None, AXES, None), P(None, AXES, None), P(), P(), P()),
        check_vma=False,
    )
```

```python
import functools
import math

import jax
import jax.numpy as jnp
from jax import lax
from jax.experimental import pallas as pl
from jax.experimental.pallas import tpu as pltpu
from jax.sharding import PartitionSpec as P

AXES = ("span", "xsec", "leaf")
SEC_NODES = 128
NODES = 256
CHUNK = 256
highest = lax.Precision.HIGHEST
VMEM = pl.BlockSpec(memory_space=pltpu.VMEM)
ANY = pl.BlockSpec(memory_space=pl.ANY)
HBM = pl.BlockSpec(memory_space=pltpu.HBM)


def dot(a, b, ca=1, cb=0):
    return lax.dot_general(
        a, b, (((ca,), (cb,)), ((), ())), precision=highest, preferred_element_type=jnp.float32
    )


def halves(x):
    high = x.astype(jnp.bfloat16)
    return high, (x - high.astype(jnp.float32)).astype(jnp.bfloat16)


def dot3(a, b, ca=1, cb=0):
    def one(x, y):
        return lax.dot_general(x, y, (((ca,), (cb,)), ((), ())), preferred_element_type=jnp.float32)

    return one(a[0], b[0]) + (one(a[0], b[1]) + one(a[1], b[0]))


def call(kernel, shapes, operands, specs=None, scratch=(), outs=None):
    return pl.pallas_call(
        kernel,
        out_shape=tuple(s if isinstance(s, jax.ShapeDtypeStruct) else jax.ShapeDtypeStruct(s, jnp.float32) for s in shapes),
        in_specs=specs or [VMEM] * len(operands),
        out_specs=outs or tuple(VMEM for _ in shapes),
        scratch_shapes=list(scratch),
        compiler_params=pltpu.CompilerParams(vmem_limit_bytes=48 << 20),
    )(*operands)


def exchange(array, bit):
    count = math.prod(lax.axis_size(a) for a in AXES)
    return lax.ppermute(array, AXES, [(i, i ^ bit) for i in range(count)])


def add_kernel(terms, handed, *refs):
    outs = refs[len(refs) - 1 - handed :]
    parts = [ref[...] for ref in refs[:terms]]
    while len(parts) > 1:
        parts = [sum(parts[i : i + 2]) for i in range(0, len(parts), 2)]
    outs[0][...] = parts[0]
    for given, out in zip(refs[terms : terms + handed], outs[1:], strict=True):
        out[...] = given[...]


def add(parts, beside=(), through=()):
    operands = (*parts, *through, *beside)
    specs = [VMEM] * (len(parts) + len(through)) + [ANY] * len(beside)
    kernel = functools.partial(add_kernel, len(parts), len(through))
    outs = call(kernel, [parts[0].shape, *(t.shape for t in through)], operands, specs)
    return outs if through else outs[0]


def sum_steps():
    count = math.prod(lax.axis_size(a) for a in AXES)
    bits = [1 << i for i in range(1, count.bit_length() - 1)]
    assert 1 << (len(bits) + 1) == count and len(bits) > 1
    return [(bits[0], bits[1], bits[0] | bits[1])] + [(bit,) for bit in bits[2:]]


def scatter_kernel(keep_ref, received_ref, tie_ref, mine_ref, *send_refs):
    del tie_ref
    place = lax.axis_index(AXES) // 2 % 4
    for i, ref in enumerate((mine_ref, *send_refs)):
        part = place ^ i
        ref[...] = (keep_ref[pl.ds(part, 1)] + received_ref[pl.ds(part, 1)])[0]


def gather_kernel(mine_ref, *rest):
    out_ref = rest[-1]
    place = lax.axis_index(AXES) // 2 % 4
    for i, ref in enumerate((mine_ref, *rest[:-1])):
        out_ref[pl.ds(place ^ i, 1)] = ref[...][None]


def sum_by_quarters(keep, send, works):
    first, *others = sum_steps()
    others = [bit for (bit,) in others]
    others = [(*pair, sum(pair))[: 2 * len(pair) - 1] for pair in (others[i : i + 2] for i in range(0, len(others), 2))]
    block = keep.shape[1:]
    received = exchange(send, 1)
    tie = works[0](keep)
    mine, *parts = call(scatter_kernel, [block] * 4, (keep, received, tie), [VMEM, VMEM, ANY])
    received = [exchange(part, bit) for part, bit in zip(parts, first, strict=True)]
    handed = works[1](mine)
    mine = add((mine, *received), (handed,))
    for i, bits in enumerate(others):
        received = [exchange(mine, bit) for bit in bits]
        tie = works[2](mine) if i == 0 else ()
        if i < len(others) - 1:
            mine = add((mine, *received), tie)
        else:
            mine, handed = add((mine, *received), tie, (handed,))
    received = [exchange(mine, bit) for bit in first]
    (total,) = call(gather_kernel, [keep.shape], (mine, *received))
    return total, handed


def shifted(array, axis, by, round_off=False):
    length = lax.axis_size(axis)
    pairs = [(i, (i + by) % length) for i in range(length) if round_off or 0 <= i + by < length]
    return lax.ppermute(array, axis, pairs)


def order_halves(mine, other):
    odd = lax.axis_index(AXES) % 2
    return jnp.where(odd == 0, mine, other), jnp.where(odd == 0, other, mine)


def pack_block(block):
    h, q = block.shape[0], block.shape[0] // 2
    e = q // 2
    lane = lax.broadcasted_iota(jnp.int32, (e, h), 1)
    corner = jnp.where(lane < q, pltpu.roll(block[q : q + e], q, 1), block[q + e :])
    return jnp.concatenate([block[:q], corner], axis=0)


def unpack_block(rows):
    h = rows.shape[1]
    q = h // 2
    lane = lax.broadcasted_iota(jnp.int32, (q, h), 1)
    low = jnp.concatenate([pltpu.roll(rows[q:], q, 1), rows[q:]], axis=0)
    square = jnp.concatenate([rows[:q], low], axis=0)
    return jnp.concatenate([rows[:q], jnp.where(lane < q, square.T[q:], low)], axis=0)


def pack(square):
    h = square.shape[0] // 2
    return jnp.concatenate([pack_block(square[:h, :h]), pack_block(square[h:, h:]), square[:h, h:]], axis=0)


def unpack(rows):
    h = rows.shape[1]
    p = 3 * h // 4
    corner = rows[2 * p :]
    upper = jnp.concatenate([unpack_block(rows[:p]), corner], axis=1)
    return jnp.concatenate([upper, jnp.concatenate([corner.T, unpack_block(rows[p : 2 * p])], axis=1)], axis=0)


def gram_kernel(s_ref, keep_ref, send_ref):
    width = s_ref.shape[2]
    flat = s_ref[...].reshape(-1, width)
    gram = dot(flat, flat, 0, 0)
    h, q = width // 2, width // 4
    even = jnp.concatenate([pack_block(gram[h:, h:]), gram[:q, h:]], axis=0)
    odd = jnp.concatenate([pack_block(gram[:h, :h]), gram[q:h, h:]], axis=0)
    keep_ref[...], send_ref[...] = order_halves(even, odd)


def pieces_of(x):
    first = x.astype(jnp.bfloat16)
    rest = x - first.astype(jnp.float32)
    second = rest.astype(jnp.bfloat16)
    third = (rest - second.astype(jnp.float32)).astype(jnp.bfloat16)
    return first, second, third


def picks(node_count, first, second):
    node = lax.broadcasted_iota(jnp.int32, (first.shape[0], node_count), 1).astype(jnp.float32)
    pick = (node == first).astype(jnp.float32) - (node == second).astype(jnp.float32)
    return pick.astype(jnp.bfloat16)


def picked(pick, pieces):
    return sum(jnp.dot(pick, piece, preferred_element_type=jnp.float32) for piece in pieces)


def own_elongation(first, table, s_ref, long_ref):
    nodes = s_ref.shape[1]
    pieces = [pieces_of(s_ref[c]) for c in range(3)]
    for start in range(0, long_ref.shape[0], CHUNK):
        rows = table[first + start : first + start + CHUNK, :]
        pick = picks(nodes, rows[:, 0:1], rows[:, 1:2])
        long_ref[start : start + CHUNK, :] = sum(rows[:, 2 + c : 3 + c] * picked(pick, pieces[c]) for c in range(3))


def first_elongation_kernel(ends_ref, dir_ref, stiff_ref, s_ref, tie_ref, long_ref, table_ref):
    del tie_ref
    ends = ends_ref[...].astype(jnp.float32)
    table_ref[...] = jnp.concatenate([ends, dir_ref[...], stiff_ref[...], jnp.zeros_like(ends)], axis=0).T
    own_elongation(0, table_ref, s_ref, long_ref)


def second_elongation_kernel(table_ref, s_ref, tie_ref, long_ref):
    del tie_ref
    own_elongation(long_ref.shape[0], table_ref, s_ref, long_ref)


def below_elongation_kernel(table_ref, below_ref, first_ref, second_ref, tie_ref, long_ref):
    del tie_ref
    stands = lax.axis_index("span") == 0
    pieces = [pieces_of(jnp.where(stands, 0.0, below_ref[c])) for c in range(3)]
    split = first_ref.shape[0]
    for half, given in enumerate((first_ref, second_ref)):
        for start in range(0, split, CHUNK):
            at = split * half + start
            rows = table_ref[at : at + CHUNK, :]
            pick = picks(SEC_NODES, rows[:, 0:1] - NODES, rows[:, 1:2] - NODES)
            added = sum(rows[:, 2 + c : 3 + c] * picked(pick, pieces[c]) for c in range(3))
            long_ref[at : at + CHUNK, :] = given[start : start + CHUNK, :] + added


def force_kernel(first, count, table_ref, ends_ref, long_ref, tie_ref, *rest):
    del tie_ref
    own_ref, back_ref = rest[-2:]
    nodes = own_ref.shape[1]
    for start in range(first, first + count, CHUNK):
        rows = table_ref[start : start + CHUNK, :]
        axial = long_ref[start : start + CHUNK, :] * rows[:, 5:6]
        ends = ends_ref[:, start : start + CHUNK]
        node = lax.broadcasted_iota(jnp.int32, (nodes + SEC_NODES, CHUNK), 0)
        spread = (node == ends[0:1]).astype(jnp.float32) - (node == ends[1:2]).astype(jnp.float32)
        spread = spread.astype(jnp.bfloat16)
        for c in range(3):
            force = picked(spread, halves(rows[:, 2 + c : 3 + c] * axial))
            if start > first:
                given = own_ref[c], back_ref[c]
            elif len(rest) > 2:
                given = rest[0][c], rest[1][c]
            else:
                given = 0.0, 0.0
            own_ref[c] = given[0] + force[:nodes]
            back_ref[c] = given[1] + force[nodes:]


def factor_block(x_ref, u_ref, m_ref, rows_ref):
    n = x_ref.shape[0]
    count = n // 8
    tiles = [x_ref[8 * i : 8 * i + 8, :] for i in range(count)]
    lane = lax.broadcasted_iota(jnp.int32, (8, n), 1)
    sub = lax.broadcasted_iota(jnp.int32, (8, n), 0)

    def column(tile, c):
        return jnp.broadcast_to(tile[:, c : c + 1], (8, n))

    for p in range(count):
        c0 = 8 * p
        rows_ref[c0 : c0 + 8, :] = tiles[p]
        u = [rows_ref[pl.ds(c0 + r, 8, stride=0), :] for r in range(8)]
        a = [[column(u[r], c0 + c) if c >= r else None for c in range(8)] for r in range(8)]
        panel = (lane >= c0) & (lane < c0 + 8)
        v = [jnp.where(panel, jnp.where(lane == c0 + k, 1.0, 0.0), u[k]) for k in range(8)]
        cols = {t: [column(tiles[t], c0 + k) for k in range(8)] for t in range(p + 1, count)}
        for t in cols:
            tiles[t] = jnp.where(panel, 0.0, tiles[t])
        for k in range(8):
            inverse = pltpu.reciprocal(a[k][k])
            scaled = v[k] * inverse
            for i in range(k + 1, 8):
                f = a[k][i] * inverse
                for j in range(i, 8):
                    a[i][j] = a[i][j] - f * a[k][j]
                v[i] = v[i] - f * v[k]
                u[i] = u[i] - f * u[k]
                for t in cols:
                    cols[t][i] = cols[t][i] - f * cols[t][k]
            for t in cols:
                tiles[t] = tiles[t] - cols[t][k] * scaled
        yt, ut = v[0], u[0]
        for i in range(1, 8):
            yt = jnp.where(sub == i, v[i], yt)
            ut = jnp.where(sub == i, u[i], ut)
        u_ref[c0 : c0 + 8, :] = ut
        m_ref[c0 : c0 + 8, :] = yt


def factored(block, x, u, m, rows):
    h = block.shape[0]
    rowi = lax.broadcasted_iota(jnp.int32, (h, h), 0)
    coli = lax.broadcasted_iota(jnp.int32, (h, h), 1)
    x[...] = block
    factor_block(x, u, m, rows)
    upper = u[...]
    s = lax.rsqrt(jnp.sum(jnp.where(rowi == coli, upper, 0.0), axis=1, keepdims=True))
    return jnp.where(rowi <= coli, upper, 0.0) * s, jnp.where(rowi >= coli, m[...], 0.0) * s


def finish_factor(r11, m1, g12, g22, w_ref, r_ref, scratch):
    h = r11.shape[0]
    r12 = dot(m1, g12)
    r22, m2 = factored(g22 - dot(r12, r12, 0, 0), *scratch)
    zero = jnp.zeros((h, h), jnp.float32)
    r_ref[:h, :h], r_ref[:h, h:], r_ref[h:, :h], r_ref[h:, h:] = r11, r12, zero, r22
    w_ref[:h, :h], w_ref[h:, h:], w_ref[h:, :h] = m1.T, m2.T, zero
    w_ref[:h, h:] = -dot(m1, dot(r12, m2, 1, 1), 0, 0)


def on_diagonal(block):
    shape = block.shape
    eye = lax.broadcasted_iota(jnp.int32, shape, 0) == lax.broadcasted_iota(jnp.int32, shape, 1)
    return jnp.sum(jnp.where(eye, block, 0.0), axis=0, keepdims=True)


def first_block_kernel(sum_ref, message_ref, *scratch):
    odd = lax.axis_index(AXES) % 2 == 1
    h = sum_ref.shape[1]
    p = 3 * h // 4

    @pl.when(odd)
    def _():
        g11 = unpack_block(sum_ref[:p])
        r11, m1 = factored(g11, *scratch)
        rowi = lax.broadcasted_iota(jnp.int32, (h, h), 0)
        coli = lax.broadcasted_iota(jnp.int32, (h, h), 1)
        message_ref[:h] = jnp.where(rowi < coli, r11, m1)
        message_ref[h : h + h // 2] = sum_ref[p:]
        message_ref[h + h // 2 :] = jnp.broadcast_to(on_diagonal(g11), (8, h))

    @pl.when(jnp.logical_not(odd))
    def _():
        message_ref[: sum_ref.shape[0]] = sum_ref[...]
        message_ref[sum_ref.shape[0] :] = jnp.zeros_like(message_ref[sum_ref.shape[0] :])


def second_block_kernel(mine_ref, other_ref, w_ref, r_ref, diag_ref, *scratch):
    h = mine_ref.shape[1]
    p, q = 3 * h // 4, h // 2
    even, odd = order_halves(mine_ref[...], other_ref[...])
    rowi = lax.broadcasted_iota(jnp.int32, (h, h), 0)
    coli = lax.broadcasted_iota(jnp.int32, (h, h), 1)
    m1 = jnp.where(rowi >= coli, odd[:h], 0.0)
    r11 = jnp.where(rowi < coli, odd[:h], jnp.where(rowi == coli, pltpu.reciprocal(odd[:h]), 0.0))
    g12 = jnp.concatenate([even[p : p + q], odd[h : h + q]], axis=0)
    g22 = unpack_block(even[:p])
    diag_ref[:, :h] = odd[h + q : h + q + 1]
    diag_ref[:, h:] = on_diagonal(g22)
    finish_factor(r11, m1, g12, g22, w_ref, r_ref, scratch)


def middle_kernel(s_ref, long_ref, table_ref, w_ref, q_ref, q_halves, long_out, keep_ref, send_ref):
    parts, nodes, width = s_ref.shape
    w = w_ref[...]
    q = dot(s_ref[...].reshape(-1, width), w)
    q_ref[...] = q.reshape(parts, nodes, width)
    long = dot(long_ref[...], w)
    long_out[...] = long
    q = halves(q)
    for i in range(2):
        q_halves[i] = q[i].reshape(parts, nodes, width)
    gram = dot3(q, q, 0, 0)
    energy = dot3(halves(long), halves(long * table_ref[:, 5:6]), 0, 0)
    keep, send = order_halves(pack(energy), pack(gram))
    keep_ref[...] = keep.reshape(keep_ref.shape)
    send_ref[...] = send.reshape(send_ref.shape)


def refine_kernel(rows_all, w_ref, r_ref, diag_ref, tie_ref, out_ref, log_ref):
    del tie_ref
    r = r_ref[...]
    size = r.shape[0]
    eye = lax.broadcasted_iota(jnp.int32, (size, size), 0) == lax.broadcasted_iota(jnp.int32, (size, size), 1)
    log_ref[...] = jnp.log(diag_ref[...] / rows_all)
    out_ref[...] = r + dot(jnp.where(eye, 1.0, 0.0) - dot(r, w_ref[...]), r)


def second_factor_kernel(rows_all, sum_ref, r1_ref, message_ref, *scratch):
    odd = lax.axis_index(AXES) % 2 == 1
    width = message_ref.shape[1]
    h = width // 2
    packed = sum_ref[...].reshape(-1, h)
    half = packed.shape[0] // 2

    @pl.when(odd)
    def _():
        second_factor(rows_all, unpack(packed), r1_ref, message_ref, *scratch)

    @pl.when(jnp.logical_not(odd))
    def _():
        message_ref[:half] = jnp.concatenate([packed[:half], packed[half:]], axis=1)
        message_ref[half:] = jnp.zeros_like(message_ref[half:])


def second_factor(rows_all, gram, r1_ref, message_ref, v_ref, e_ref, w2, r2, *scratch):
    width = gram.shape[0]
    h = width // 2
    rowi = lax.broadcasted_iota(jnp.int32, (width, width), 0)
    coli = lax.broadcasted_iota(jnp.int32, (width, width), 1)
    eye = jnp.where(rowi == coli, 1.0, 0.0)
    start = gram - eye

    def upper_half(e):
        return jnp.where(rowi < coli, e, jnp.where(rowi == coli, 0.5 * e, 0.0))

    e_ref[...] = start
    size = jnp.sum(start * start)

    @pl.when(size < 0.02)
    def _():
        first = upper_half(start)
        low = first.astype(jnp.bfloat16)
        p = jnp.dot(start.astype(jnp.bfloat16), low, preferred_element_type=jnp.float32)
        e = lax.dot_general(
            low, (first + p).astype(jnp.bfloat16), (((0,), (0,)), ((), ())), preferred_element_type=jnp.float32
        )
        upper = upper_half(e - (p + p.T))
        both = jnp.dot(low, upper.astype(jnp.bfloat16), preferred_element_type=jnp.float32)
        v_ref[...] = both - (first + upper)

    @pl.when((size >= 0.02) & (size < 0.06))
    def _():
        v_ref[...] = -upper_half(start)

        def improve(i, carry):
            e = e_ref[...]
            upper = upper_half(e)
            split = halves(upper)
            p = dot3(halves(e), split)
            e = dot3(split, halves(upper + p), 0, 0) - (p + p.T)
            e_ref[...] = e
            upper = upper_half(e)
            v = v_ref[...]
            v_ref[...] = v - (upper + dot3(halves(v), halves(upper)))
            return carry

        lax.fori_loop(0, 2, improve, 0)

    @pl.when(jnp.logical_not(size < 0.06))
    def _():
        r11, m1 = factored(gram[:h, :h], *scratch)
        finish_factor(r11, m1, gram[:h, h:], gram[h:, h:], w2, r2, scratch)
        v_ref[...] = w2[...] - eye

    v = v_ref[...]
    change = jnp.where(rowi <= coli, v.T + start + dot3(halves(v), halves(start), 0, 0), 0.0)
    r1 = r1_ref[...]
    coef = (r1 + dot3(halves(change), halves(r1))) * (1.0 / math.sqrt(rows_all))
    message_ref[:width] = jnp.where(rowi < coli, v, coef.T)
    message_ref[width:] = jnp.broadcast_to(on_diagonal(v), (8, width))


def copied(held, target, sems, blocks):
    copies = []
    for k, block in enumerate(blocks):
        held[k] = block
        copies.append(pltpu.make_async_copy(held.at[k], target.at[k], sems.at[k]))
        copies[-1].start()
    return copies


def basis_kernel(
    rows_all, mine_ref, other_ref, q_ref, q_halves, basis_ref, reduced_ref, coef_ref, v_ref, held, sems
):
    width = v_ref.shape[0]
    h = width // 2
    even, odd = order_halves(mine_ref[...], other_ref[...])
    rowi = lax.broadcasted_iota(jnp.int32, (width, width), 0)
    coli = lax.broadcasted_iota(jnp.int32, (width, width), 1)
    diag = jnp.where(rowi == coli, odd[width : width + 1], 0.0)
    v = jnp.where(rowi < coli, odd[:width], diag)
    v_ref[...] = v
    v = halves(v)
    root = math.sqrt(rows_all)
    blocks = ((q_ref[c] + dot3((q_halves[0, c], q_halves[1, c]), v)) * root for c in range(q_ref.shape[0]))
    copies = copied(held, basis_ref, sems, blocks)
    coef_ref[...] = jnp.where(rowi <= coli, odd[:width].T, 0.0)
    half = 5 * h // 4
    energy = unpack(jnp.concatenate([even[:half, :h], even[:half, h:]], axis=0))
    right = energy + dot3(halves(energy), v)
    reduced_ref[...] = right + dot3(v, halves(right), 0, 0)
    for copy in copies:
        copy.wait()


def forces_kernel(rows_all, own_ref, back_ref, v_ref, forces_ref, held, sems):
    parts, nodes, _ = own_ref.shape
    top = lax.axis_index("span") == lax.axis_size("span") - 1
    v = halves(v_ref[...])

    def block(c):
        returned = jnp.where(top, 0.0, back_ref[c])
        low, high = own_ref[c, : nodes - SEC_NODES], own_ref[c, nodes - SEC_NODES :]
        forces = jnp.concatenate([low, high + returned], axis=0)
        return (forces + dot3(halves(forces), v)) * math.sqrt(rows_all)

    copies = copied(held, forces_ref, sems, (block(c) for c in range(parts)))
    for copy in copies:
        copy.wait()


def local(snapshots, member_ends, member_dir, member_stiff):
    parts, nodes, width = snapshots.shape
    h = width // 2
    count = math.prod(lax.axis_size(a) for a in AXES)
    rows_all = parts * nodes * count
    steps = sum_steps()
    square = (width, width)
    field = (parts, nodes, width)
    level = (parts, SEC_NODES, width)
    packed = (5 * width // 8, h)
    scratch = [pltpu.VMEM((h, h), jnp.float32)] * 4

    below = shifted(snapshots[:, nodes - SEC_NODES :, :], "span", 1, True)
    keep, send = call(gram_kernel, [packed, packed], (snapshots,))
    members = member_dir.shape[1]
    split = members // 2
    total = add((keep, exchange(send, 1)))
    for i, bits in enumerate(steps):
        received = [exchange(total, bit) for bit in bits]
        if i == 0:
            first, table = call(
                first_elongation_kernel,
                [(split, width), (members, 8)],
                (member_ends, member_dir, member_stiff[None], snapshots, total),
                [VMEM] * 4 + [ANY],
            )
            second = call(second_elongation_kernel, [(split, width)], (table, snapshots, total), [VMEM, VMEM, ANY])
            long = [first, *second]
            total = add((total, *received), long)
        elif i < len(steps) - 1:
            total = add((total, *received))
        else:
            operands = (table, below, *long, total)
            (stretch,) = call(below_elongation_kernel, [(members, width)], operands, [VMEM] * 4 + [ANY])
            total = add((total, *received), (stretch,))
    (message,) = call(first_block_kernel, [(h + h // 2 + 8, h)], (total,), scratch=scratch)
    w1, r1, diag = call(
        second_block_kernel, [square, square, (1, width)], (message, exchange(message, 1)), scratch=scratch
    )

    quarters = (4, 5 * width // 16, h)
    q, q_halves, stretch, keep, send = call(
        middle_kernel,
        [field, jax.ShapeDtypeStruct((2, *field), jnp.bfloat16), (members, width), quarters, quarters],
        (snapshots, stretch, table, w1),
    )
    held = []

    def members_forces(tie):
        operands = (table, member_ends, stretch, tie, *held)
        first = split if held else 0
        kernel = functools.partial(force_kernel, first, split)
        held[:] = call(kernel, [field, level], operands, [VMEM] * 3 + [ANY] + [VMEM] * len(held))
        return held[1]

    def refined(tie):
        refine = functools.partial(refine_kernel, rows_all)
        r1_and_log.extend(call(refine, [square, (1, width)], (w1, r1, diag, tie), [VMEM] * 3 + [ANY]))
        return r1_and_log[:1]

    r1_and_log = []
    total, back = sum_by_quarters(keep, send, [members_forces, members_forces, refined])
    own = held[0]
    returned = shifted(back, "span", -1)
    r1, column_energy = r1_and_log

    (message,) = call(
        functools.partial(second_factor_kernel, rows_all),
        [(width + 8, width)],
        (total, r1),
        scratch=[pltpu.VMEM(square, jnp.float32)] * 4 + scratch,
    )
    staged = [pltpu.VMEM(field, jnp.float32), pltpu.SemaphoreType.DMA((parts,))]
    basis, reduced, coef, v = call(
        functools.partial(basis_kernel, rows_all),
        [field, square, square, square],
        (message, exchange(message, 1), q, q_halves),
        scratch=staged,
        outs=(HBM, VMEM, VMEM, VMEM),
    )
    (forces,) = call(
        functools.partial(forces_kernel, rows_all), [field], (own, returned, v), scratch=staged, outs=(HBM,)
    )
    return (basis, forces, reduced, coef, column_energy[0])


def solution(mesh):
    placed = (
        P(None, AXES, None),
        P(None, AXES),
        P(None, AXES),
        P(AXES),
    )
    return jax.shard_map(
        local,
        mesh=mesh,
        in_specs=placed,
        out_specs=(P(None, AXES, None), P(None, AXES, None), P(), P(), P()),
        check_vma=False,
    )
```

```python
import functools
import math

import jax
import jax.numpy as jnp
from jax import lax
from jax.experimental import pallas as pl
from jax.experimental.pallas import tpu as pltpu
from jax.sharding import PartitionSpec as P

AXES = ("span", "xsec", "leaf")
SEC_NODES = 128
NODES = 256
CHUNK = 256
highest = lax.Precision.HIGHEST
VMEM = pl.BlockSpec(memory_space=pltpu.VMEM)
ANY = pl.BlockSpec(memory_space=pl.ANY)
HBM = pl.BlockSpec(memory_space=pltpu.HBM)


def dot(a, b, ca=1, cb=0):
    return lax.dot_general(
        a, b, (((ca,), (cb,)), ((), ())), precision=highest, preferred_element_type=jnp.float32
    )


def halves(x):
    high = x.astype(jnp.bfloat16)
    return high, (x - high.astype(jnp.float32)).astype(jnp.bfloat16)


def dot3(a, b, ca=1, cb=0):
    def one(x, y):
        return lax.dot_general(x, y, (((ca,), (cb,)), ((), ())), preferred_element_type=jnp.float32)

    return one(a[0], b[0]) + (one(a[0], b[1]) + one(a[1], b[0]))


def call(kernel, shapes, operands, specs=None, scratch=(), outs=None, us=0.1):
    return pl.pallas_call(
        kernel,
        out_shape=tuple(s if isinstance(s, jax.ShapeDtypeStruct) else jax.ShapeDtypeStruct(s, jnp.float32) for s in shapes),
        in_specs=specs or [VMEM] * len(operands),
        out_specs=outs or tuple(VMEM for _ in shapes),
        scratch_shapes=list(scratch),
        compiler_params=pltpu.CompilerParams(vmem_limit_bytes=48 << 20),
        cost_estimate=pl.CostEstimate(flops=0, bytes_accessed=int(us * 3.69e6), transcendentals=0),
    )(*operands)


def exchange(array, bit):
    count = math.prod(lax.axis_size(a) for a in AXES)
    return lax.ppermute(array, AXES, [(i, i ^ bit) for i in range(count)])


def add_kernel(terms, handed, *refs):
    outs = refs[len(refs) - 1 - handed :]
    parts = [ref[...] for ref in refs[:terms]]
    while len(parts) > 1:
        parts = [sum(parts[i : i + 2]) for i in range(0, len(parts), 2)]
    outs[0][...] = parts[0]
    for given, out in zip(refs[terms : terms + handed], outs[1:], strict=True):
        out[...] = given[...]


def add(parts, beside=(), through=()):
    operands = (*parts, *through, *beside)
    specs = [VMEM] * (len(parts) + len(through)) + [ANY] * len(beside)
    kernel = functools.partial(add_kernel, len(parts), len(through))
    outs = call(kernel, [parts[0].shape, *(t.shape for t in through)], operands, specs)
    return outs if through else outs[0]


def sum_steps():
    count = math.prod(lax.axis_size(a) for a in AXES)
    bits = [1 << i for i in range(1, count.bit_length() - 1)]
    assert 1 << (len(bits) + 1) == count and len(bits) > 1
    return [(bits[0], bits[1], bits[0] | bits[1])] + [(bit,) for bit in bits[2:]]


def scatter_kernel(keep_ref, received_ref, tie_ref, mine_ref, *send_refs):
    del tie_ref
    place = lax.axis_index(AXES) // 2 % 4
    for i, ref in enumerate((mine_ref, *send_refs)):
        part = place ^ i
        ref[...] = (keep_ref[pl.ds(part, 1)] + received_ref[pl.ds(part, 1)])[0]


def gather_kernel(mine_ref, *rest):
    out_ref = rest[-1]
    place = lax.axis_index(AXES) // 2 % 4
    for i, ref in enumerate((mine_ref, *rest[:-2])):
        out_ref[pl.ds(place ^ i, 1)] = ref[...][None]


def sum_by_quarters(keep, send, works):
    first, *others = sum_steps()
    others = [bit for (bit,) in others]
    others = [(*pair, sum(pair))[: 2 * len(pair) - 1] for pair in (others[i : i + 2] for i in range(0, len(others), 2))]
    block = keep.shape[1:]
    operands = (keep, exchange(send, 1), works[0](keep))
    mine, *parts = call(scatter_kernel, [block] * 4, operands, [VMEM, VMEM, ANY])
    received = [exchange(part, bit) for part, bit in zip(parts, first, strict=True)]
    mine = add((mine, *received), works[1](mine))
    for i, bits in enumerate(others):
        received = [exchange(mine, bit) for bit in bits]
        mine = add((mine, *received), works[2](mine) if i == len(others) - 1 else ())
    received = [exchange(mine, bit) for bit in first]
    operands = (mine, *received, works[3](mine))
    (total,) = call(gather_kernel, [keep.shape], operands, [VMEM] * 4 + [ANY])
    return total


def shifted(array, axis, by, round_off=False):
    length = lax.axis_size(axis)
    pairs = [(i, (i + by) % length) for i in range(length) if round_off or 0 <= i + by < length]
    return lax.ppermute(array, axis, pairs)


def order_halves(mine, other):
    odd = lax.axis_index(AXES) % 2
    return jnp.where(odd == 0, mine, other), jnp.where(odd == 0, other, mine)


def pack_block(block):
    h, q = block.shape[0], block.shape[0] // 2
    e = q // 2
    lane = lax.broadcasted_iota(jnp.int32, (e, h), 1)
    corner = jnp.where(lane < q, pltpu.roll(block[q : q + e], q, 1), block[q + e :])
    return jnp.concatenate([block[:q], corner], axis=0)


def unpack_block(rows):
    h = rows.shape[1]
    q = h // 2
    lane = lax.broadcasted_iota(jnp.int32, (q, h), 1)
    low = jnp.concatenate([pltpu.roll(rows[q:], q, 1), rows[q:]], axis=0)
    square = jnp.concatenate([rows[:q], low], axis=0)
    return jnp.concatenate([rows[:q], jnp.where(lane < q, square.T[q:], low)], axis=0)


def pack(square):
    h = square.shape[0] // 2
    return jnp.concatenate([pack_block(square[:h, :h]), pack_block(square[h:, h:]), square[:h, h:]], axis=0)


def unpack(rows):
    h = rows.shape[1]
    p = 3 * h // 4
    corner = rows[2 * p :]
    upper = jnp.concatenate([unpack_block(rows[:p]), corner], axis=1)
    return jnp.concatenate([upper, jnp.concatenate([corner.T, unpack_block(rows[p : 2 * p])], axis=1)], axis=0)


def gram_kernel(s_ref, keep_ref, send_ref):
    width = s_ref.shape[2]
    flat = s_ref[...].reshape(-1, width)
    gram = dot(flat, flat, 0, 0)
    h, q = width // 2, width // 4
    even = jnp.concatenate([pack_block(gram[h:, h:]), gram[:q, h:]], axis=0)
    odd = jnp.concatenate([pack_block(gram[:h, :h]), gram[q:h, h:]], axis=0)
    keep_ref[...], send_ref[...] = order_halves(even, odd)


def pieces_of(x):
    first = x.astype(jnp.bfloat16)
    rest = x - first.astype(jnp.float32)
    second = rest.astype(jnp.bfloat16)
    third = (rest - second.astype(jnp.float32)).astype(jnp.bfloat16)
    return first, second, third


def picks(node_count, first, second):
    node = lax.broadcasted_iota(jnp.int32, (first.shape[0], node_count), 1).astype(jnp.float32)
    pick = (node == first).astype(jnp.float32) - (node == second).astype(jnp.float32)
    return pick.astype(jnp.bfloat16)


def picked(pick, pieces):
    return sum(jnp.dot(pick, piece, preferred_element_type=jnp.float32) for piece in pieces)


def own_elongation(first, table, s_ref, long_ref):
    nodes = s_ref.shape[1]
    pieces = [pieces_of(s_ref[c]) for c in range(3)]
    for start in range(0, long_ref.shape[0], CHUNK):
        rows = table[first + start : first + start + CHUNK, :]
        pick = picks(nodes, rows[:, 0:1], rows[:, 1:2])
        long_ref[start : start + CHUNK, :] = sum(rows[:, 2 + c : 3 + c] * picked(pick, pieces[c]) for c in range(3))


def first_elongation_kernel(ends_ref, dir_ref, stiff_ref, s_ref, tie_ref, long_ref, table_ref):
    del tie_ref
    ends = ends_ref[...].astype(jnp.float32)
    table_ref[...] = jnp.concatenate([ends, dir_ref[...], stiff_ref[...], jnp.zeros_like(ends)], axis=0).T
    own_elongation(0, table_ref, s_ref, long_ref)


def second_elongation_kernel(table_ref, s_ref, tie_ref, long_ref):
    del tie_ref
    own_elongation(long_ref.shape[0], table_ref, s_ref, long_ref)


def below_elongation_kernel(table_ref, below_ref, first_ref, second_ref, tie_ref, long_ref):
    del tie_ref
    stands = lax.axis_index("span") == 0
    pieces = [pieces_of(jnp.where(stands, 0.0, below_ref[c])) for c in range(3)]
    split = first_ref.shape[0]
    for half, given in enumerate((first_ref, second_ref)):
        for start in range(0, split, CHUNK):
            at = split * half + start
            rows = table_ref[at : at + CHUNK, :]
            pick = picks(SEC_NODES, rows[:, 0:1] - NODES, rows[:, 1:2] - NODES)
            added = sum(rows[:, 2 + c : 3 + c] * picked(pick, pieces[c]) for c in range(3))
            long_ref[at : at + CHUNK, :] = given[start : start + CHUNK, :] + added


def force_kernel(table_ref, ends_ref, long_ref, top_ref, tie_ref, own_ref):
    del tie_ref
    nodes = own_ref.shape[1]
    members = long_ref.shape[0]
    axial = long_ref[...] * table_ref[:, 5:6]
    node = lax.broadcasted_iota(jnp.int32, (nodes, members), 0)
    ends = ends_ref[...]
    spread = (node == ends[0:1]).astype(jnp.float32) - (node == ends[1:2]).astype(jnp.float32)
    spread = spread.astype(jnp.bfloat16)
    for c in range(3):
        force = picked(spread, halves(table_ref[:, 2 + c : 3 + c] * axial))
        own_ref[c, : nodes - SEC_NODES] = force[: nodes - SEC_NODES]
        own_ref[c, nodes - SEC_NODES :] = force[nodes - SEC_NODES :] - top_ref[c]


def downward_kernel(s_ref, ends_ref, dir_ref, stiff_ref, tie_ref, out_ref):
    del tie_ref
    width = out_ref.shape[1]
    rows = 3 * SEC_NODES
    out_ref[:rows] = s_ref[:, :SEC_NODES].reshape(rows, width)
    table = jnp.concatenate([ends_ref[...].astype(jnp.float32), dir_ref[...], stiff_ref[...]], axis=0)
    out_ref[rows:] = jnp.concatenate([table[:, at : at + width] for at in range(0, table.shape[1], width)], axis=0)


def above_elongation_kernel(above_ref, s_ref, tie_ref, long_ref, table_ref, seconds_ref):
    del tie_ref
    nodes, width = s_ref.shape[1:]
    rows = 3 * SEC_NODES
    held = above_ref[rows:]
    table = jnp.concatenate([held[at : at + 6] for at in range(0, held.shape[0], 6)], axis=1)
    table = jnp.concatenate([table, jnp.zeros_like(table[:2])], axis=0)
    seconds_ref[...] = table
    table_ref[...] = table.T
    top = lax.axis_index("span") == lax.axis_size("span") - 1
    pieces = []
    for c in range(3):
        both = jnp.concatenate([above_ref[SEC_NODES * c : SEC_NODES * (c + 1)], s_ref[c, nodes - SEC_NODES :]], axis=0)
        pieces.append(pieces_of(jnp.where(top, 0.0, both)))
    for start in range(0, long_ref.shape[0], CHUNK):
        members = table_ref[start : start + CHUNK, :]
        second = members[:, 1:2] - nodes
        first = jnp.where(second >= 0.0, members[:, 0:1], -1.0)
        pick = picks(2 * SEC_NODES, first, second + jnp.where(second >= 0.0, 1.0 * SEC_NODES, -1.0 * nodes))
        long_ref[start : start + CHUNK, :] = sum(members[:, 2 + c : 3 + c] * picked(pick, pieces[c]) for c in range(3))


def above_force_kernel(nodes, table_ref, seconds_ref, long_ref, w_ref, tie_ref, top_ref):
    del tie_ref
    axial = dot(long_ref[...], w_ref[...]) * table_ref[:, 5:6]
    node = lax.broadcasted_iota(jnp.int32, (SEC_NODES, long_ref.shape[0]), 0).astype(jnp.float32)
    spread = (node == seconds_ref[1:2] - nodes).astype(jnp.float32).astype(jnp.bfloat16)
    for c in range(3):
        top_ref[c] = picked(spread, halves(table_ref[:, 2 + c : 3 + c] * axial))


def factor_block(x_ref, u_ref, m_ref, rows_ref):
    n = x_ref.shape[0]
    count = n // 8
    tiles = [x_ref[8 * i : 8 * i + 8, :] for i in range(count)]
    lane = lax.broadcasted_iota(jnp.int32, (8, n), 1)
    sub = lax.broadcasted_iota(jnp.int32, (8, n), 0)

    def column(tile, c):
        return jnp.broadcast_to(tile[:, c : c + 1], (8, n))

    for p in range(count):
        c0 = 8 * p
        rows_ref[c0 : c0 + 8, :] = tiles[p]
        u = [rows_ref[pl.ds(c0 + r, 8, stride=0), :] for r in range(8)]
        a = [[column(u[r], c0 + c) if c >= r else None for c in range(8)] for r in range(8)]
        panel = (lane >= c0) & (lane < c0 + 8)
        v = [jnp.where(panel, jnp.where(lane == c0 + k, 1.0, 0.0), u[k]) for k in range(8)]
        cols = {t: [column(tiles[t], c0 + k) for k in range(8)] for t in range(p + 1, count)}
        for t in cols:
            tiles[t] = jnp.where(panel, 0.0, tiles[t])
        for k in range(8):
            inverse = pltpu.reciprocal(a[k][k])
            scaled = v[k] * inverse
            for i in range(k + 1, 8):
                f = a[k][i] * inverse
                for j in range(i, 8):
                    a[i][j] = a[i][j] - f * a[k][j]
                v[i] = v[i] - f * v[k]
                u[i] = u[i] - f * u[k]
                for t in cols:
                    cols[t][i] = cols[t][i] - f * cols[t][k]
            for t in cols:
                tiles[t] = tiles[t] - cols[t][k] * scaled
        yt, ut = v[0], u[0]
        for i in range(1, 8):
            yt = jnp.where(sub == i, v[i], yt)
            ut = jnp.where(sub == i, u[i], ut)
        u_ref[c0 : c0 + 8, :] = ut
        m_ref[c0 : c0 + 8, :] = yt


def factored(block, x, u, m, rows):
    h = block.shape[0]
    rowi = lax.broadcasted_iota(jnp.int32, (h, h), 0)
    coli = lax.broadcasted_iota(jnp.int32, (h, h), 1)
    x[...] = block
    factor_block(x, u, m, rows)
    upper = u[...]
    s = lax.rsqrt(jnp.sum(jnp.where(rowi == coli, upper, 0.0), axis=1, keepdims=True))
    return jnp.where(rowi <= coli, upper, 0.0) * s, jnp.where(rowi >= coli, m[...], 0.0) * s


def finish_factor(r11, m1, g12, g22, w_ref, r_ref, scratch):
    h = r11.shape[0]
    r12 = dot(m1, g12)
    r22, m2 = factored(g22 - dot(r12, r12, 0, 0), *scratch)
    zero = jnp.zeros((h, h), jnp.float32)
    r_ref[:h, :h], r_ref[:h, h:], r_ref[h:, :h], r_ref[h:, h:] = r11, r12, zero, r22
    w_ref[:h, :h], w_ref[h:, h:], w_ref[h:, :h] = m1.T, m2.T, zero
    w_ref[:h, h:] = -dot(m1, dot(r12, m2, 1, 1), 0, 0)


def on_diagonal(block):
    shape = block.shape
    eye = lax.broadcasted_iota(jnp.int32, shape, 0) == lax.broadcasted_iota(jnp.int32, shape, 1)
    return jnp.sum(jnp.where(eye, block, 0.0), axis=0, keepdims=True)


def first_block_kernel(sum_ref, message_ref, *scratch):
    odd = lax.axis_index(AXES) % 2 == 1
    h = sum_ref.shape[1]
    p = 3 * h // 4

    @pl.when(odd)
    def _():
        g11 = unpack_block(sum_ref[:p])
        r11, m1 = factored(g11, *scratch)
        rowi = lax.broadcasted_iota(jnp.int32, (h, h), 0)
        coli = lax.broadcasted_iota(jnp.int32, (h, h), 1)
        message_ref[:h] = jnp.where(rowi < coli, r11, m1)
        message_ref[h : h + h // 2] = sum_ref[p:]
        message_ref[h + h // 2 :] = jnp.broadcast_to(on_diagonal(g11), (8, h))

    @pl.when(jnp.logical_not(odd))
    def _():
        message_ref[: sum_ref.shape[0]] = sum_ref[...]
        message_ref[sum_ref.shape[0] :] = jnp.zeros_like(message_ref[sum_ref.shape[0] :])


def second_block_kernel(mine_ref, other_ref, w_ref, r_ref, diag_ref, *scratch):
    h = mine_ref.shape[1]
    p, q = 3 * h // 4, h // 2
    even, odd = order_halves(mine_ref[...], other_ref[...])
    rowi = lax.broadcasted_iota(jnp.int32, (h, h), 0)
    coli = lax.broadcasted_iota(jnp.int32, (h, h), 1)
    m1 = jnp.where(rowi >= coli, odd[:h], 0.0)
    r11 = jnp.where(rowi < coli, odd[:h], jnp.where(rowi == coli, pltpu.reciprocal(odd[:h]), 0.0))
    g12 = jnp.concatenate([even[p : p + q], odd[h : h + q]], axis=0)
    g22 = unpack_block(even[:p])
    diag_ref[:, :h] = odd[h + q : h + q + 1]
    diag_ref[:, h:] = on_diagonal(g22)
    finish_factor(r11, m1, g12, g22, w_ref, r_ref, scratch)


def middle_kernel(s_ref, long_ref, table_ref, w_ref, q_ref, q_halves, long_out, keep_ref, send_ref):
    parts, nodes, width = s_ref.shape
    w = w_ref[...]
    q = dot(s_ref[...].reshape(-1, width), w)
    q_ref[...] = q.reshape(parts, nodes, width)
    long = dot(long_ref[...], w)
    long_out[...] = long
    q = halves(q)
    for i in range(2):
        q_halves[i] = q[i].reshape(parts, nodes, width)
    gram = dot3(q, q, 0, 0)
    energy = dot3(halves(long), halves(long * table_ref[:, 5:6]), 0, 0)
    keep, send = order_halves(pack(energy), pack(gram))
    keep_ref[...] = keep.reshape(keep_ref.shape)
    send_ref[...] = send.reshape(send_ref.shape)


def refine_kernel(rows_all, w_ref, r_ref, diag_ref, tie_ref, out_ref, log_ref):
    del tie_ref
    r = r_ref[...]
    size = r.shape[0]
    eye = lax.broadcasted_iota(jnp.int32, (size, size), 0) == lax.broadcasted_iota(jnp.int32, (size, size), 1)
    log_ref[...] = jnp.log(diag_ref[...] / rows_all)
    out_ref[...] = r + dot(jnp.where(eye, 1.0, 0.0) - dot(r, w_ref[...]), r)


def second_factor_kernel(rows_all, sum_ref, r1_ref, message_ref, *scratch):
    odd = lax.axis_index(AXES) % 2 == 1
    width = message_ref.shape[1]
    h = width // 2
    packed = sum_ref[...].reshape(-1, h)
    half = packed.shape[0] // 2

    @pl.when(odd)
    def _():
        second_factor(rows_all, unpack(packed), r1_ref, message_ref, *scratch)

    @pl.when(jnp.logical_not(odd))
    def _():
        message_ref[:half] = jnp.concatenate([packed[:half], packed[half:]], axis=1)
        message_ref[half:] = jnp.zeros_like(message_ref[half:])


def second_factor(rows_all, gram, r1_ref, message_ref, v_ref, e_ref, w2, r2, *scratch):
    width = gram.shape[0]
    h = width // 2
    rowi = lax.broadcasted_iota(jnp.int32, (width, width), 0)
    coli = lax.broadcasted_iota(jnp.int32, (width, width), 1)
    eye = jnp.where(rowi == coli, 1.0, 0.0)
    start = gram - eye

    def upper_half(e):
        return jnp.where(rowi < coli, e, jnp.where(rowi == coli, 0.5 * e, 0.0))

    e_ref[...] = start
    size = jnp.sum(start * start)

    @pl.when(size < 0.02)
    def _():
        first = upper_half(start)
        low = first.astype(jnp.bfloat16)
        p = jnp.dot(start.astype(jnp.bfloat16), low, preferred_element_type=jnp.float32)
        e = lax.dot_general(
            low, (first + p).astype(jnp.bfloat16), (((0,), (0,)), ((), ())), preferred_element_type=jnp.float32
        )
        upper = upper_half(e - (p + p.T))
        both = jnp.dot(low, upper.astype(jnp.bfloat16), preferred_element_type=jnp.float32)
        v_ref[...] = both - (first + upper)

    @pl.when((size >= 0.02) & (size < 0.06))
    def _():
        v_ref[...] = -upper_half(start)

        def improve(i, carry):
            e = e_ref[...]
            upper = upper_half(e)
            split = halves(upper)
            p = dot3(halves(e), split)
            e = dot3(split, halves(upper + p), 0, 0) - (p + p.T)
            e_ref[...] = e
            upper = upper_half(e)
            v = v_ref[...]
            v_ref[...] = v - (upper + dot3(halves(v), halves(upper)))
            return carry

        lax.fori_loop(0, 2, improve, 0)

    @pl.when(jnp.logical_not(size < 0.06))
    def _():
        r11, m1 = factored(gram[:h, :h], *scratch)
        finish_factor(r11, m1, gram[:h, h:], gram[h:, h:], w2, r2, scratch)
        v_ref[...] = w2[...] - eye

    v = v_ref[...]
    change = jnp.where(rowi <= coli, v.T + start + dot3(halves(v), halves(start), 0, 0), 0.0)
    r1 = r1_ref[...]
    coef = (r1 + dot3(halves(change), halves(r1))) * (1.0 / math.sqrt(rows_all))
    message_ref[:width] = jnp.where(rowi < coli, v, coef.T)
    message_ref[width:] = jnp.broadcast_to(on_diagonal(v), (8, width))


def final_kernel(
    rows_all, mine_ref, other_ref, q_ref, q_halves, own_ref,
    basis_ref, forces_ref, reduced_ref, coef_ref, held, sems,
):
    parts, nodes, width = q_ref.shape
    h = width // 2
    even, odd = order_halves(mine_ref[...], other_ref[...])
    rowi = lax.broadcasted_iota(jnp.int32, (width, width), 0)
    coli = lax.broadcasted_iota(jnp.int32, (width, width), 1)
    diag = jnp.where(rowi == coli, odd[width : width + 1], 0.0)
    v = halves(jnp.where(rowi < coli, odd[:width], diag))
    root = math.sqrt(rows_all)
    copies = []
    for k in range(2 * parts):
        c = k % parts
        if k < parts:
            source, split, target = q_ref[c], (q_halves[0, c], q_halves[1, c]), basis_ref
        else:
            source, target = own_ref[c], forces_ref
            split = halves(source)
        held[k] = (source + dot3(split, v)) * root
        copies.append(pltpu.make_async_copy(held.at[k], target.at[c], sems.at[k]))
        copies[-1].start()
    coef_ref[...] = jnp.where(rowi <= coli, odd[:width].T, 0.0)
    half = 5 * h // 4
    energy = unpack(jnp.concatenate([even[:half, :h], even[:half, h:]], axis=0))
    right = energy + dot3(halves(energy), v)
    reduced_ref[...] = right + dot3(v, halves(right), 0, 0)
    for copy in copies:
        copy.wait()


def local(snapshots, member_ends, member_dir, member_stiff):
    parts, nodes, width = snapshots.shape
    h = width // 2
    count = math.prod(lax.axis_size(a) for a in AXES)
    rows_all = parts * nodes * count
    steps = sum_steps()
    square = (width, width)
    field = (parts, nodes, width)
    packed = (5 * width // 8, h)
    scratch = [pltpu.VMEM((h, h), jnp.float32)] * 3 + [pltpu.VMEM((h + 8, h), jnp.float32)]

    below = shifted(snapshots[:, nodes - SEC_NODES :, :], "span", 1, True)
    keep, send = call(gram_kernel, [packed, packed], (snapshots,))
    members = member_dir.shape[1]
    split = members // 2
    total = add((keep, exchange(send, 1)))
    for i, bits in enumerate(steps):
        received = [exchange(total, bit) for bit in bits]
        if i == 0:
            first, table = call(
                first_elongation_kernel,
                [(split, width), (members, 8)],
                (member_ends, member_dir, member_stiff[None], snapshots, total),
                [VMEM] * 4 + [ANY],
            )
            second = call(second_elongation_kernel, [(split, width)], (table, snapshots, total), [VMEM, VMEM, ANY])
            long = [first, *second]
            total = add((total, *received), long)
        elif i < len(steps) - 1:
            total = add((total, *received))
        else:
            operands = (table, below, *long, total)
            (stretch,) = call(below_elongation_kernel, [(members, width)], operands, [VMEM] * 4 + [ANY])
            (downward,) = call(
                downward_kernel,
                [(3 * SEC_NODES + 6 * members // width, width)],
                (snapshots, member_ends, member_dir, member_stiff[None], total),
                [VMEM] * 4 + [ANY],
            )
            total, downward = add((total, *received), (stretch,), (downward,))
    above = shifted(downward, "span", -1, True)
    (message,) = call(first_block_kernel, [(h + h // 2 + 8, h)], (total,), scratch=scratch, us=2)
    w1, r1, diag = call(
        second_block_kernel, [square, square, (1, width)], (message, exchange(message, 1)), scratch=scratch, us=5
    )

    quarters = (4, 5 * width // 16, h)
    q, q_halves, stretch, keep, send = call(
        middle_kernel,
        [field, jax.ShapeDtypeStruct((2, *field), jnp.bfloat16), (members, width), quarters, quarters],
        (snapshots, stretch, table, w1),
        us=3,
    )
    def refined(tie):
        refine = functools.partial(refine_kernel, rows_all)
        made["r1"] = call(refine, [square, (1, width)], (w1, r1, diag, tie), [VMEM] * 3 + [ANY], us=1)
        return made["r1"][0]

    def above_elongation(tie):
        shapes = [(members, width), (members, 8), (8, members)]
        made["above"] = call(above_elongation_kernel, shapes, (above, snapshots, tie), [VMEM] * 2 + [ANY], us=2)
        return made["above"][:1]

    def above_forces(tie):
        stretch_above, table_above, seconds = made["above"]
        operands = (table_above, seconds, stretch_above, w1, tie)
        kernel = functools.partial(above_force_kernel, nodes)
        made["top"] = call(kernel, [(parts, SEC_NODES, width)], operands, [VMEM] * 4 + [ANY], us=2.5)
        return made["top"]

    def own_forces(tie):
        operands = (table, member_ends, stretch, made["top"][0], tie)
        (made["own"],) = call(force_kernel, [field], operands, [VMEM] * 4 + [ANY], us=1.5)
        return made["own"]

    made = {}
    total = sum_by_quarters(keep, send, [refined, above_elongation, above_forces, own_forces])
    r1, column_energy = made["r1"]

    (message,) = call(
        functools.partial(second_factor_kernel, rows_all),
        [(width + 8, width)],
        (total, r1),
        scratch=[pltpu.VMEM(square, jnp.float32)] * 4 + scratch,
    )
    basis, forces, reduced, coef = call(
        functools.partial(final_kernel, rows_all),
        [field, field, square, square],
        (message, exchange(message, 1), q, q_halves, made["own"]),
        scratch=[pltpu.VMEM((2 * parts, nodes, width), jnp.float32), pltpu.SemaphoreType.DMA((2 * parts,))],
        outs=(HBM, HBM, VMEM, VMEM),
    )
    return (basis, forces, reduced, coef, column_energy[0])


def solution(mesh):
    placed = (
        P(None, AXES, None),
        P(None, AXES),
        P(None, AXES),
        P(AXES),
    )
    return jax.shard_map(
        local,
        mesh=mesh,
        in_specs=placed,
        out_specs=(P(None, AXES, None), P(None, AXES, None), P(), P(), P()),
        check_vma=False,
    )
```

```python
import functools
import math

import jax
import jax.numpy as jnp
from jax import lax
from jax.experimental import pallas as pl
from jax.experimental.pallas import tpu as pltpu
from jax.sharding import PartitionSpec as P

AXES = ("span", "xsec", "leaf")
SEC_NODES = 128
NODES = 256
CHUNK = 256
highest = lax.Precision.HIGHEST
VMEM = pl.BlockSpec(memory_space=pltpu.VMEM)
ANY = pl.BlockSpec(memory_space=pl.ANY)
HBM = pl.BlockSpec(memory_space=pltpu.HBM)


def dot(a, b, ca=1, cb=0):
    return lax.dot_general(
        a, b, (((ca,), (cb,)), ((), ())), precision=highest, preferred_element_type=jnp.float32
    )


def halves(x):
    high = x.astype(jnp.bfloat16)
    return high, (x - high.astype(jnp.float32)).astype(jnp.bfloat16)


def dot3(a, b, ca=1, cb=0):
    def one(x, y):
        return lax.dot_general(x, y, (((ca,), (cb,)), ((), ())), preferred_element_type=jnp.float32)

    return one(a[0], b[0]) + (one(a[0], b[1]) + one(a[1], b[0]))


def pieces_of(x):
    first = x.astype(jnp.bfloat16)
    rest = x - first.astype(jnp.float32)
    second = rest.astype(jnp.bfloat16)
    third = (rest - second.astype(jnp.float32)).astype(jnp.bfloat16)
    return first, second, third


def dot6(a, b, ca=1, cb=0):
    def one(i, j):
        return lax.dot_general(a[i], b[j], (((ca,), (cb,)), ((), ())), preferred_element_type=jnp.float32)

    return one(0, 0) + ((one(0, 1) + one(1, 0)) + ((one(0, 2) + one(2, 0)) + one(1, 1)))


def call(kernel, shapes, operands, specs=None, scratch=(), outs=None, us=0.1):
    return pl.pallas_call(
        kernel,
        out_shape=tuple(s if isinstance(s, jax.ShapeDtypeStruct) else jax.ShapeDtypeStruct(s, jnp.float32) for s in shapes),
        in_specs=specs or [VMEM] * len(operands),
        out_specs=outs or tuple(VMEM for _ in shapes),
        scratch_shapes=list(scratch),
        compiler_params=pltpu.CompilerParams(vmem_limit_bytes=48 << 20),
        cost_estimate=pl.CostEstimate(flops=0, bytes_accessed=int(us * 3.69e6), transcendentals=0),
    )(*operands)


def exchange(array, bit):
    count = math.prod(lax.axis_size(a) for a in AXES)
    return lax.ppermute(array, AXES, [(i, i ^ bit) for i in range(count)])


def add_kernel(terms, handed, *refs):
    outs = refs[len(refs) - 1 - handed :]
    parts = [ref[...] for ref in refs[:terms]]
    while len(parts) > 1:
        parts = [sum(parts[i : i + 2]) for i in range(0, len(parts), 2)]
    outs[0][...] = parts[0]
    for given, out in zip(refs[terms : terms + handed], outs[1:], strict=True):
        out[...] = given[...]


def add(parts, beside=(), through=()):
    operands = (*parts, *through, *beside)
    specs = [VMEM] * (len(parts) + len(through)) + [ANY] * len(beside)
    kernel = functools.partial(add_kernel, len(parts), len(through))
    outs = call(kernel, [parts[0].shape, *(t.shape for t in through)], operands, specs)
    return outs if through else outs[0]


def sum_steps():
    count = math.prod(lax.axis_size(a) for a in AXES)
    bits = [1 << i for i in range(1, count.bit_length() - 1)]
    assert 1 << (len(bits) + 1) == count and len(bits) > 1
    return [(bits[0], bits[1], bits[0] | bits[1])] + [(bit,) for bit in bits[2:]]


def scatter_kernel(keep_ref, received_ref, tie_ref, mine_ref, *send_refs):
    del tie_ref
    place = lax.axis_index(AXES) // 2 % 4
    for i, ref in enumerate((mine_ref, *send_refs)):
        part = place ^ i
        ref[...] = (keep_ref[pl.ds(part, 1)] + received_ref[pl.ds(part, 1)])[0]


def gather_kernel(mine_ref, *rest):
    out_ref = rest[-1]
    place = lax.axis_index(AXES) // 2 % 4
    for i, ref in enumerate((mine_ref, *rest[:-2])):
        out_ref[pl.ds(place ^ i, 1)] = ref[...][None]


def sum_by_quarters(keep, send, works):
    first, *others = sum_steps()
    others = [bit for (bit,) in others]
    others = [(*pair, sum(pair))[: 2 * len(pair) - 1] for pair in (others[i : i + 2] for i in range(0, len(others), 2))]
    block = keep.shape[1:]
    operands = (keep, exchange(send, 1), works[0](keep))
    mine, *parts = call(scatter_kernel, [block] * 4, operands, [VMEM, VMEM, ANY])
    received = [exchange(part, bit) for part, bit in zip(parts, first, strict=True)]
    mine = add((mine, *received), works[1](mine))
    for i, bits in enumerate(others):
        received = [exchange(mine, bit) for bit in bits]
        mine = add((mine, *received), works[2](mine) if i == len(others) - 1 else ())
    received = [exchange(mine, bit) for bit in first]
    operands = (mine, *received, works[3](mine))
    (total,) = call(gather_kernel, [keep.shape], operands, [VMEM] * 4 + [ANY])
    return total


def shifted(array, axis, by, round_off=False):
    length = lax.axis_size(axis)
    pairs = [(i, (i + by) % length) for i in range(length) if round_off or 0 <= i + by < length]
    return lax.ppermute(array, axis, pairs)


def order_halves(mine, other):
    odd = lax.axis_index(AXES) % 2
    return jnp.where(odd == 0, mine, other), jnp.where(odd == 0, other, mine)


def pack_block(block):
    h, q = block.shape[0], block.shape[0] // 2
    e = q // 2
    lane = lax.broadcasted_iota(jnp.int32, (e, h), 1)
    corner = jnp.where(lane < q, pltpu.roll(block[q : q + e], q, 1), block[q + e :])
    return jnp.concatenate([block[:q], corner], axis=0)


def unpack_block(rows):
    h = rows.shape[1]
    q = h // 2
    lane = lax.broadcasted_iota(jnp.int32, (q, h), 1)
    low = jnp.concatenate([pltpu.roll(rows[q:], q, 1), rows[q:]], axis=0)
    square = jnp.concatenate([rows[:q], low], axis=0)
    return jnp.concatenate([rows[:q], jnp.where(lane < q, square.T[q:], low)], axis=0)


def pack(square):
    h = square.shape[0] // 2
    return jnp.concatenate([pack_block(square[:h, :h]), pack_block(square[h:, h:]), square[:h, h:]], axis=0)


def unpack(rows):
    h = rows.shape[1]
    p = 3 * h // 4
    corner = rows[2 * p :]
    upper = jnp.concatenate([unpack_block(rows[:p]), corner], axis=1)
    return jnp.concatenate([upper, jnp.concatenate([corner.T, unpack_block(rows[p : 2 * p])], axis=1)], axis=0)


def gram_kernel(s_ref, keep_ref, send_ref):
    width = s_ref.shape[2]
    flat = s_ref[...].reshape(-1, width)
    flat = pieces_of(flat)
    gram = dot6(flat, flat, 0, 0)
    h, q = width // 2, width // 4
    even = jnp.concatenate([pack_block(gram[h:, h:]), gram[:q, h:]], axis=0)
    odd = jnp.concatenate([pack_block(gram[:h, :h]), gram[q:h, h:]], axis=0)
    keep_ref[...], send_ref[...] = order_halves(even, odd)


def picks(node_count, first, second):
    node = lax.broadcasted_iota(jnp.int32, (first.shape[0], node_count), 1).astype(jnp.float32)
    pick = (node == first).astype(jnp.float32) - (node == second).astype(jnp.float32)
    return pick.astype(jnp.bfloat16)


def picked(pick, pieces):
    return sum(jnp.dot(pick, piece, preferred_element_type=jnp.float32) for piece in pieces)


def own_elongation(first, table, s_ref, long_ref):
    nodes = s_ref.shape[1]
    pieces = [pieces_of(s_ref[c]) for c in range(3)]
    for start in range(0, long_ref.shape[0], CHUNK):
        rows = table[first + start : first + start + CHUNK, :]
        pick = picks(nodes, rows[:, 0:1], rows[:, 1:2])
        long_ref[start : start + CHUNK, :] = sum(rows[:, 2 + c : 3 + c] * picked(pick, pieces[c]) for c in range(3))


def first_elongation_kernel(ends_ref, dir_ref, stiff_ref, s_ref, tie_ref, long_ref, table_ref):
    del tie_ref
    ends = ends_ref[...].astype(jnp.float32)
    table_ref[...] = jnp.concatenate([ends, dir_ref[...], stiff_ref[...], jnp.zeros_like(ends)], axis=0).T
    own_elongation(0, table_ref, s_ref, long_ref)


def second_elongation_kernel(table_ref, s_ref, tie_ref, long_ref):
    del tie_ref
    own_elongation(long_ref.shape[0], table_ref, s_ref, long_ref)


def below_elongation_kernel(table_ref, below_ref, first_ref, second_ref, tie_ref, long_ref):
    del tie_ref
    stands = lax.axis_index("span") == 0
    pieces = [pieces_of(jnp.where(stands, 0.0, below_ref[c])) for c in range(3)]
    split = first_ref.shape[0]
    for half, given in enumerate((first_ref, second_ref)):
        for start in range(0, split, CHUNK):
            at = split * half + start
            rows = table_ref[at : at + CHUNK, :]
            pick = picks(SEC_NODES, rows[:, 0:1] - NODES, rows[:, 1:2] - NODES)
            added = sum(rows[:, 2 + c : 3 + c] * picked(pick, pieces[c]) for c in range(3))
            long_ref[at : at + CHUNK, :] = given[start : start + CHUNK, :] + added


def force_kernel(table_ref, ends_ref, long_ref, top_ref, tie_ref, own_ref):
    del tie_ref
    nodes = own_ref.shape[1]
    members = long_ref.shape[0]
    axial = long_ref[...] * table_ref[:, 5:6]
    node = lax.broadcasted_iota(jnp.int32, (nodes, members), 0)
    ends = ends_ref[...]
    spread = (node == ends[0:1]).astype(jnp.float32) - (node == ends[1:2]).astype(jnp.float32)
    spread = spread.astype(jnp.bfloat16)
    for c in range(3):
        force = picked(spread, halves(table_ref[:, 2 + c : 3 + c] * axial))
        own_ref[c, : nodes - SEC_NODES] = force[: nodes - SEC_NODES]
        own_ref[c, nodes - SEC_NODES :] = force[nodes - SEC_NODES :] - top_ref[c]


def downward_kernel(s_ref, ends_ref, dir_ref, stiff_ref, tie_ref, out_ref):
    del tie_ref
    width = out_ref.shape[1]
    rows = 3 * SEC_NODES
    out_ref[:rows] = s_ref[:, :SEC_NODES].reshape(rows, width)
    table = jnp.concatenate([ends_ref[...].astype(jnp.float32), dir_ref[...], stiff_ref[...]], axis=0)
    out_ref[rows:] = jnp.concatenate([table[:, at : at + width] for at in range(0, table.shape[1], width)], axis=0)


def above_elongation_kernel(above_ref, s_ref, tie_ref, long_ref, table_ref, seconds_ref):
    del tie_ref
    nodes, width = s_ref.shape[1:]
    rows = 3 * SEC_NODES
    held = above_ref[rows:]
    table = jnp.concatenate([held[at : at + 6] for at in range(0, held.shape[0], 6)], axis=1)
    table = jnp.concatenate([table, jnp.zeros_like(table[:2])], axis=0)
    seconds_ref[...] = table
    table_ref[...] = table.T
    top = lax.axis_index("span") == lax.axis_size("span") - 1
    pieces = []
    for c in range(3):
        both = jnp.concatenate([above_ref[SEC_NODES * c : SEC_NODES * (c + 1)], s_ref[c, nodes - SEC_NODES :]], axis=0)
        pieces.append(pieces_of(jnp.where(top, 0.0, both)))
    for start in range(0, long_ref.shape[0], CHUNK):
        members = table_ref[start : start + CHUNK, :]
        second = members[:, 1:2] - nodes
        first = jnp.where(second >= 0.0, members[:, 0:1], -1.0)
        pick = picks(2 * SEC_NODES, first, second + jnp.where(second >= 0.0, 1.0 * SEC_NODES, -1.0 * nodes))
        long_ref[start : start + CHUNK, :] = sum(members[:, 2 + c : 3 + c] * picked(pick, pieces[c]) for c in range(3))


def above_force_kernel(nodes, table_ref, seconds_ref, long_ref, w_ref, tie_ref, top_ref):
    del tie_ref
    axial = dot6(pieces_of(long_ref[...]), pieces_of(w_ref[...])) * table_ref[:, 5:6]
    node = lax.broadcasted_iota(jnp.int32, (SEC_NODES, long_ref.shape[0]), 0).astype(jnp.float32)
    spread = (node == seconds_ref[1:2] - nodes).astype(jnp.float32).astype(jnp.bfloat16)
    for c in range(3):
        top_ref[c] = picked(spread, halves(table_ref[:, 2 + c : 3 + c] * axial))


def factor_block(x_ref, u_ref, m_ref, rows_ref):
    n = x_ref.shape[0]
    count = n // 8
    tiles = [x_ref[8 * i : 8 * i + 8, :] for i in range(count)]
    lane = lax.broadcasted_iota(jnp.int32, (8, n), 1)
    sub = lax.broadcasted_iota(jnp.int32, (8, n), 0)

    def column(tile, c):
        return jnp.broadcast_to(tile[:, c : c + 1], (8, n))

    for p in range(count):
        c0 = 8 * p
        rows_ref[c0 : c0 + 8, :] = tiles[p]
        u = [rows_ref[pl.ds(c0 + r, 8, stride=0), :] for r in range(8)]
        a = [[column(u[r], c0 + c) if c >= r else None for c in range(8)] for r in range(8)]
        panel = (lane >= c0) & (lane < c0 + 8)
        v = [jnp.where(panel, jnp.where(lane == c0 + k, 1.0, 0.0), u[k]) for k in range(8)]
        cols = {t: [column(tiles[t], c0 + k) for k in range(8)] for t in range(p + 1, count)}
        for t in cols:
            tiles[t] = jnp.where(panel, 0.0, tiles[t])
        for k in range(8):
            inverse = pltpu.reciprocal(a[k][k])
            scaled = v[k] * inverse
            for i in range(k + 1, 8):
                f = a[k][i] * inverse
                for j in range(i, 8):
                    a[i][j] = a[i][j] - f * a[k][j]
                v[i] = v[i] - f * v[k]
                u[i] = u[i] - f * u[k]
                for t in cols:
                    cols[t][i] = cols[t][i] - f * cols[t][k]
            for t in cols:
                tiles[t] = tiles[t] - cols[t][k] * scaled
        yt, ut = v[0], u[0]
        for i in range(1, 8):
            yt = jnp.where(sub == i, v[i], yt)
            ut = jnp.where(sub == i, u[i], ut)
        u_ref[c0 : c0 + 8, :] = ut
        m_ref[c0 : c0 + 8, :] = yt


def factored(block, x, u, m, rows):
    h = block.shape[0]
    rowi = lax.broadcasted_iota(jnp.int32, (h, h), 0)
    coli = lax.broadcasted_iota(jnp.int32, (h, h), 1)
    x[...] = block
    factor_block(x, u, m, rows)
    upper = u[...]
    s = lax.rsqrt(jnp.sum(jnp.where(rowi == coli, upper, 0.0), axis=1, keepdims=True))
    return jnp.where(rowi <= coli, upper, 0.0) * s, jnp.where(rowi >= coli, m[...], 0.0) * s


def finish_factor(r11, m1, g12, g22, w_ref, r_ref, scratch):
    h = r11.shape[0]
    r12 = dot(m1, g12)
    r22, m2 = factored(g22 - dot(r12, r12, 0, 0), *scratch)
    zero = jnp.zeros((h, h), jnp.float32)
    r_ref[:h, :h], r_ref[:h, h:], r_ref[h:, :h], r_ref[h:, h:] = r11, r12, zero, r22
    w_ref[:h, :h], w_ref[h:, h:], w_ref[h:, :h] = m1.T, m2.T, zero
    w_ref[:h, h:] = -dot(m1, dot(r12, m2, 1, 1), 0, 0)


def on_diagonal(block):
    shape = block.shape
    eye = lax.broadcasted_iota(jnp.int32, shape, 0) == lax.broadcasted_iota(jnp.int32, shape, 1)
    return jnp.sum(jnp.where(eye, block, 0.0), axis=0, keepdims=True)


def first_block_kernel(sum_ref, message_ref, *scratch):
    odd = lax.axis_index(AXES) % 2 == 1
    h = sum_ref.shape[1]
    p = 3 * h // 4

    @pl.when(odd)
    def _():
        g11 = unpack_block(sum_ref[:p])
        r11, m1 = factored(g11, *scratch)
        rowi = lax.broadcasted_iota(jnp.int32, (h, h), 0)
        coli = lax.broadcasted_iota(jnp.int32, (h, h), 1)
        message_ref[:h] = jnp.where(rowi < coli, r11, m1)
        message_ref[h : h + h // 2] = sum_ref[p:]
        message_ref[h + h // 2 :] = jnp.broadcast_to(on_diagonal(g11), (8, h))

    @pl.when(jnp.logical_not(odd))
    def _():
        message_ref[: sum_ref.shape[0]] = sum_ref[...]
        message_ref[sum_ref.shape[0] :] = jnp.zeros_like(message_ref[sum_ref.shape[0] :])


def second_block_kernel(mine_ref, other_ref, w_ref, r_ref, diag_ref, *scratch):
    h = mine_ref.shape[1]
    p, q = 3 * h // 4, h // 2
    even, odd = order_halves(mine_ref[...], other_ref[...])
    rowi = lax.broadcasted_iota(jnp.int32, (h, h), 0)
    coli = lax.broadcasted_iota(jnp.int32, (h, h), 1)
    m1 = jnp.where(rowi >= coli, odd[:h], 0.0)
    r11 = jnp.where(rowi < coli, odd[:h], jnp.where(rowi == coli, pltpu.reciprocal(odd[:h]), 0.0))
    g12 = jnp.concatenate([even[p : p + q], odd[h : h + q]], axis=0)
    g22 = unpack_block(even[:p])
    diag_ref[:, :h] = odd[h + q : h + q + 1]
    diag_ref[:, h:] = on_diagonal(g22)
    finish_factor(r11, m1, g12, g22, w_ref, r_ref, scratch)


def middle_kernel(s_ref, long_ref, table_ref, w_ref, q_ref, q_halves, long_out, keep_ref, send_ref):
    parts, nodes, width = s_ref.shape
    w = w_ref[...]
    w = pieces_of(w)
    q = dot6(pieces_of(s_ref[...].reshape(-1, width)), w)
    q_ref[...] = q.reshape(parts, nodes, width)
    long = dot6(pieces_of(long_ref[...]), w)
    long_out[...] = long
    q = halves(q)
    for i in range(2):
        q_halves[i] = q[i].reshape(parts, nodes, width)
    gram = dot3(q, q, 0, 0)
    energy = dot3(halves(long), halves(long * table_ref[:, 5:6]), 0, 0)
    keep, send = order_halves(pack(energy), pack(gram))
    keep_ref[...] = keep.reshape(keep_ref.shape)
    send_ref[...] = send.reshape(send_ref.shape)


def refine_kernel(rows_all, w_ref, r_ref, diag_ref, tie_ref, out_ref, log_ref):
    del tie_ref
    log_ref[...] = jnp.log(diag_ref[...] / rows_all)

    @pl.when(lax.axis_index(AXES) % 2 == 1)
    def _():
        r = r_ref[...]
        size = r.shape[0]
        eye = lax.broadcasted_iota(jnp.int32, (size, size), 0) == lax.broadcasted_iota(jnp.int32, (size, size), 1)
        out_ref[...] = r + dot(jnp.where(eye, 1.0, 0.0) - dot(r, w_ref[...]), r)


def second_factor_kernel(rows_all, sum_ref, r1_ref, message_ref, *scratch):
    odd = lax.axis_index(AXES) % 2 == 1
    width = message_ref.shape[1]
    h = width // 2
    packed = sum_ref[...].reshape(-1, h)
    half = packed.shape[0] // 2

    @pl.when(odd)
    def _():
        second_factor(rows_all, unpack(packed), r1_ref, message_ref, *scratch)

    @pl.when(jnp.logical_not(odd))
    def _():
        message_ref[:half] = jnp.concatenate([packed[:half], packed[half:]], axis=1)
        message_ref[half:] = jnp.zeros_like(message_ref[half:])


def second_factor(rows_all, gram, r1_ref, message_ref, v_ref, e_ref, w2, r2, *scratch):
    width = gram.shape[0]
    h = width // 2
    rowi = lax.broadcasted_iota(jnp.int32, (width, width), 0)
    coli = lax.broadcasted_iota(jnp.int32, (width, width), 1)
    eye = jnp.where(rowi == coli, 1.0, 0.0)
    start = gram - eye

    def upper_half(e):
        return jnp.where(rowi < coli, e, jnp.where(rowi == coli, 0.5 * e, 0.0))

    e_ref[...] = start
    size = jnp.sum(start * start)

    @pl.when(size < 0.06)
    def _():
        v_ref[...] = -upper_half(start)

        def improve(i, carry):
            e = e_ref[...]
            upper = upper_half(e)
            split = halves(upper)
            p = dot3(halves(e), split)
            e = dot3(split, halves(upper + p), 0, 0) - (p + p.T)
            e_ref[...] = e
            upper = upper_half(e)
            v = v_ref[...]
            v_ref[...] = v - (upper + dot3(halves(v), halves(upper)))
            return carry

        lax.fori_loop(0, 2, improve, 0)

    @pl.when(jnp.logical_not(size < 0.06))
    def _():
        r11, m1 = factored(gram[:h, :h], *scratch)
        finish_factor(r11, m1, gram[:h, h:], gram[h:, h:], w2, r2, scratch)
        v_ref[...] = w2[...] - eye

    v = v_ref[...]
    change = jnp.where(rowi <= coli, v.T + start + dot3(halves(v), halves(start), 0, 0), 0.0)
    r1 = r1_ref[...]
    coef = (r1 + dot3(halves(change), halves(r1))) * (1.0 / math.sqrt(rows_all))
    message_ref[:width] = jnp.where(rowi < coli, v, coef.T)
    message_ref[width:] = jnp.broadcast_to(on_diagonal(v), (8, width))


def final_kernel(
    rows_all, mine_ref, other_ref, q_ref, q_halves, own_ref,
    basis_ref, forces_ref, reduced_ref, coef_ref, held, sems,
):
    parts, nodes, width = q_ref.shape
    h = width // 2
    even, odd = order_halves(mine_ref[...], other_ref[...])
    rowi = lax.broadcasted_iota(jnp.int32, (width, width), 0)
    coli = lax.broadcasted_iota(jnp.int32, (width, width), 1)
    diag = jnp.where(rowi == coli, odd[width : width + 1], 0.0)
    v = halves(jnp.where(rowi < coli, odd[:width], diag))
    root = math.sqrt(rows_all)
    copies = []
    for k in range(2 * parts):
        c = k % parts
        if k < parts:
            source, split, target = q_ref[c], (q_halves[0, c], q_halves[1, c]), basis_ref
        else:
            source, target = own_ref[c], forces_ref
            split = halves(source)
        held[k] = (source + dot3(split, v)) * root
        copies.append(pltpu.make_async_copy(held.at[k], target.at[c], sems.at[k]))
        copies[-1].start()
    coef_ref[...] = jnp.where(rowi <= coli, odd[:width].T, 0.0)
    half = 5 * h // 4
    energy = unpack(jnp.concatenate([even[:half, :h], even[:half, h:]], axis=0))
    right = energy + dot3(halves(energy), v)
    reduced_ref[...] = right + dot3(v, halves(right), 0, 0)
    for copy in copies:
        copy.wait()


def local(snapshots, member_ends, member_dir, member_stiff):
    parts, nodes, width = snapshots.shape
    h = width // 2
    count = math.prod(lax.axis_size(a) for a in AXES)
    rows_all = parts * nodes * count
    steps = sum_steps()
    square = (width, width)
    field = (parts, nodes, width)
    packed = (5 * width // 8, h)
    scratch = [pltpu.VMEM((h, h), jnp.float32)] * 3 + [pltpu.VMEM((h + 8, h), jnp.float32)]

    below = shifted(snapshots[:, nodes - SEC_NODES :, :], "span", 1, True)
    keep, send = call(gram_kernel, [packed, packed], (snapshots,))
    members = member_dir.shape[1]
    split = members // 2
    total = add((keep, exchange(send, 1)))
    for i, bits in enumerate(steps):
        received = [exchange(total, bit) for bit in bits]
        if i == 0:
            first, table = call(
                first_elongation_kernel,
                [(split, width), (members, 8)],
                (member_ends, member_dir, member_stiff[None], snapshots, total),
                [VMEM] * 4 + [ANY],
            )
            second = call(second_elongation_kernel, [(split, width)], (table, snapshots, total), [VMEM, VMEM, ANY])
            long = [first, *second]
            total = add((total, *received), long)
        elif i < len(steps) - 1:
            total = add((total, *received))
        else:
            operands = (table, below, *long, total)
            (stretch,) = call(below_elongation_kernel, [(members, width)], operands, [VMEM] * 4 + [ANY])
            (downward,) = call(
                downward_kernel,
                [(3 * SEC_NODES + 6 * members // width, width)],
                (snapshots, member_ends, member_dir, member_stiff[None], total),
                [VMEM] * 4 + [ANY],
            )
            total, downward = add((total, *received), (stretch,), (downward,))
    above = shifted(downward, "span", -1, True)
    (message,) = call(first_block_kernel, [(h + h // 2 + 8, h)], (total,), scratch=scratch, us=2)
    w1, r1, diag = call(
        second_block_kernel, [square, square, (1, width)], (message, exchange(message, 1)), scratch=scratch, us=5
    )

    quarters = (4, 5 * width // 16, h)
    q, q_halves, stretch, keep, send = call(
        middle_kernel,
        [field, jax.ShapeDtypeStruct((2, *field), jnp.bfloat16), (members, width), quarters, quarters],
        (snapshots, stretch, table, w1),
        us=3,
    )
    def refined(tie):
        refine = functools.partial(refine_kernel, rows_all)
        made["r1"] = call(refine, [square, (1, width)], (w1, r1, diag, tie), [VMEM] * 3 + [ANY], us=1)
        return made["r1"][0]

    def above_elongation(tie):
        shapes = [(members, width), (members, 8), (8, members)]
        made["above"] = call(above_elongation_kernel, shapes, (above, snapshots, tie), [VMEM] * 2 + [ANY], us=2)
        return made["above"][:1]

    def above_forces(tie):
        stretch_above, table_above, seconds = made["above"]
        operands = (table_above, seconds, stretch_above, w1, tie)
        kernel = functools.partial(above_force_kernel, nodes)
        made["top"] = call(kernel, [(parts, SEC_NODES, width)], operands, [VMEM] * 4 + [ANY], us=2.5)
        return made["top"]

    def own_forces(tie):
        operands = (table, member_ends, stretch, made["top"][0], tie)
        (made["own"],) = call(force_kernel, [field], operands, [VMEM] * 4 + [ANY], us=1.5)
        return made["own"]

    made = {}
    total = sum_by_quarters(keep, send, [refined, above_elongation, above_forces, own_forces])
    r1, column_energy = made["r1"]

    (message,) = call(
        functools.partial(second_factor_kernel, rows_all),
        [(width + 8, width)],
        (total, r1),
        scratch=[pltpu.VMEM(square, jnp.float32)] * 4 + scratch,
    )
    basis, forces, reduced, coef = call(
        functools.partial(final_kernel, rows_all),
        [field, field, square, square],
        (message, exchange(message, 1), q, q_halves, made["own"]),
        scratch=[pltpu.VMEM((2 * parts, nodes, width), jnp.float32), pltpu.SemaphoreType.DMA((2 * parts,))],
        outs=(HBM, HBM, VMEM, VMEM),
    )
    return (basis, forces, reduced, coef, column_energy[0])


def solution(mesh):
    placed = (
        P(None, AXES, None),
        P(None, AXES),
        P(None, AXES),
        P(AXES),
    )
    return jax.shard_map(
        local,
        mesh=mesh,
        in_specs=placed,
        out_specs=(P(None, AXES, None), P(None, AXES, None), P(), P(), P()),
        check_vma=False,
    )
```

```python
import functools
import math

import jax
import jax.numpy as jnp
from jax import lax
from jax.experimental import pallas as pl
from jax.experimental.pallas import tpu as pltpu
from jax.sharding import PartitionSpec as P

AXES = ("span", "xsec", "leaf")
SEC_NODES = 128
NODES = 256
CHUNK = 256
highest = lax.Precision.HIGHEST
VMEM = pl.BlockSpec(memory_space=pltpu.VMEM)
ANY = pl.BlockSpec(memory_space=pl.ANY)
HBM = pl.BlockSpec(memory_space=pltpu.HBM)


def dot(a, b, ca=1, cb=0):
    return lax.dot_general(
        a, b, (((ca,), (cb,)), ((), ())), precision=highest, preferred_element_type=jnp.float32
    )


def halves(x):
    high = x.astype(jnp.bfloat16)
    return high, (x - high.astype(jnp.float32)).astype(jnp.bfloat16)


def dot3(a, b, ca=1, cb=0):
    def one(x, y):
        return lax.dot_general(x, y, (((ca,), (cb,)), ((), ())), preferred_element_type=jnp.float32)

    return one(a[0], b[0]) + (one(a[0], b[1]) + one(a[1], b[0]))


def pieces_of(x):
    first = x.astype(jnp.bfloat16)
    rest = x - first.astype(jnp.float32)
    second = rest.astype(jnp.bfloat16)
    third = (rest - second.astype(jnp.float32)).astype(jnp.bfloat16)
    return first, second, third


def dot6(a, b, ca=1, cb=0):
    def one(i, j):
        return lax.dot_general(a[i], b[j], (((ca,), (cb,)), ((), ())), preferred_element_type=jnp.float32)

    return one(0, 0) + ((one(0, 1) + one(1, 0)) + ((one(0, 2) + one(2, 0)) + one(1, 1)))


def gram_of(parts):
    def one(i, j):
        return lax.dot_general(parts[i], parts[j], (((0,), (0,)), ((), ())), preferred_element_type=jnp.float32)

    mixed = one(0, 1) if len(parts) == 2 else one(0, 1) + one(0, 2)
    mixed = mixed + mixed.T
    return one(0, 0) + (mixed if len(parts) == 2 else mixed + one(1, 1))


def call(kernel, shapes, operands, specs=None, scratch=(), outs=None, us=0.1):
    return pl.pallas_call(
        kernel,
        out_shape=tuple(s if isinstance(s, jax.ShapeDtypeStruct) else jax.ShapeDtypeStruct(s, jnp.float32) for s in shapes),
        in_specs=specs or [VMEM] * len(operands),
        out_specs=outs or tuple(VMEM for _ in shapes),
        scratch_shapes=list(scratch),
        compiler_params=pltpu.CompilerParams(vmem_limit_bytes=48 << 20),
        cost_estimate=pl.CostEstimate(flops=0, bytes_accessed=int(us * 3.69e6), transcendentals=0),
    )(*operands)


def exchange(array, bit):
    count = math.prod(lax.axis_size(a) for a in AXES)
    return lax.ppermute(array, AXES, [(i, i ^ bit) for i in range(count)])


def add_kernel(terms, handed, *refs):
    outs = refs[len(refs) - 1 - handed :]
    parts = [ref[...] for ref in refs[:terms]]
    while len(parts) > 1:
        parts = [sum(parts[i : i + 2]) for i in range(0, len(parts), 2)]
    outs[0][...] = parts[0]
    for given, out in zip(refs[terms : terms + handed], outs[1:], strict=True):
        out[...] = given[...]


def add(parts, beside=(), through=()):
    operands = (*parts, *through, *beside)
    specs = [VMEM] * (len(parts) + len(through)) + [ANY] * len(beside)
    kernel = functools.partial(add_kernel, len(parts), len(through))
    outs = call(kernel, [parts[0].shape, *(t.shape for t in through)], operands, specs)
    return outs if through else outs[0]


def sum_steps():
    count = math.prod(lax.axis_size(a) for a in AXES)
    bits = [1 << i for i in range(1, count.bit_length() - 1)]
    assert 1 << (len(bits) + 1) == count and len(bits) > 1
    return [(bits[0], bits[1], bits[0] | bits[1])] + [(bit,) for bit in bits[2:]]


def scatter_kernel(keep_ref, received_ref, tie_ref, mine_ref, *send_refs):
    del tie_ref
    place = lax.axis_index(AXES) // 2 % 4
    for i, ref in enumerate((mine_ref, *send_refs)):
        part = place ^ i
        ref[...] = (keep_ref[pl.ds(part, 1)] + received_ref[pl.ds(part, 1)])[0]


def gather_kernel(mine_ref, *rest):
    out_ref = rest[-1]
    place = lax.axis_index(AXES) // 2 % 4
    for i, ref in enumerate((mine_ref, *rest[:-2])):
        out_ref[pl.ds(place ^ i, 1)] = ref[...][None]


def sum_by_quarters(keep, send, works):
    first, *others = sum_steps()
    others = [bit for (bit,) in others]
    others = [(*pair, sum(pair))[: 2 * len(pair) - 1] for pair in (others[i : i + 2] for i in range(0, len(others), 2))]
    block = keep.shape[1:]
    operands = (keep, exchange(send, 1), works[0](keep))
    mine, *parts = call(scatter_kernel, [block] * 4, operands, [VMEM, VMEM, ANY])
    received = [exchange(part, bit) for part, bit in zip(parts, first, strict=True)]
    mine = add((mine, *received), works[1](mine))
    for i, bits in enumerate(others):
        received = [exchange(mine, bit) for bit in bits]
        mine = add((mine, *received), works[2](mine) if i == len(others) - 1 else ())
    received = [exchange(mine, bit) for bit in first]
    operands = (mine, *received, works[3](mine))
    (total,) = call(gather_kernel, [keep.shape], operands, [VMEM] * 4 + [ANY])
    return total


def shifted(array, axis, by, round_off=False):
    length = lax.axis_size(axis)
    pairs = [(i, (i + by) % length) for i in range(length) if round_off or 0 <= i + by < length]
    return lax.ppermute(array, axis, pairs)


def order_halves(mine, other):
    odd = lax.axis_index(AXES) % 2
    return jnp.where(odd == 0, mine, other), jnp.where(odd == 0, other, mine)


def pack_block(block):
    h, q = block.shape[0], block.shape[0] // 2
    e = q // 2
    lane = lax.broadcasted_iota(jnp.int32, (e, h), 1)
    corner = jnp.where(lane < q, pltpu.roll(block[q : q + e], q, 1), block[q + e :])
    return jnp.concatenate([block[:q], corner], axis=0)


def unpack_block(rows):
    h = rows.shape[1]
    q = h // 2
    lane = lax.broadcasted_iota(jnp.int32, (q, h), 1)
    low = jnp.concatenate([pltpu.roll(rows[q:], q, 1), rows[q:]], axis=0)
    square = jnp.concatenate([rows[:q], low], axis=0)
    return jnp.concatenate([rows[:q], jnp.where(lane < q, square.T[q:], low)], axis=0)


def pack(square):
    h = square.shape[0] // 2
    return jnp.concatenate([pack_block(square[:h, :h]), pack_block(square[h:, h:]), square[:h, h:]], axis=0)


def unpack(rows):
    h = rows.shape[1]
    p = 3 * h // 4
    corner = rows[2 * p :]
    upper = jnp.concatenate([unpack_block(rows[:p]), corner], axis=1)
    return jnp.concatenate([upper, jnp.concatenate([corner.T, unpack_block(rows[p : 2 * p])], axis=1)], axis=0)


def gram_kernel(s_ref, keep_ref, send_ref):
    width = s_ref.shape[2]
    flat = s_ref[...].reshape(-1, width)
    flat = pieces_of(flat)
    gram = gram_of(flat)
    h, q = width // 2, width // 4
    even = jnp.concatenate([pack_block(gram[h:, h:]), gram[:q, h:]], axis=0)
    odd = jnp.concatenate([pack_block(gram[:h, :h]), gram[q:h, h:]], axis=0)
    keep_ref[...], send_ref[...] = order_halves(even, odd)


def picks(node_count, first, second):
    node = lax.broadcasted_iota(jnp.int32, (first.shape[0], node_count), 1).astype(jnp.float32)
    pick = (node == first).astype(jnp.float32) - (node == second).astype(jnp.float32)
    return pick.astype(jnp.bfloat16)


def picked(pick, pieces):
    return sum(jnp.dot(pick, piece, preferred_element_type=jnp.float32) for piece in pieces)


def own_elongation(first, table, s_ref, long_ref):
    nodes = s_ref.shape[1]
    pieces = [pieces_of(s_ref[c]) for c in range(3)]
    for start in range(0, long_ref.shape[0], CHUNK):
        rows = table[first + start : first + start + CHUNK, :]
        pick = picks(nodes, rows[:, 0:1], rows[:, 1:2])
        long_ref[start : start + CHUNK, :] = sum(rows[:, 2 + c : 3 + c] * picked(pick, pieces[c]) for c in range(3))


def first_elongation_kernel(ends_ref, dir_ref, stiff_ref, s_ref, tie_ref, long_ref, table_ref):
    del tie_ref
    ends = ends_ref[...].astype(jnp.float32)
    table_ref[...] = jnp.concatenate([ends, dir_ref[...], stiff_ref[...], jnp.zeros_like(ends)], axis=0).T
    own_elongation(0, table_ref, s_ref, long_ref)


def second_elongation_kernel(table_ref, s_ref, tie_ref, long_ref):
    del tie_ref
    own_elongation(long_ref.shape[0], table_ref, s_ref, long_ref)


def below_elongation_kernel(table_ref, below_ref, first_ref, second_ref, tie_ref, long_ref):
    del tie_ref
    stands = lax.axis_index("span") == 0
    pieces = [pieces_of(jnp.where(stands, 0.0, below_ref[c])) for c in range(3)]
    split = first_ref.shape[0]
    for half, given in enumerate((first_ref, second_ref)):
        for start in range(0, split, CHUNK):
            at = split * half + start
            rows = table_ref[at : at + CHUNK, :]
            pick = picks(SEC_NODES, rows[:, 0:1] - NODES, rows[:, 1:2] - NODES)
            added = sum(rows[:, 2 + c : 3 + c] * picked(pick, pieces[c]) for c in range(3))
            long_ref[at : at + CHUNK, :] = given[start : start + CHUNK, :] + added


def force_kernel(table_ref, ends_ref, long_ref, top_ref, tie_ref, own_ref):
    del tie_ref
    nodes = own_ref.shape[1]
    members = long_ref.shape[0]
    axial = long_ref[...] * table_ref[:, 5:6]
    node = lax.broadcasted_iota(jnp.int32, (nodes, members), 0)
    ends = ends_ref[...]
    spread = (node == ends[0:1]).astype(jnp.float32) - (node == ends[1:2]).astype(jnp.float32)
    spread = spread.astype(jnp.bfloat16)
    for c in range(3):
        force = picked(spread, halves(table_ref[:, 2 + c : 3 + c] * axial))
        own_ref[c, : nodes - SEC_NODES] = force[: nodes - SEC_NODES]
        own_ref[c, nodes - SEC_NODES :] = force[nodes - SEC_NODES :] - top_ref[c]


def downward_kernel(s_ref, ends_ref, dir_ref, stiff_ref, tie_ref, out_ref):
    del tie_ref
    width = out_ref.shape[1]
    rows = 3 * SEC_NODES
    out_ref[:rows] = s_ref[:, :SEC_NODES].reshape(rows, width)
    table = jnp.concatenate([ends_ref[...].astype(jnp.float32), dir_ref[...], stiff_ref[...]], axis=0)
    out_ref[rows:] = jnp.concatenate([table[:, at : at + width] for at in range(0, table.shape[1], width)], axis=0)


def above_elongation_kernel(above_ref, s_ref, tie_ref, long_ref, table_ref, seconds_ref):
    del tie_ref
    nodes, width = s_ref.shape[1:]
    rows = 3 * SEC_NODES
    held = above_ref[rows:]
    table = jnp.concatenate([held[at : at + 6] for at in range(0, held.shape[0], 6)], axis=1)
    table = jnp.concatenate([table, jnp.zeros_like(table[:2])], axis=0)
    seconds_ref[...] = table
    table_ref[...] = table.T
    top = lax.axis_index("span") == lax.axis_size("span") - 1
    pieces = []
    for c in range(3):
        both = jnp.concatenate([above_ref[SEC_NODES * c : SEC_NODES * (c + 1)], s_ref[c, nodes - SEC_NODES :]], axis=0)
        pieces.append(pieces_of(jnp.where(top, 0.0, both)))
    for start in range(0, long_ref.shape[0], CHUNK):
        members = table_ref[start : start + CHUNK, :]
        second = members[:, 1:2] - nodes
        first = jnp.where(second >= 0.0, members[:, 0:1], -1.0)
        pick = picks(2 * SEC_NODES, first, second + jnp.where(second >= 0.0, 1.0 * SEC_NODES, -1.0 * nodes))
        long_ref[start : start + CHUNK, :] = sum(members[:, 2 + c : 3 + c] * picked(pick, pieces[c]) for c in range(3))


def above_force_kernel(nodes, table_ref, seconds_ref, long_ref, w_ref, tie_ref, top_ref):
    del tie_ref
    axial = dot6(pieces_of(long_ref[...]), pieces_of(w_ref[...])) * table_ref[:, 5:6]
    node = lax.broadcasted_iota(jnp.int32, (SEC_NODES, long_ref.shape[0]), 0).astype(jnp.float32)
    spread = (node == seconds_ref[1:2] - nodes).astype(jnp.float32).astype(jnp.bfloat16)
    for c in range(3):
        top_ref[c] = picked(spread, halves(table_ref[:, 2 + c : 3 + c] * axial))


def factor_block(x_ref, u_ref, m_ref, rows_ref):
    n = x_ref.shape[0]
    count = n // 8
    tiles = [x_ref[8 * i : 8 * i + 8, :] for i in range(count)]
    lane = lax.broadcasted_iota(jnp.int32, (8, n), 1)
    sub = lax.broadcasted_iota(jnp.int32, (8, n), 0)

    def column(tile, c):
        return jnp.broadcast_to(tile[:, c : c + 1], (8, n))

    for p in range(count):
        c0 = 8 * p
        rows_ref[c0 : c0 + 8, :] = tiles[p]
        u = [rows_ref[pl.ds(c0 + r, 8, stride=0), :] for r in range(8)]
        a = [[column(u[r], c0 + c) if c >= r else None for c in range(8)] for r in range(8)]
        panel = (lane >= c0) & (lane < c0 + 8)
        v = [jnp.where(panel, jnp.where(lane == c0 + k, 1.0, 0.0), u[k]) for k in range(8)]
        cols = {t: [column(tiles[t], c0 + k) for k in range(8)] for t in range(p + 1, count)}
        for t in cols:
            tiles[t] = jnp.where(panel, 0.0, tiles[t])
        for k in range(8):
            inverse = pltpu.reciprocal(a[k][k])
            scaled = v[k] * inverse
            for i in range(k + 1, 8):
                f = a[k][i] * inverse
                for j in range(i, 8):
                    a[i][j] = a[i][j] - f * a[k][j]
                v[i] = v[i] - f * v[k]
                u[i] = u[i] - f * u[k]
                for t in cols:
                    cols[t][i] = cols[t][i] - f * cols[t][k]
            for t in cols:
                tiles[t] = tiles[t] - cols[t][k] * scaled
        yt, ut = v[0], u[0]
        for i in range(1, 8):
            yt = jnp.where(sub == i, v[i], yt)
            ut = jnp.where(sub == i, u[i], ut)
        u_ref[c0 : c0 + 8, :] = ut
        m_ref[c0 : c0 + 8, :] = yt


def factored(block, x, u, m, rows):
    h = block.shape[0]
    rowi = lax.broadcasted_iota(jnp.int32, (h, h), 0)
    coli = lax.broadcasted_iota(jnp.int32, (h, h), 1)
    x[...] = block
    factor_block(x, u, m, rows)
    upper = u[...]
    s = lax.rsqrt(jnp.sum(jnp.where(rowi == coli, upper, 0.0), axis=1, keepdims=True))
    return jnp.where(rowi <= coli, upper, 0.0) * s, jnp.where(rowi >= coli, m[...], 0.0) * s


def finish_factor(r11, m1, g12, g22, w_ref, r_ref, scratch):
    h = r11.shape[0]
    r12 = dot(m1, g12)
    r22, m2 = factored(g22 - dot(r12, r12, 0, 0), *scratch)
    zero = jnp.zeros((h, h), jnp.float32)
    r_ref[:h, :h], r_ref[:h, h:], r_ref[h:, :h], r_ref[h:, h:] = r11, r12, zero, r22
    w_ref[:h, :h], w_ref[h:, h:], w_ref[h:, :h] = m1.T, m2.T, zero
    w_ref[:h, h:] = -dot(m1, dot(r12, m2, 1, 1), 0, 0)


def on_diagonal(block):
    shape = block.shape
    eye = lax.broadcasted_iota(jnp.int32, shape, 0) == lax.broadcasted_iota(jnp.int32, shape, 1)
    return jnp.sum(jnp.where(eye, block, 0.0), axis=0, keepdims=True)


def first_block_kernel(sum_ref, message_ref, *scratch):
    odd = lax.axis_index(AXES) % 2 == 1
    h = sum_ref.shape[1]
    p = 3 * h // 4

    @pl.when(odd)
    def _():
        g11 = unpack_block(sum_ref[:p])
        r11, m1 = factored(g11, *scratch)
        rowi = lax.broadcasted_iota(jnp.int32, (h, h), 0)
        coli = lax.broadcasted_iota(jnp.int32, (h, h), 1)
        message_ref[:h] = jnp.where(rowi < coli, r11, m1)
        message_ref[h : h + h // 2] = sum_ref[p:]
        message_ref[h + h // 2 :] = jnp.broadcast_to(on_diagonal(g11), (8, h))

    @pl.when(jnp.logical_not(odd))
    def _():
        message_ref[: sum_ref.shape[0]] = sum_ref[...]
        message_ref[sum_ref.shape[0] :] = jnp.zeros_like(message_ref[sum_ref.shape[0] :])


def second_block_kernel(mine_ref, other_ref, w_ref, r_ref, diag_ref, *scratch):
    h = mine_ref.shape[1]
    p, q = 3 * h // 4, h // 2
    even, odd = order_halves(mine_ref[...], other_ref[...])
    rowi = lax.broadcasted_iota(jnp.int32, (h, h), 0)
    coli = lax.broadcasted_iota(jnp.int32, (h, h), 1)
    m1 = jnp.where(rowi >= coli, odd[:h], 0.0)
    r11 = jnp.where(rowi < coli, odd[:h], jnp.where(rowi == coli, pltpu.reciprocal(odd[:h]), 0.0))
    g12 = jnp.concatenate([even[p : p + q], odd[h : h + q]], axis=0)
    g22 = unpack_block(even[:p])
    diag_ref[:, :h] = odd[h + q : h + q + 1]
    diag_ref[:, h:] = on_diagonal(g22)
    finish_factor(r11, m1, g12, g22, w_ref, r_ref, scratch)


def middle_kernel(s_ref, long_ref, table_ref, w_ref, q_ref, q_halves, long_out, keep_ref, send_ref):
    parts, nodes, width = s_ref.shape
    w = w_ref[...]
    w = pieces_of(w)
    q = dot6(pieces_of(s_ref[...].reshape(-1, width)), w)
    q_ref[...] = q.reshape(parts, nodes, width)
    long = dot6(pieces_of(long_ref[...]), w)
    long_out[...] = long
    q = halves(q)
    for i in range(2):
        q_halves[i] = q[i].reshape(parts, nodes, width)
    gram = gram_of(q)
    energy = gram_of(halves(long * jnp.sqrt(table_ref[:, 5:6])))
    keep, send = order_halves(pack(energy), pack(gram))
    keep_ref[...] = keep.reshape(keep_ref.shape)
    send_ref[...] = send.reshape(send_ref.shape)


def refine_kernel(rows_all, w_ref, r_ref, diag_ref, tie_ref, out_ref, log_ref):
    del tie_ref
    log_ref[...] = jnp.log(diag_ref[...] / rows_all)

    @pl.when(lax.axis_index(AXES) % 2 == 1)
    def _():
        r = r_ref[...]
        size = r.shape[0]
        eye = lax.broadcasted_iota(jnp.int32, (size, size), 0) == lax.broadcasted_iota(jnp.int32, (size, size), 1)
        out_ref[...] = r + dot(jnp.where(eye, 1.0, 0.0) - dot(r, w_ref[...]), r)


def second_factor_kernel(rows_all, sum_ref, r1_ref, message_ref, *scratch):
    odd = lax.axis_index(AXES) % 2 == 1
    width = message_ref.shape[1]
    h = width // 2
    packed = sum_ref[...].reshape(-1, h)
    half = packed.shape[0] // 2

    @pl.when(odd)
    def _():
        second_factor(rows_all, unpack(packed), r1_ref, message_ref, *scratch)

    @pl.when(jnp.logical_not(odd))
    def _():
        message_ref[:half] = jnp.concatenate([packed[:half], packed[half:]], axis=1)
        message_ref[half:] = jnp.zeros_like(message_ref[half:])


def second_factor(rows_all, gram, r1_ref, message_ref, v_ref, e_ref, w2, r2, *scratch):
    width = gram.shape[0]
    h = width // 2
    rowi = lax.broadcasted_iota(jnp.int32, (width, width), 0)
    coli = lax.broadcasted_iota(jnp.int32, (width, width), 1)
    eye = jnp.where(rowi == coli, 1.0, 0.0)
    start = gram - eye

    def upper_half(e):
        return jnp.where(rowi < coli, e, jnp.where(rowi == coli, 0.5 * e, 0.0))

    e_ref[...] = start
    size = jnp.sum(start * start)

    @pl.when(size < 0.06)
    def _():
        v_ref[...] = -upper_half(start)

        def improve(i, carry):
            e = e_ref[...]
            upper = upper_half(e)
            split = halves(upper)
            p = dot3(halves(e), split)
            e = dot3(split, halves(upper + p), 0, 0) - (p + p.T)
            e_ref[...] = e
            upper = upper_half(e)
            v = v_ref[...]
            v_ref[...] = v - (upper + dot3(halves(v), halves(upper)))
            return carry

        lax.fori_loop(0, 2, improve, 0)

    @pl.when(jnp.logical_not(size < 0.06))
    def _():
        r11, m1 = factored(gram[:h, :h], *scratch)
        finish_factor(r11, m1, gram[:h, h:], gram[h:, h:], w2, r2, scratch)
        v_ref[...] = w2[...] - eye

    v = v_ref[...]
    change = jnp.where(rowi <= coli, v.T + start + dot3(halves(v), halves(start), 0, 0), 0.0)
    r1 = r1_ref[...]
    coef = (r1 + dot3(halves(change), halves(r1))) * (1.0 / math.sqrt(rows_all))
    message_ref[:width] = jnp.where(rowi < coli, v, coef.T)
    message_ref[width:] = jnp.broadcast_to(on_diagonal(v), (8, width))


def final_kernel(
    rows_all, mine_ref, other_ref, q_ref, q_halves, own_ref,
    basis_ref, forces_ref, reduced_ref, coef_ref, held, sems,
):
    parts, nodes, width = q_ref.shape
    h = width // 2
    even, odd = order_halves(mine_ref[...], other_ref[...])
    rowi = lax.broadcasted_iota(jnp.int32, (width, width), 0)
    coli = lax.broadcasted_iota(jnp.int32, (width, width), 1)
    diag = jnp.where(rowi == coli, odd[width : width + 1], 0.0)
    v = halves(jnp.where(rowi < coli, odd[:width], diag))
    root = math.sqrt(rows_all)
    copies = []
    for k in range(2 * parts):
        c = k % parts
        if k < parts:
            source, split, target = q_ref[c], (q_halves[0, c], q_halves[1, c]), basis_ref
        else:
            source, target = own_ref[c], forces_ref
            split = halves(source)
        held[k] = (source + dot3(split, v)) * root
        copies.append(pltpu.make_async_copy(held.at[k], target.at[c], sems.at[k]))
        copies[-1].start()
    coef_ref[...] = jnp.where(rowi <= coli, odd[:width].T, 0.0)
    half = 5 * h // 4
    energy = unpack(jnp.concatenate([even[:half, :h], even[:half, h:]], axis=0))
    right = energy + dot3(halves(energy), v)
    reduced_ref[...] = right + dot3(v, halves(right), 0, 0)
    for copy in copies:
        copy.wait()


def local(snapshots, member_ends, member_dir, member_stiff):
    parts, nodes, width = snapshots.shape
    h = width // 2
    count = math.prod(lax.axis_size(a) for a in AXES)
    rows_all = parts * nodes * count
    steps = sum_steps()
    square = (width, width)
    field = (parts, nodes, width)
    packed = (5 * width // 8, h)
    scratch = [pltpu.VMEM((h, h), jnp.float32)] * 3 + [pltpu.VMEM((h + 8, h), jnp.float32)]

    below = shifted(snapshots[:, nodes - SEC_NODES :, :], "span", 1, True)
    keep, send = call(gram_kernel, [packed, packed], (snapshots,))
    members = member_dir.shape[1]
    split = members // 2
    total = add((keep, exchange(send, 1)))
    for i, bits in enumerate(steps):
        received = [exchange(total, bit) for bit in bits]
        if i == 0:
            first, table = call(
                first_elongation_kernel,
                [(split, width), (members, 8)],
                (member_ends, member_dir, member_stiff[None], snapshots, total),
                [VMEM] * 4 + [ANY],
            )
            second = call(second_elongation_kernel, [(split, width)], (table, snapshots, total), [VMEM, VMEM, ANY])
            long = [first, *second]
            total = add((total, *received), long)
        elif i < len(steps) - 1:
            total = add((total, *received))
        else:
            operands = (table, below, *long, total)
            (stretch,) = call(below_elongation_kernel, [(members, width)], operands, [VMEM] * 4 + [ANY])
            (downward,) = call(
                downward_kernel,
                [(3 * SEC_NODES + 6 * members // width, width)],
                (snapshots, member_ends, member_dir, member_stiff[None], total),
                [VMEM] * 4 + [ANY],
            )
            total, downward = add((total, *received), (stretch,), (downward,))
    above = shifted(downward, "span", -1, True)
    (message,) = call(first_block_kernel, [(h + h // 2 + 8, h)], (total,), scratch=scratch, us=2)
    w1, r1, diag = call(
        second_block_kernel, [square, square, (1, width)], (message, exchange(message, 1)), scratch=scratch, us=5
    )

    quarters = (4, 5 * width // 16, h)
    q, q_halves, stretch, keep, send = call(
        middle_kernel,
        [field, jax.ShapeDtypeStruct((2, *field), jnp.bfloat16), (members, width), quarters, quarters],
        (snapshots, stretch, table, w1),
        us=3,
    )
    def refined(tie):
        refine = functools.partial(refine_kernel, rows_all)
        made["r1"] = call(refine, [square, (1, width)], (w1, r1, diag, tie), [VMEM] * 3 + [ANY], us=1)
        return made["r1"][0]

    def above_elongation(tie):
        shapes = [(members, width), (members, 8), (8, members)]
        made["above"] = call(above_elongation_kernel, shapes, (above, snapshots, tie), [VMEM] * 2 + [ANY], us=2)
        return made["above"][:1]

    def above_forces(tie):
        stretch_above, table_above, seconds = made["above"]
        operands = (table_above, seconds, stretch_above, w1, tie)
        kernel = functools.partial(above_force_kernel, nodes)
        made["top"] = call(kernel, [(parts, SEC_NODES, width)], operands, [VMEM] * 4 + [ANY], us=2.5)
        return made["top"]

    def own_forces(tie):
        operands = (table, member_ends, stretch, made["top"][0], tie)
        (made["own"],) = call(force_kernel, [field], operands, [VMEM] * 4 + [ANY], us=1.5)
        return made["own"]

    made = {}
    total = sum_by_quarters(keep, send, [refined, above_elongation, above_forces, own_forces])
    r1, column_energy = made["r1"]

    (message,) = call(
        functools.partial(second_factor_kernel, rows_all),
        [(width + 8, width)],
        (total, r1),
        scratch=[pltpu.VMEM(square, jnp.float32)] * 4 + scratch,
    )
    basis, forces, reduced, coef = call(
        functools.partial(final_kernel, rows_all),
        [field, field, square, square],
        (message, exchange(message, 1), q, q_halves, made["own"]),
        scratch=[pltpu.VMEM((2 * parts, nodes, width), jnp.float32), pltpu.SemaphoreType.DMA((2 * parts,))],
        outs=(HBM, HBM, VMEM, VMEM),
    )
    return (basis, forces, reduced, coef, column_energy[0])


def solution(mesh):
    placed = (
        P(None, AXES, None),
        P(None, AXES),
        P(None, AXES),
        P(AXES),
    )
    return jax.shard_map(
        local,
        mesh=mesh,
        in_specs=placed,
        out_specs=(P(None, AXES, None), P(None, AXES, None), P(), P(), P()),
        check_vma=False,
    )
```

```python
import functools
import math

import jax
import jax.numpy as jnp
from jax import lax
from jax.experimental import pallas as pl
from jax.experimental.pallas import tpu as pltpu
from jax.sharding import PartitionSpec as P

AXES = ("span", "xsec", "leaf")
SEC_NODES = 128
NODES = 256
CHUNK = 256
highest = lax.Precision.HIGHEST
VMEM = pl.BlockSpec(memory_space=pltpu.VMEM)
ANY = pl.BlockSpec(memory_space=pl.ANY)
HBM = pl.BlockSpec(memory_space=pltpu.HBM)


def dot(a, b, ca=1, cb=0):
    return lax.dot_general(
        a, b, (((ca,), (cb,)), ((), ())), precision=highest, preferred_element_type=jnp.float32
    )


def halves(x):
    high = x.astype(jnp.bfloat16)
    return high, (x - high.astype(jnp.float32)).astype(jnp.bfloat16)


def dot3(a, b, ca=1, cb=0):
    def one(x, y):
        return lax.dot_general(x, y, (((ca,), (cb,)), ((), ())), preferred_element_type=jnp.float32)

    return one(a[0], b[0]) + (one(a[0], b[1]) + one(a[1], b[0]))


def pieces_of(x):
    first = x.astype(jnp.bfloat16)
    rest = x - first.astype(jnp.float32)
    second = rest.astype(jnp.bfloat16)
    third = (rest - second.astype(jnp.float32)).astype(jnp.bfloat16)
    return first, second, third


def dot6(a, b, ca=1, cb=0):
    def one(i, j):
        return lax.dot_general(a[i], b[j], (((ca,), (cb,)), ((), ())), preferred_element_type=jnp.float32)

    return one(0, 0) + ((one(0, 1) + one(1, 0)) + ((one(0, 2) + one(2, 0)) + one(1, 1)))


def gram_of(parts):
    def one(i, j):
        return lax.dot_general(parts[i], parts[j], (((0,), (0,)), ((), ())), preferred_element_type=jnp.float32)

    mixed = one(0, 1) if len(parts) == 2 else one(0, 1) + one(0, 2)
    mixed = mixed + mixed.T
    return one(0, 0) + (mixed if len(parts) == 2 else mixed + one(1, 1))


def call(kernel, shapes, operands, specs=None, scratch=(), outs=None, us=0.1):
    return pl.pallas_call(
        kernel,
        out_shape=tuple(s if isinstance(s, jax.ShapeDtypeStruct) else jax.ShapeDtypeStruct(s, jnp.float32) for s in shapes),
        in_specs=specs or [VMEM] * len(operands),
        out_specs=outs or tuple(VMEM for _ in shapes),
        scratch_shapes=list(scratch),
        compiler_params=pltpu.CompilerParams(vmem_limit_bytes=48 << 20),
        cost_estimate=pl.CostEstimate(flops=0, bytes_accessed=int(us * 3.69e6), transcendentals=0),
    )(*operands)


def exchange(array, bit):
    count = math.prod(lax.axis_size(a) for a in AXES)
    return lax.ppermute(array, AXES, [(i, i ^ bit) for i in range(count)])


def add_kernel(terms, handed, *refs):
    outs = refs[len(refs) - 1 - handed :]
    parts = [ref[...] for ref in refs[:terms]]
    while len(parts) > 1:
        parts = [sum(parts[i : i + 2]) for i in range(0, len(parts), 2)]
    outs[0][...] = parts[0]
    for given, out in zip(refs[terms : terms + handed], outs[1:], strict=True):
        out[...] = given[...]


def add(parts, beside=(), through=()):
    operands = (*parts, *through, *beside)
    specs = [VMEM] * (len(parts) + len(through)) + [ANY] * len(beside)
    kernel = functools.partial(add_kernel, len(parts), len(through))
    outs = call(kernel, [parts[0].shape, *(t.shape for t in through)], operands, specs)
    return outs if through else outs[0]


def sum_steps():
    count = math.prod(lax.axis_size(a) for a in AXES)
    bits = [1 << i for i in range(1, count.bit_length() - 1)]
    assert 1 << (len(bits) + 1) == count and len(bits) > 1
    return [(bits[0], bits[1], bits[0] | bits[1])] + [(bit,) for bit in bits[2:]]


def scatter_kernel(keep_ref, received_ref, tie_ref, mine_ref, *send_refs):
    del tie_ref
    place = lax.axis_index(AXES) // 2 % 4
    for i, ref in enumerate((mine_ref, *send_refs)):
        part = place ^ i
        ref[...] = (keep_ref[pl.ds(part, 1)] + received_ref[pl.ds(part, 1)])[0]


def gather_kernel(mine_ref, *rest):
    out_ref = rest[-1]
    place = lax.axis_index(AXES) // 2 % 4
    for i, ref in enumerate((mine_ref, *rest[:-2])):
        out_ref[pl.ds(place ^ i, 1)] = ref[...][None]


def sum_by_quarters(keep, send, works):
    first, *others = sum_steps()
    others = [bit for (bit,) in others]
    others = [(*pair, sum(pair))[: 2 * len(pair) - 1] for pair in (others[i : i + 2] for i in range(0, len(others), 2))]
    block = keep.shape[1:]
    operands = (keep, exchange(send, 1), works[0](keep))
    mine, *parts = call(scatter_kernel, [block] * 4, operands, [VMEM, VMEM, ANY])
    received = [exchange(part, bit) for part, bit in zip(parts, first, strict=True)]
    mine = add((mine, *received), works[1](mine))
    for i, bits in enumerate(others):
        received = [exchange(mine, bit) for bit in bits]
        mine = add((mine, *received), works[2](mine) if i == len(others) - 1 else ())
    received = [exchange(mine, bit) for bit in first]
    operands = (mine, *received, works[3](mine))
    (total,) = call(gather_kernel, [keep.shape], operands, [VMEM] * 4 + [ANY])
    return total


def shifted(array, axis, by, round_off=False):
    length = lax.axis_size(axis)
    pairs = [(i, (i + by) % length) for i in range(length) if round_off or 0 <= i + by < length]
    return lax.ppermute(array, axis, pairs)


def order_halves(mine, other):
    odd = lax.axis_index(AXES) % 2
    return jnp.where(odd == 0, mine, other), jnp.where(odd == 0, other, mine)


def pack_block(block):
    h, q = block.shape[0], block.shape[0] // 2
    e = q // 2
    lane = lax.broadcasted_iota(jnp.int32, (e, h), 1)
    corner = jnp.where(lane < q, pltpu.roll(block[q : q + e], q, 1), block[q + e :])
    return jnp.concatenate([block[:q], corner], axis=0)


def unpack_block(rows):
    h = rows.shape[1]
    q = h // 2
    lane = lax.broadcasted_iota(jnp.int32, (q, h), 1)
    low = jnp.concatenate([pltpu.roll(rows[q:], q, 1), rows[q:]], axis=0)
    square = jnp.concatenate([rows[:q], low], axis=0)
    return jnp.concatenate([rows[:q], jnp.where(lane < q, square.T[q:], low)], axis=0)


def pack(square):
    h = square.shape[0] // 2
    return jnp.concatenate([pack_block(square[:h, :h]), pack_block(square[h:, h:]), square[:h, h:]], axis=0)


def unpack(rows):
    h = rows.shape[1]
    p = 3 * h // 4
    corner = rows[2 * p :]
    upper = jnp.concatenate([unpack_block(rows[:p]), corner], axis=1)
    return jnp.concatenate([upper, jnp.concatenate([corner.T, unpack_block(rows[p : 2 * p])], axis=1)], axis=0)


def gram_kernel(s_ref, keep_ref, send_ref):
    width = s_ref.shape[2]
    flat = s_ref[...].reshape(-1, width)
    flat = pieces_of(flat)
    gram = gram_of(flat)
    h, q = width // 2, width // 4
    even = jnp.concatenate([pack_block(gram[h:, h:]), gram[:q, h:]], axis=0)
    odd = jnp.concatenate([pack_block(gram[:h, :h]), gram[q:h, h:]], axis=0)
    keep_ref[...], send_ref[...] = order_halves(even, odd)


def picks(node_count, first, second):
    node = lax.broadcasted_iota(jnp.int32, (first.shape[0], node_count), 1).astype(jnp.float32)
    pick = (node == first).astype(jnp.float32) - (node == second).astype(jnp.float32)
    return pick.astype(jnp.bfloat16)


def picked(pick, pieces):
    return sum(jnp.dot(pick, piece, preferred_element_type=jnp.float32) for piece in pieces)


def own_elongation(first, table, s_ref, long_ref):
    nodes = s_ref.shape[1]
    pieces = [pieces_of(s_ref[c]) for c in range(3)]
    for start in range(0, long_ref.shape[0], CHUNK):
        rows = table[first + start : first + start + CHUNK, :]
        pick = picks(nodes, rows[:, 0:1], rows[:, 1:2])
        long_ref[start : start + CHUNK, :] = sum(rows[:, 2 + c : 3 + c] * picked(pick, pieces[c]) for c in range(3))


def first_elongation_kernel(ends_ref, dir_ref, stiff_ref, s_ref, tie_ref, long_ref, table_ref):
    del tie_ref
    ends = ends_ref[...].astype(jnp.float32)
    table_ref[...] = jnp.concatenate([ends, dir_ref[...], stiff_ref[...], jnp.zeros_like(ends)], axis=0).T
    own_elongation(0, table_ref, s_ref, long_ref)


def second_elongation_kernel(table_ref, s_ref, tie_ref, long_ref):
    del tie_ref
    own_elongation(long_ref.shape[0], table_ref, s_ref, long_ref)


def below_elongation_kernel(table_ref, below_ref, first_ref, second_ref, tie_ref, long_ref):
    del tie_ref
    stands = lax.axis_index("span") == 0
    pieces = [pieces_of(jnp.where(stands, 0.0, below_ref[c])) for c in range(3)]
    split = first_ref.shape[0]
    for half, given in enumerate((first_ref, second_ref)):
        for start in range(0, split, CHUNK):
            at = split * half + start
            rows = table_ref[at : at + CHUNK, :]
            pick = picks(SEC_NODES, rows[:, 0:1] - NODES, rows[:, 1:2] - NODES)
            added = sum(rows[:, 2 + c : 3 + c] * picked(pick, pieces[c]) for c in range(3))
            long_ref[at : at + CHUNK, :] = given[start : start + CHUNK, :] + added


def force_kernel(table_ref, ends_ref, long_ref, top_ref, tie_ref, own_ref):
    del tie_ref
    nodes = own_ref.shape[1]
    members = long_ref.shape[0]
    axial = long_ref[...] * table_ref[:, 5:6]
    node = lax.broadcasted_iota(jnp.int32, (nodes, members), 0)
    ends = ends_ref[...]
    spread = (node == ends[0:1]).astype(jnp.float32) - (node == ends[1:2]).astype(jnp.float32)
    spread = spread.astype(jnp.bfloat16)
    for c in range(3):
        force = picked(spread, halves(table_ref[:, 2 + c : 3 + c] * axial))
        own_ref[c, : nodes - SEC_NODES] = force[: nodes - SEC_NODES]
        own_ref[c, nodes - SEC_NODES :] = force[nodes - SEC_NODES :] - top_ref[c]


def downward_kernel(s_ref, ends_ref, dir_ref, stiff_ref, tie_ref, out_ref):
    del tie_ref
    width = out_ref.shape[1]
    rows = 3 * SEC_NODES
    out_ref[:rows] = s_ref[:, :SEC_NODES].reshape(rows, width)
    table = jnp.concatenate([ends_ref[...].astype(jnp.float32), dir_ref[...], stiff_ref[...]], axis=0)
    out_ref[rows:] = jnp.concatenate([table[:, at : at + width] for at in range(0, table.shape[1], width)], axis=0)


def above_elongation_kernel(above_ref, s_ref, tie_ref, long_ref, table_ref, seconds_ref):
    del tie_ref
    nodes, width = s_ref.shape[1:]
    rows = 3 * SEC_NODES
    held = above_ref[rows:]
    table = jnp.concatenate([held[at : at + 6] for at in range(0, held.shape[0], 6)], axis=1)
    table = jnp.concatenate([table, jnp.zeros_like(table[:2])], axis=0)
    seconds_ref[...] = table
    table_ref[...] = table.T
    top = lax.axis_index("span") == lax.axis_size("span") - 1
    pieces = []
    for c in range(3):
        both = jnp.concatenate([above_ref[SEC_NODES * c : SEC_NODES * (c + 1)], s_ref[c, nodes - SEC_NODES :]], axis=0)
        pieces.append(pieces_of(jnp.where(top, 0.0, both)))
    for start in range(0, long_ref.shape[0], CHUNK):
        members = table_ref[start : start + CHUNK, :]
        second = members[:, 1:2] - nodes
        first = jnp.where(second >= 0.0, members[:, 0:1], -1.0)
        pick = picks(2 * SEC_NODES, first, second + jnp.where(second >= 0.0, 1.0 * SEC_NODES, -1.0 * nodes))
        long_ref[start : start + CHUNK, :] = sum(members[:, 2 + c : 3 + c] * picked(pick, pieces[c]) for c in range(3))


def above_force_kernel(nodes, table_ref, seconds_ref, long_ref, w_ref, tie_ref, top_ref):
    del tie_ref
    axial = dot6(pieces_of(long_ref[...]), pieces_of(w_ref[...])) * table_ref[:, 5:6]
    node = lax.broadcasted_iota(jnp.int32, (SEC_NODES, long_ref.shape[0]), 0).astype(jnp.float32)
    spread = (node == seconds_ref[1:2] - nodes).astype(jnp.float32).astype(jnp.bfloat16)
    for c in range(3):
        top_ref[c] = picked(spread, halves(table_ref[:, 2 + c : 3 + c] * axial))


def factor_block(x_ref, u_ref, m_ref, rows_ref):
    n = x_ref.shape[0]
    count = n // 8
    tiles = [x_ref[8 * i : 8 * i + 8, :] for i in range(count)]
    lane = lax.broadcasted_iota(jnp.int32, (8, n), 1)
    sub = lax.broadcasted_iota(jnp.int32, (8, n), 0)

    def column(tile, c):
        return jnp.broadcast_to(tile[:, c : c + 1], (8, n))

    for p in range(count):
        c0 = 8 * p
        rows_ref[c0 : c0 + 8, :] = tiles[p]
        u = [rows_ref[pl.ds(c0 + r, 8, stride=0), :] for r in range(8)]
        a = [[column(u[r], c0 + c) if c >= r else None for c in range(8)] for r in range(8)]
        panel = (lane >= c0) & (lane < c0 + 8)
        v = [jnp.where(panel, jnp.where(lane == c0 + k, 1.0, 0.0), u[k]) for k in range(8)]
        cols = {t: [column(tiles[t], c0 + k) for k in range(8)] for t in range(p + 1, count)}
        for t in cols:
            tiles[t] = jnp.where(panel, 0.0, tiles[t])
        for k in range(8):
            inverse = pltpu.reciprocal(a[k][k])
            scaled = v[k] * inverse
            for i in range(k + 1, 8):
                f = a[k][i] * inverse
                for j in range(i, 8):
                    a[i][j] = a[i][j] - f * a[k][j]
                v[i] = v[i] - f * v[k]
                u[i] = u[i] - f * u[k]
                for t in cols:
                    cols[t][i] = cols[t][i] - f * cols[t][k]
            for t in cols:
                tiles[t] = tiles[t] - cols[t][k] * scaled
        yt, ut = v[0], u[0]
        for i in range(1, 8):
            yt = jnp.where(sub == i, v[i], yt)
            ut = jnp.where(sub == i, u[i], ut)
        u_ref[c0 : c0 + 8, :] = ut
        m_ref[c0 : c0 + 8, :] = yt


def factored(block, x, u, m, rows):
    h = block.shape[0]
    rowi = lax.broadcasted_iota(jnp.int32, (h, h), 0)
    coli = lax.broadcasted_iota(jnp.int32, (h, h), 1)
    x[...] = block
    factor_block(x, u, m, rows)
    upper = u[...]
    s = lax.rsqrt(jnp.sum(jnp.where(rowi == coli, upper, 0.0), axis=1, keepdims=True))
    return jnp.where(rowi <= coli, upper, 0.0) * s, jnp.where(rowi >= coli, m[...], 0.0) * s


def finish_factor(r11, m1, g12, g22, w_ref, r_ref, scratch):
    h = r11.shape[0]
    r12 = dot(m1, g12)
    r22, m2 = factored(g22 - gram_of(pieces_of(r12)), *scratch)
    zero = jnp.zeros((h, h), jnp.float32)
    r_ref[:h, :h], r_ref[:h, h:], r_ref[h:, :h], r_ref[h:, h:] = r11, r12, zero, r22
    w_ref[:h, :h], w_ref[h:, h:], w_ref[h:, :h] = m1.T, m2.T, zero
    w_ref[:h, h:] = -dot(m1, dot(r12, m2, 1, 1), 0, 0)


def on_diagonal(block):
    shape = block.shape
    eye = lax.broadcasted_iota(jnp.int32, shape, 0) == lax.broadcasted_iota(jnp.int32, shape, 1)
    return jnp.sum(jnp.where(eye, block, 0.0), axis=0, keepdims=True)


def first_block_kernel(sum_ref, message_ref, *scratch):
    odd = lax.axis_index(AXES) % 2 == 1
    h = sum_ref.shape[1]
    p = 3 * h // 4

    @pl.when(odd)
    def _():
        g11 = unpack_block(sum_ref[:p])
        r11, m1 = factored(g11, *scratch)
        rowi = lax.broadcasted_iota(jnp.int32, (h, h), 0)
        coli = lax.broadcasted_iota(jnp.int32, (h, h), 1)
        message_ref[:h] = jnp.where(rowi < coli, r11, m1)
        message_ref[h : h + h // 2] = sum_ref[p:]
        message_ref[h + h // 2 :] = jnp.broadcast_to(on_diagonal(g11), (8, h))

    @pl.when(jnp.logical_not(odd))
    def _():
        message_ref[: sum_ref.shape[0]] = sum_ref[...]
        message_ref[sum_ref.shape[0] :] = jnp.zeros_like(message_ref[sum_ref.shape[0] :])


def second_block_kernel(mine_ref, other_ref, w_ref, r_ref, diag_ref, *scratch):
    h = mine_ref.shape[1]
    p, q = 3 * h // 4, h // 2
    even, odd = order_halves(mine_ref[...], other_ref[...])
    rowi = lax.broadcasted_iota(jnp.int32, (h, h), 0)
    coli = lax.broadcasted_iota(jnp.int32, (h, h), 1)
    m1 = jnp.where(rowi >= coli, odd[:h], 0.0)
    r11 = jnp.where(rowi < coli, odd[:h], jnp.where(rowi == coli, pltpu.reciprocal(odd[:h]), 0.0))
    g12 = jnp.concatenate([even[p : p + q], odd[h : h + q]], axis=0)
    g22 = unpack_block(even[:p])
    diag_ref[:, :h] = odd[h + q : h + q + 1]
    diag_ref[:, h:] = on_diagonal(g22)
    finish_factor(r11, m1, g12, g22, w_ref, r_ref, scratch)


def middle_kernel(s_ref, long_ref, table_ref, w_ref, q_ref, q_halves, long_out, keep_ref, send_ref):
    parts, nodes, width = s_ref.shape
    w = w_ref[...]
    w = pieces_of(w)
    q = dot6(pieces_of(s_ref[...].reshape(-1, width)), w)
    q_ref[...] = q.reshape(parts, nodes, width)
    long = dot6(pieces_of(long_ref[...]), w)
    long_out[...] = long
    q = halves(q)
    for i in range(2):
        q_halves[i] = q[i].reshape(parts, nodes, width)
    gram = gram_of(q)
    energy = gram_of(halves(long * jnp.sqrt(table_ref[:, 5:6])))
    keep, send = order_halves(pack(energy), pack(gram))
    keep_ref[...] = keep.reshape(keep_ref.shape)
    send_ref[...] = send.reshape(send_ref.shape)


def refine_kernel(rows_all, w_ref, r_ref, diag_ref, tie_ref, out_ref, log_ref):
    del tie_ref
    log_ref[...] = jnp.log(diag_ref[...] / rows_all)

    @pl.when(lax.axis_index(AXES) % 2 == 1)
    def _():
        r = r_ref[...]
        size = r.shape[0]
        eye = lax.broadcasted_iota(jnp.int32, (size, size), 0) == lax.broadcasted_iota(jnp.int32, (size, size), 1)
        out_ref[...] = r + dot(jnp.where(eye, 1.0, 0.0) - dot(r, w_ref[...]), r)


def second_factor_kernel(rows_all, sum_ref, r1_ref, message_ref, *scratch):
    odd = lax.axis_index(AXES) % 2 == 1
    width = message_ref.shape[1]
    h = width // 2
    packed = sum_ref[...].reshape(-1, h)
    half = packed.shape[0] // 2

    @pl.when(odd)
    def _():
        second_factor(rows_all, unpack(packed), r1_ref, message_ref, *scratch)

    @pl.when(jnp.logical_not(odd))
    def _():
        message_ref[:half] = jnp.concatenate([packed[:half], packed[half:]], axis=1)
        message_ref[half:] = jnp.zeros_like(message_ref[half:])


def second_factor(rows_all, gram, r1_ref, message_ref, v_ref, e_ref, w2, r2, *scratch):
    width = gram.shape[0]
    h = width // 2
    rowi = lax.broadcasted_iota(jnp.int32, (width, width), 0)
    coli = lax.broadcasted_iota(jnp.int32, (width, width), 1)
    eye = jnp.where(rowi == coli, 1.0, 0.0)
    start = gram - eye

    def upper_half(e):
        return jnp.where(rowi < coli, e, jnp.where(rowi == coli, 0.5 * e, 0.0))

    e_ref[...] = start
    size = jnp.sum(start * start)

    @pl.when(size < 0.06)
    def _():
        v_ref[...] = -upper_half(start)

        def improve(i, carry):
            e = e_ref[...]
            upper = upper_half(e)
            split = halves(upper)
            p = dot3(halves(e), split)
            e = dot3(split, halves(upper + p), 0, 0) - (p + p.T)
            e_ref[...] = e
            upper = upper_half(e)
            v = v_ref[...]
            v_ref[...] = v - (upper + dot3(halves(v), halves(upper)))
            return carry

        lax.fori_loop(0, 2, improve, 0)

    @pl.when(jnp.logical_not(size < 0.06))
    def _():
        r11, m1 = factored(gram[:h, :h], *scratch)
        finish_factor(r11, m1, gram[:h, h:], gram[h:, h:], w2, r2, scratch)
        v_ref[...] = w2[...] - eye

    v = v_ref[...]
    change = jnp.where(rowi <= coli, v.T + start + dot3(halves(v), halves(start), 0, 0), 0.0)
    r1 = r1_ref[...]
    coef = (r1 + dot3(halves(change), halves(r1))) * (1.0 / math.sqrt(rows_all))
    message_ref[:width] = jnp.where(rowi < coli, v, coef.T)
    message_ref[width:] = jnp.broadcast_to(on_diagonal(v), (8, width))


def final_kernel(
    rows_all, mine_ref, other_ref, q_ref, q_halves, own_ref,
    basis_ref, forces_ref, reduced_ref, coef_ref, held, sems,
):
    parts, nodes, width = q_ref.shape
    h = width // 2
    even, odd = order_halves(mine_ref[...], other_ref[...])
    rowi = lax.broadcasted_iota(jnp.int32, (width, width), 0)
    coli = lax.broadcasted_iota(jnp.int32, (width, width), 1)
    diag = jnp.where(rowi == coli, odd[width : width + 1], 0.0)
    v = halves(jnp.where(rowi < coli, odd[:width], diag))
    root = math.sqrt(rows_all)
    copies = []
    for k in range(2 * parts):
        c = k % parts
        if k < parts:
            source, split, target = q_ref[c], (q_halves[0, c], q_halves[1, c]), basis_ref
        else:
            source, target = own_ref[c], forces_ref
            split = halves(source)
        held[k] = (source + dot3(split, v)) * root
        copies.append(pltpu.make_async_copy(held.at[k], target.at[c], sems.at[k]))
        copies[-1].start()
    coef_ref[...] = jnp.where(rowi <= coli, odd[:width].T, 0.0)
    half = 5 * h // 4
    energy = unpack(jnp.concatenate([even[:half, :h], even[:half, h:]], axis=0))
    right = energy + dot3(halves(energy), v)
    reduced_ref[...] = right + dot3(v, halves(right), 0, 0)
    for copy in copies:
        copy.wait()


def local(snapshots, member_ends, member_dir, member_stiff):
    parts, nodes, width = snapshots.shape
    h = width // 2
    count = math.prod(lax.axis_size(a) for a in AXES)
    rows_all = parts * nodes * count
    steps = sum_steps()
    square = (width, width)
    field = (parts, nodes, width)
    packed = (5 * width // 8, h)
    scratch = [pltpu.VMEM((h, h), jnp.float32)] * 3 + [pltpu.VMEM((h + 8, h), jnp.float32)]

    below = shifted(snapshots[:, nodes - SEC_NODES :, :], "span", 1, True)
    keep, send = call(gram_kernel, [packed, packed], (snapshots,))
    members = member_dir.shape[1]
    split = members // 2
    total = add((keep, exchange(send, 1)))
    for i, bits in enumerate(steps):
        received = [exchange(total, bit) for bit in bits]
        if i == 0:
            first, table = call(
                first_elongation_kernel,
                [(split, width), (members, 8)],
                (member_ends, member_dir, member_stiff[None], snapshots, total),
                [VMEM] * 4 + [ANY],
            )
            second = call(second_elongation_kernel, [(split, width)], (table, snapshots, total), [VMEM, VMEM, ANY])
            long = [first, *second]
            total = add((total, *received), long)
        elif i < len(steps) - 1:
            total = add((total, *received))
        else:
            operands = (table, below, *long, total)
            (stretch,) = call(below_elongation_kernel, [(members, width)], operands, [VMEM] * 4 + [ANY])
            (downward,) = call(
                downward_kernel,
                [(3 * SEC_NODES + 6 * members // width, width)],
                (snapshots, member_ends, member_dir, member_stiff[None], total),
                [VMEM] * 4 + [ANY],
            )
            total, downward = add((total, *received), (stretch,), (downward,))
    above = shifted(downward, "span", -1, True)
    (message,) = call(first_block_kernel, [(h + h // 2 + 8, h)], (total,), scratch=scratch, us=2)
    w1, r1, diag = call(
        second_block_kernel, [square, square, (1, width)], (message, exchange(message, 1)), scratch=scratch, us=5
    )

    quarters = (4, 5 * width // 16, h)
    q, q_halves, stretch, keep, send = call(
        middle_kernel,
        [field, jax.ShapeDtypeStruct((2, *field), jnp.bfloat16), (members, width), quarters, quarters],
        (snapshots, stretch, table, w1),
        us=3,
    )
    def refined(tie):
        refine = functools.partial(refine_kernel, rows_all)
        made["r1"] = call(refine, [square, (1, width)], (w1, r1, diag, tie), [VMEM] * 3 + [ANY], us=1)
        return made["r1"][0]

    def above_elongation(tie):
        shapes = [(members, width), (members, 8), (8, members)]
        made["above"] = call(above_elongation_kernel, shapes, (above, snapshots, tie), [VMEM] * 2 + [ANY], us=2)
        return made["above"][:1]

    def above_forces(tie):
        stretch_above, table_above, seconds = made["above"]
        operands = (table_above, seconds, stretch_above, w1, tie)
        kernel = functools.partial(above_force_kernel, nodes)
        made["top"] = call(kernel, [(parts, SEC_NODES, width)], operands, [VMEM] * 4 + [ANY], us=2.5)
        return made["top"]

    def own_forces(tie):
        operands = (table, member_ends, stretch, made["top"][0], tie)
        (made["own"],) = call(force_kernel, [field], operands, [VMEM] * 4 + [ANY], us=1.5)
        return made["own"]

    made = {}
    total = sum_by_quarters(keep, send, [refined, above_elongation, above_forces, own_forces])
    r1, column_energy = made["r1"]

    (message,) = call(
        functools.partial(second_factor_kernel, rows_all),
        [(width + 8, width)],
        (total, r1),
        scratch=[pltpu.VMEM(square, jnp.float32)] * 4 + scratch,
    )
    basis, forces, reduced, coef = call(
        functools.partial(final_kernel, rows_all),
        [field, field, square, square],
        (message, exchange(message, 1), q, q_halves, made["own"]),
        scratch=[pltpu.VMEM((2 * parts, nodes, width), jnp.float32), pltpu.SemaphoreType.DMA((2 * parts,))],
        outs=(HBM, HBM, VMEM, VMEM),
    )
    return (basis, forces, reduced, coef, column_energy[0])


def solution(mesh):
    placed = (
        P(None, AXES, None),
        P(None, AXES),
        P(None, AXES),
        P(AXES),
    )
    return jax.shard_map(
        local,
        mesh=mesh,
        in_specs=placed,
        out_specs=(P(None, AXES, None), P(None, AXES, None), P(), P(), P()),
        check_vma=False,
    )
```
